32 devices in a mesh: section: 2 (over core), dp: 16 (over z, y, x).
Axes of the slice: x: 2, y: 2, z: 4, core: 2. Of those that a mesh axis runs over, the one named last changes fastest.
Arguments:
- byte_codes: int32 [2, 32, 128], P('section', 'dp'), may hold values from 0 to 383
- encoder_segments: int32 [32, 128], P('dp'), may hold values from 0 to 2, never falling along the last dimension, each value on 1 to 64 neighbouring positions
- target_segments: int32 [32, 128], P('dp'), may hold values from 0 to 2, never falling along the last dimension, each value on 1 to 64 neighbouring positions
- embedding: bfloat16 [384, 1472], replicated, may hold values from -6 to 6
- attention_in: bfloat16 [2, 1472, 1152], P('section', None, 'dp'), may hold values from -0.15625 to 0.15625
- attention_out: bfloat16 [2, 384, 1472], P('section', 'dp'), may hold values from -0.875 to 0.875
- widen_weight: bfloat16 [2, 1472, 7168], P('section', None, 'dp'), may hold values from -0.15625 to 0.15625
- narrow_weight: bfloat16 [2, 3584, 1472], P('section', 'dp'), may hold values from -0.09375 to 0.09375
- cross_first: bfloat16 [2, 1472, 384], P('section', None, 'dp'), may hold values from -0.15625 to 0.15625
- cross_second: bfloat16 [2, 1472, 384], P('section', None, 'dp'), may hold values from -0.4375 to 0.4375
- norm_gains: bfloat16 [2, 3, 1472], P('section'), may hold values from 0.5 to 1.5
- cotangent: bfloat16 [2, 32, 128, 1472], P('section', 'dp'), may hold values from -6 to 6
Outputs:
- block_outputs: bfloat16 [2, 32, 128, 1472], P('section', 'dp')
- embedding_grad: float32 [384, 1472], replicated
- attention_in_grad: float32 [2, 1472, 1152], P('section', None, 'dp')
- attention_out_grad: float32 [2, 384, 1472], P('section', 'dp')
- widen_grad: float32 [2, 1472, 7168], P('section', None, 'dp')
- narrow_grad: float32 [2, 3584, 1472], P('section', 'dp')
- cross_first_grad: float32 [2, 1472, 384], P('section', None, 'dp')
- cross_second_grad: float32 [2, 1472, 384], P('section', None, 'dp')
- norm_gains_grad: float32 [2, 3, 1472], P('section')
The draws below stay inside these ranges and needn't reach their ends.
Inputs may be any that keep to these rules, and one draw needn't show every extreme that they name: `encoder_segments`: non-decreasing along each row; every number from 0 to 2 occurs in each row, at most 128 // 2 times. `target_segments`: non-decreasing along each row; every number from 0 to 2 occurs in each row, at most 128 // 2 times.
All inputs are finite; a program needn't handle non-finite values.
Results may differ from the reference program's by a relative error of at most 0.023.
Values may be sent and summed in bfloat16 or wider, within the bound.
No kernel may reach another device: no remote copies, remote signals or barrier semaphores. Data moves between devices by JAX's collectives and lax.ppermute only.
A program may use at most 512 MiB of HBM per device.

```python
import math
import jax
import jax.numpy as jnp
import numpy as np
from jax import lax

D = 1472
FF = 3584
HEADS = 6
HEAD_DIM = 64
VOCAB = 384
LEN = 128
SEGS = 3
INNER = 384
ROWS = 32


def place_ends(drawn, stream_key, low, top_value):
    place = [jax.random.randint(jax.random.fold_in(stream_key, axis), (), 0, length) for axis, length in enumerate(drawn.shape)]
    main_axis = drawn.shape.index(max(drawn.shape))
    next_to = place[:main_axis] + [(place[main_axis] + 1) % drawn.shape[main_axis]] + place[main_axis + 1:]
    return drawn.at[tuple(place)].set(low).at[tuple(next_to)].set(top_value)


def block_scale(stream_key, extent, pieces, smallest, high):
    loudness = 1.0
    for axis_at, parts in pieces:
        heights = jax.random.uniform(jax.random.fold_in(jax.random.fold_in(stream_key, 6), axis_at), (parts,), jnp.float32, smallest / len(pieces), high / len(pieces))
        loudness = loudness * jnp.repeat(jnp.exp(heights), extent[axis_at] // parts).reshape((-1,) + (1,) * (len(extent) - 1 - axis_at))
    return loudness


def length_profile(amount, total, limit, skew):
    weights = [(1 << 20) // math.isqrt(standing ** skew) + 1 for standing in range(2, amount + 1)]
    spare, given = total - limit - (amount - 1), [1] * (amount - 1)
    while spare > 0:
        free = [i for i in range(amount - 1) if given[i] < limit]
        whole, left = sum([weights[i] for i in free]), spare
        for i in free:
            addition = min(limit - given[i], max(1, left * weights[i] // whole), spare)
            given[i] = given[i] + addition
            spare = spare - addition
    return np.array([limit] + given)


def uneven_parts(stream_key, amount, total, most, skew):
    if amount == 2:
        one = jax.random.randint(stream_key, (), max(1, total - most), min(most, total - 1) + 1)
        return jnp.stack([one, total - one])
    tallies = jnp.asarray(length_profile(amount, total, most, skew), jnp.int32)
    pairs = (amount - 1) // 2
    source_of, receiver = tallies[1:1 + 2 * pairs:2], tallies[2:2 + 2 * pairs:2]
    slack = jnp.minimum(source_of - 1, most - receiver)
    passed = jax.random.randint(jax.random.fold_in(stream_key, 1), (pairs,), 0, 1 << 20) % (slack + 1)
    tallies = tallies.at[1:1 + 2 * pairs:2].set(source_of - passed).at[2:2 + 2 * pairs:2].set(receiver + passed)
    return tallies[jax.random.permutation(jax.random.fold_in(stream_key, 2), amount)]


def noise(own_key, extent, spread, limit, pieces=(), held_as=jnp.bfloat16):
    values = jax.random.normal(own_key, extent, jnp.float32) * spread
    if len(pieces) > 0:
        values = block_scale(own_key, extent, pieces, -0.22, 0.18) * values
    return jnp.clip(values, min=-limit, max=limit).astype(held_as)


def setup_inputs(seed: int = 0) -> dict:
    seeds = jax.random.split(jax.random.key(seed), 13)
    byte_codes = place_ends(jax.random.randint(seeds[0], (2, ROWS, LEN), 0, VOCAB), jax.random.fold_in(seeds[0], 1), 0, VOCAB - 1).astype(jnp.int32)
    encoder_segments = jax.vmap(lambda own: jnp.searchsorted(jnp.cumsum(uneven_parts(own, SEGS, LEN, LEN // 2, 0)), jnp.arange(LEN), side="right"))(jax.random.split(seeds[1], ROWS)).reshape((ROWS, LEN)).astype(jnp.int32)
    target_segments = jax.vmap(lambda own: jnp.searchsorted(jnp.cumsum(uneven_parts(own, SEGS, LEN, LEN // 2, 0)), jnp.arange(LEN), side="right"))(jax.random.split(seeds[2], ROWS)).reshape((ROWS, LEN)).astype(jnp.int32)
    embedding = noise(seeds[3], (VOCAB, D), 1.0, 6.0)
    attention_in = noise(seeds[4], (2, D, 3 * INNER), D ** -0.5, 0.15625, ((0, 2), (2, 16)))
    attention_out = noise(seeds[5], (2, INNER, D), (INNER // 8) ** -0.5, 0.875, ((0, 2), (1, 16)))
    widen_weight = noise(seeds[6], (2, D, 2 * FF), D ** -0.5, 0.15625, ((0, 2), (2, 16)))
    narrow_weight = noise(seeds[7], (2, FF, D), FF ** -0.5, 0.09375, ((0, 2), (1, 16)))
    cross_first = noise(seeds[8], (2, D, INNER), D ** -0.5, 0.15625, ((0, 2), (2, 16)))
    cross_second = noise(seeds[9], (2, D, INNER), (INNER // 2) ** -0.5, 0.4375, ((0, 2), (2, 16)))
    norm_gains = jnp.clip(1.0 + 0.1 * jax.random.normal(seeds[10], (2, 3, D), jnp.float32), 0.5, 1.5).astype(jnp.bfloat16)
    cotangent = noise(seeds[11], (2, ROWS, LEN, D), 1.0, 6.0, ((0, 2), (1, 16)))
    return dict(byte_codes=byte_codes, encoder_segments=encoder_segments, target_segments=target_segments, embedding=embedding, attention_in=attention_in, attention_out=attention_out, widen_weight=widen_weight, narrow_weight=narrow_weight, cross_first=cross_first, cross_second=cross_second, norm_gains=norm_gains, cotangent=cotangent)


@jax.custom_vjp
def low(v):
    return lax.optimization_barrier(v.astype(jnp.bfloat16)).astype(jnp.float32)

@jax.custom_vjp
def low_back(v):
    return v

def low_keep(v):
    return (low(v), None)

def low_pass(kept, grad):
    return (grad,)

def back_keep(v):
    return (v, None)

def back_low(kept, grad):
    return (low(grad),)
low.defvjp(low_keep, low_pass)
low_back.defvjp(back_keep, back_low)
epsilon = 1e-06
masked_value = -1000000000.0
precise = lax.Precision.HIGHEST

def round_both(value):
    return low(low_back(value))

def product(first_factor, second_factor):
    return jnp.dot(first_factor, second_factor, precision=precise)

def rms_norm(inputs, gain_row):
    return inputs * lax.rsqrt(lax.optimization_barrier(jnp.mean(inputs * inputs, -1, keepdims=True)) + epsilon) * gain_row

def split_heads(matrix):
    return matrix.reshape(matrix.shape[0], HEADS, HEAD_DIM)

def attend(queries, key_rows, value_rows, allowed):
    raw_scores = HEAD_DIM ** (-0.5) * jnp.einsum('qhd,khd->hqk', split_heads(queries), split_heads(key_rows), precision=precise)
    scores = jnp.where(allowed[None], low_back(raw_scores), masked_value)
    attend_weights = low(jax.nn.softmax(scores, axis=-1))
    context = jnp.einsum('hqk,khd->qhd', attend_weights, split_heads(value_rows), precision=precise)
    return round_both(context.reshape(queries.shape))

def self_branch(inputs, gain_row, in_weight, out_weight, allowed):
    normed = low(rms_norm(inputs, gain_row))
    projected = round_both(product(normed, in_weight))
    inner_width = out_weight.shape[0]
    context = attend(projected[:, :inner_width], projected[:, inner_width:2 * inner_width], projected[:, 2 * inner_width:], allowed)
    return low_back(product(context, out_weight))

def feed_branch(inputs, gain_row, widen, narrow):
    normed = low(rms_norm(inputs, gain_row))
    gate_up = low_back(product(normed, widen))
    half_width = gate_up.shape[1] // 2
    hidden = low(jax.nn.gelu(gate_up[:, :half_width], approximate=True) * gate_up[:, half_width:])
    return low_back(product(hidden, narrow))

def encoder_row(inputs, segments, in_weight, out_weight, widen, narrow, first_cross, second_cross, gain_rows):
    allowed = segments[:, None] == segments[None, :]
    first_sum = inputs + self_branch(inputs, gain_rows[0], in_weight, out_weight, allowed)
    second_sum = first_sum + feed_branch(first_sum, gain_rows[1], widen, narrow)
    normed = low(rms_norm(second_sum, gain_rows[2]))
    states = round_both(product(normed, jnp.concatenate([first_cross, second_cross], 1)))
    return (second_sum, states)

def decoder_row(inputs, segments, encoder_seg, states, in_weight, out_weight, widen, narrow, first_cross, second_cross, gain_rows):
    positions = jnp.arange(segments.shape[0])
    allowed = (segments[:, None] == segments[None, :]) & (positions[None, :] <= positions[:, None])
    first_sum = inputs + self_branch(inputs, gain_rows[0], in_weight, out_weight, allowed)
    normed = low(rms_norm(first_sum, gain_rows[1]))
    queries = round_both(product(normed, first_cross))
    inner_width = first_cross.shape[1]
    context = attend(queries, states[:, :inner_width], states[:, inner_width:], segments[:, None] == encoder_seg[None, :])
    second_sum = first_sum + low_back(product(context, second_cross.T))
    return second_sum + feed_branch(second_sum, gain_rows[2], widen, narrow)

def forward(weights, byte_codes, encoder_segments, target_segments):
    embedding, attention_in, attention_out, widen_weight, narrow_weight, cross_first, cross_second, norm_gains = weights

    def row_pair(encoder_codes, target_codes, encoder_seg, target_seg):
        encoder_out, states = encoder_row(embedding[encoder_codes], encoder_seg, attention_in[0], attention_out[0], widen_weight[0], narrow_weight[0], cross_first[0], cross_second[0], norm_gains[0])
        target_out = decoder_row(embedding[target_codes], target_seg, encoder_seg, states, attention_in[1], attention_out[1], widen_weight[1], narrow_weight[1], cross_first[1], cross_second[1], norm_gains[1])
        return (encoder_out, target_out)
    row_count = encoder_segments.shape[0]
    group_size = math.gcd(row_count, 16)

    def scan_step(carried, block_data):
        return (carried, jax.vmap(row_pair)(*block_data))
    blocks = tuple((source.reshape((row_count // group_size, group_size) + source.shape[1:]) for source in (byte_codes[0], byte_codes[1], encoder_segments, target_segments)))
    _, (encoder_out, target_out) = lax.scan(jax.checkpoint(scan_step), jnp.zeros((), jnp.float32), blocks)
    full_shape = (row_count, encoder_segments.shape[1], embedding.shape[1])
    return (encoder_out.reshape(full_shape), target_out.reshape(full_shape))

def reference(byte_codes, encoder_segments, target_segments, embedding, attention_in, attention_out, widen_weight, narrow_weight, cross_first, cross_second, norm_gains, cotangent):
    weights = tuple((source.astype(jnp.float32) for source in (embedding, attention_in, attention_out, widen_weight, narrow_weight, cross_first, cross_second, norm_gains)))

    def forward_only(weight_set):
        return forward(weight_set, byte_codes, encoder_segments, target_segments)
    outputs, pull_back = jax.vjp(forward_only, weights)
    gradients = pull_back((cotangent[0].astype(jnp.float32), cotangent[1].astype(jnp.float32)))[0]
    stacked = jnp.stack(outputs).astype(jnp.bfloat16)
    return (stacked, gradients[0], gradients[1], gradients[2], gradients[3], gradients[4], gradients[5], gradients[6], gradients[7])
```

```python
import jax
import jax.numpy as jnp
from jax import lax
from jax.sharding import Mesh, PartitionSpec as P

HEADS = 6
HEAD_DIM = 64
PLANE = 4

epsilon = 1e-06
masked_value = -1000000000.0
AXES = ("section", "line", "plane")
bf16 = jnp.bfloat16
f32 = jnp.float32


def nn(a, b):
    return lax.dot_general(a, b, (((1,), (0,)), ((), ())), preferred_element_type=f32)


def nt(a, b):
    return lax.dot_general(a, b, (((1,), (1,)), ((), ())), preferred_element_type=f32)


def tn(a, b):
    return lax.dot_general(a, b, (((0,), (0,)), ((), ())), preferred_element_type=f32)


def rms_norm(inputs, gain_row):
    return inputs * lax.rsqrt(jnp.mean(inputs * inputs, -1, keepdims=True) + epsilon) * gain_row


def rms_back(inputs, gain_row, upstream):
    scale = lax.rsqrt(jnp.mean(inputs * inputs, -1, keepdims=True) + epsilon)
    normed = inputs * scale
    weighted = upstream * gain_row
    grad = (weighted - normed * jnp.mean(weighted * normed, -1, keepdims=True)) * scale
    return grad, jnp.sum(upstream * normed, 0)


def gated_value(gate_part, up_part):
    return jax.nn.gelu(gate_part, approximate=True) * up_part


def heads_of(matrix, rows):
    return matrix.reshape(rows, -1, HEADS, HEAD_DIM)


def score_table(queries, keys, allowed):
    raw = jnp.einsum("rqhd,rkhd->rhqk", queries, keys, preferred_element_type=f32)
    return jnp.where(allowed[:, None], raw * HEAD_DIM ** (-0.5), masked_value)


def attend(queries, keys, values, allowed):
    rows = allowed.shape[0]
    scores = score_table(heads_of(queries, rows), heads_of(keys, rows), allowed)
    top = jnp.max(scores, -1, keepdims=True)
    exponent = jnp.exp(scores - top)
    totals = jnp.sum(exponent, -1, keepdims=True)
    weights = (exponent / totals).astype(bf16)
    context = jnp.einsum("rhqk,rkhd->rqhd", weights, heads_of(values, rows), preferred_element_type=f32)
    return context.reshape(queries.shape).astype(bf16), top + jnp.log(totals)


def attend_back(queries, keys, values, allowed, log_total, context_grad):
    rows = allowed.shape[0]
    q, k, v, g = (heads_of(m, rows) for m in (queries, keys, values, context_grad))
    chances = jnp.exp(score_table(q, k, allowed) - log_total)
    weight_grad = jnp.einsum("rqhd,rkhd->rhqk", g, v, preferred_element_type=f32)
    value_grad = jnp.einsum("rhqk,rqhd->rkhd", chances.astype(bf16), g, preferred_element_type=f32)
    score_grad = (
        chances * (weight_grad - jnp.sum(weight_grad * chances, -1, keepdims=True))
    ).astype(bf16)
    query_grad = jnp.einsum("rhqk,rkhd->rqhd", score_grad, k, preferred_element_type=f32)
    key_grad = jnp.einsum("rhqk,rqhd->rkhd", score_grad, q, preferred_element_type=f32)
    scale = HEAD_DIM ** (-0.5)
    shape = queries.shape
    return (
        (query_grad.reshape(shape) * scale).astype(bf16),
        (key_grad.reshape(shape) * scale).astype(bf16),
        value_grad.reshape(shape).astype(bf16),
    )


def build(lines):
    devices = lines * PLANE

    def place(section, line, plane):
        return section * devices + line * PLANE + plane

    def hop(block, offset, sections=(0, 1)):
        route = [
            (place(s, z, j), place(s, z, j ^ offset))
            for s in sections
            for z in range(lines)
            for j in range(PLANE)
        ]
        return lax.ppermute(block, AXES, route)

    def cross(block, sources):
        return lax.ppermute(block, "section", [(s, 1 - s) for s in sources])

    def along(block, step):
        route = [(z, z + step) for z in range(lines) if 0 <= z + step < lines]
        return lax.ppermute(block, "line", route)

    def narrow_route(section, half):
        route = []
        for block in range(devices):
            target = (block % 2, 2 * (block // 8) + half, (block % 8) // 2)
            route.append((section * devices + block, place(*target)))
        return route

    def gather_line(block):
        if lines > 8:
            return lax.all_gather(block, "line", axis=0)
        z = lax.axis_index("line")
        right, left = [block], [block]
        for _ in range(lines - 1):
            right.append(along(right[-1], 1))
            left.append(along(left[-1], -1))
        out = jnp.zeros((lines,) + block.shape, block.dtype)
        out = lax.dynamic_update_index_in_dim(out, block, z, 0)
        for step in range(1, lines):
            piece = jnp.where(z >= step, right[step], left[lines - step])
            out = lax.dynamic_update_index_in_dim(out, piece, lax.rem(z - step + lines, lines), 0)
        return out

    def scatter_line(partial):
        if lines > 8:
            return lax.psum_scatter(partial, "line", scatter_dimension=0).astype(f32)
        z = lax.axis_index("line")

        def own(index):
            return lax.dynamic_index_in_dim(partial, jnp.clip(index, 0, lines - 1), 0, False).astype(f32)

        right = left = None
        for step in range(1, lines):
            to_right, to_left = own(z + lines - step), own(z - lines + step)
            if right is not None:
                to_right, to_left = to_right + right.astype(f32), to_left + left.astype(f32)
            right, left = along(to_right.astype(bf16), 1), along(to_left.astype(bf16), -1)
        return own(z) + right.astype(f32) + left.astype(f32)

    def gather_plane(block):
        j = lax.axis_index("plane")
        out = jnp.zeros((PLANE,) + block.shape, block.dtype)
        out = lax.dynamic_update_index_in_dim(out, block, j, 0)
        for offset in range(1, PLANE):
            out = lax.dynamic_update_index_in_dim(out, hop(block, offset), j ^ offset, 0)
        return out

    def gather_all(block):
        column = gather_line(block)
        return gather_plane(column).swapaxes(0, 1).reshape((devices,) + block.shape)

    def scatter_all(partial):
        j = lax.axis_index("plane")
        parts = partial.reshape((lines, PLANE) + partial.shape[1:])
        total = lax.dynamic_index_in_dim(parts, j, 1, False).astype(f32)
        for offset in range(1, PLANE):
            sent = lax.dynamic_index_in_dim(parts, j ^ offset, 1, False)
            total = total + hop(sent, offset).astype(f32)
        return scatter_line(total.astype(bf16))

    def per_device(
        byte_codes,
        encoder_segments,
        target_segments,
        embedding,
        attention_in,
        attention_out,
        widen_weight,
        narrow_weight,
        cross_first,
        cross_second,
        norm_gains,
        cotangent,
    ):
        section = lax.axis_index("section")
        z = lax.axis_index("line")
        is_encoder = section == 0
        inner = cross_first.shape[2] * devices
        width = embedding.shape[1]
        rows, length = encoder_segments.shape
        tokens = rows * length
        gains = norm_gains[0].astype(f32)

        def spread(block, source):
            blocks = [block] + [hop(block, k, (source,)) for k in range(1, PLANE)]
            here = section == source
            return jnp.concatenate([jnp.where(here, b, cross(b, (source,))) for b in blocks], 0)

        def collect(partial, source):
            partial = partial.astype(bf16)
            total = (partial.astype(f32) + cross(partial, (1 - source,)).astype(f32)).reshape(
                PLANE, tokens, width
            )
            result = total[0]
            for k in range(1, PLANE):
                result = result + hop(total[k].astype(bf16), k, (source,)).astype(f32)
            return result

        in_cols = attention_in.shape[2]
        cross_cols = cross_first.shape[2]
        out_rows = attention_out.shape[1]
        attention_pack = jnp.concatenate(
            [attention_in[0].T, cross_first[0].T, cross_second[0].T, attention_out[0]], 0
        )
        cuts = (0, in_cols, in_cols + cross_cols, in_cols + 2 * cross_cols, attention_pack.shape[0])
        widen_half = widen_weight.shape[2] // 2
        halves = widen_weight[0].T.reshape(2, widen_half, width)
        kept = lax.dynamic_index_in_dim(halves, section, 0, False)
        got = cross(lax.dynamic_index_in_dim(halves, 1 - section, 0, False), (0, 1))
        narrow_half = narrow_weight.shape[1] // 2
        narrow_parts = narrow_weight[0].reshape(2, narrow_half, width)
        even_line = lax.rem(z, 2) == 0

        def feed_weights(own_section):
            widen_piece = jnp.where(section == own_section, kept, got)
            pieces = [
                lax.ppermute(narrow_parts[half], AXES, narrow_route(own_section, half))
                for half in range(2)
            ]
            narrow_piece = jnp.where(even_line, pieces[0], pieces[1])
            full = lax.all_gather(jnp.concatenate([widen_piece, narrow_piece], 0), "line", axis=0)
            return (
                full[: lines // 2, :widen_half].reshape(-1, width),
                full[lines // 2 :, :widen_half].reshape(-1, width),
                full[:, widen_half:].reshape(-1, width),
            )

        encoder_feed = feed_weights(0)
        decoder_feed = feed_weights(1)
        gathered = gather_all(attention_pack)
        in_t, first_t, second_t, out_w = (
            gathered[:, cuts[i] : cuts[i + 1]].reshape(-1, width) for i in range(4)
        )

        codes = byte_codes[0].reshape(tokens)
        one_hot = (
            codes[:, None] == lax.broadcasted_iota(jnp.int32, (tokens, embedding.shape[0]), 1)
        ).astype(bf16)
        inputs = nn(one_hot, embedding)
        own_segments = jnp.where(is_encoder, encoder_segments, target_segments)
        earlier = lax.broadcasted_iota(jnp.int32, (length, length), 1) <= lax.broadcasted_iota(
            jnp.int32, (length, length), 0
        )
        allowed = (own_segments[:, :, None] == own_segments[:, None, :]) & (earlier | is_encoder)[None]
        normed_self = rms_norm(inputs, gains[0]).astype(bf16)
        projected = nt(normed_self, in_t).astype(bf16)
        queries, keys, values = (projected[:, i * inner : (i + 1) * inner] for i in range(3))
        context, log_total = attend(queries, keys, values, allowed)
        first_sum = inputs + nn(context, out_w)
        normed_first = rms_norm(first_sum, gains[1]).astype(bf16)

        def feed_forward(stream, weights):
            gate, up = nt(stream, weights[0]), nt(stream, weights[1])
            hidden = gated_value(gate, up).astype(bf16)
            return gate, up, hidden, nn(hidden, weights[2])

        def feed_back(output_grad, gate, up, weights):
            hidden_grad = nt(output_grad, weights[2])
            _, pull_back = jax.vjp(gated_value, gate, up)
            gate_grad, up_grad = (part.astype(bf16) for part in pull_back(hidden_grad))
            return gate_grad, up_grad, nn(gate_grad, weights[0]) + nn(up_grad, weights[1])

        def feed_grads(stream, hidden, gate_grad, up_grad, output_grad):
            gate_part = tn(gate_grad, stream).astype(bf16).reshape(lines // 2, widen_half, width)
            up_part = tn(up_grad, stream).astype(bf16).reshape(lines // 2, widen_half, width)
            narrow_part = tn(hidden, output_grad).astype(bf16).reshape(lines, narrow_half, width)
            pack = jnp.concatenate([jnp.concatenate([gate_part, up_part], 0), narrow_part], 1)
            return lax.psum_scatter(pack, "line", scatter_dimension=0)

        stream_e = spread(normed_first, 0)
        gate_e, up_e, hidden_e, part_e = feed_forward(stream_e, encoder_feed)
        second_e = first_sum + collect(part_e, 0)
        normed_final = rms_norm(second_e, gains[2]).astype(bf16)
        first_product = nt(jnp.where(is_encoder, normed_final, normed_first), first_t).astype(bf16)
        second_product = nt(normed_final, second_t).astype(bf16)
        states = cross(jnp.concatenate([first_product, second_product], 1), (0,))

        cross_queries, state_keys, state_values = first_product, states[:, :inner], states[:, inner:]
        cross_allowed = target_segments[:, :, None] == encoder_segments[:, None, :]
        cross_context, cross_total = attend(cross_queries, state_keys, state_values, cross_allowed)
        second_t_sum = first_sum + nn(cross_context, second_t)
        normed_last = rms_norm(second_t_sum, gains[2]).astype(bf16)
        own_cotangent = cotangent[0].reshape(tokens, width)
        cotangent_d = spread(own_cotangent, 1)
        stream_d = spread(normed_last, 1)
        gate_d, up_d, hidden_d, part_d = feed_forward(stream_d, decoder_feed)
        gate_grad_d, up_grad_d, back_d = feed_back(cotangent_d, gate_d, up_d, decoder_feed)
        last_grad = collect(back_d, 1)
        outputs_d = second_t_sum + collect(part_d, 1)
        summed_d = feed_grads(stream_d, hidden_d, gate_grad_d, up_grad_d, cotangent_d)
        long_cotangent = own_cotangent.astype(f32)
        input_grad, gain_two_d = rms_back(second_t_sum, gains[2], last_grad)
        stream_two_d = long_cotangent + input_grad
        cross_branch = stream_two_d.astype(bf16)
        cross_context_grad = nt(cross_branch, second_t).astype(bf16)
        cross_query_grad, state_key_grad, state_value_grad = attend_back(
            cross_queries, state_keys, state_values, cross_allowed, cross_total, cross_context_grad
        )
        state_grads = cross(jnp.concatenate([state_key_grad, state_value_grad], 1), (1,))
        input_grad, gain_one_d = rms_back(first_sum, gains[1], nn(cross_query_grad, first_t))
        stream_one_d = stream_two_d + input_grad

        key_grads, value_grads = state_grads[:, :inner], state_grads[:, inner:]
        final_grad = nn(key_grads, first_t) + nn(value_grads, second_t)
        input_grad, gain_two_e = rms_back(second_e, gains[2], final_grad)
        stream_two_e = long_cotangent + input_grad
        output_grad_e = spread(stream_two_e.astype(bf16), 0)
        gate_grad_e, up_grad_e, back_e = feed_back(output_grad_e, gate_e, up_e, encoder_feed)
        middle_grad = collect(back_e, 0)
        summed_e = feed_grads(stream_e, hidden_e, gate_grad_e, up_grad_e, output_grad_e)
        input_grad, gain_one_e = rms_back(first_sum, gains[1], middle_grad)
        stream_one_e = stream_two_e + input_grad

        stream_one = jnp.where(is_encoder, stream_one_e, stream_one_d)
        branch_grad = stream_one.astype(bf16)
        context_grad = nt(branch_grad, out_w).astype(bf16)
        projected_grad = jnp.concatenate(
            attend_back(queries, keys, values, allowed, log_total, context_grad), 1
        )
        input_grad, gain_zero = rms_back(inputs, gains[0], nn(projected_grad, in_t))
        table_grad = tn(one_hot, (stream_one + input_grad).astype(bf16))

        first_left = jnp.where(is_encoder, key_grads, cross_query_grad)
        first_right = jnp.where(is_encoder, normed_final, normed_first)
        second_left = jnp.where(is_encoder, value_grads, cross_context)
        second_right = jnp.where(is_encoder, normed_final, cross_branch)
        products = (
            tn(projected_grad, normed_self),
            tn(first_left, first_right),
            tn(second_left, second_right),
            tn(context, branch_grad),
        )
        attention_sum = scatter_all(
            jnp.concatenate([m.astype(bf16).reshape(devices, -1, width) for m in products], 1)
        )

        gain_rows = jnp.stack(
            [
                gain_zero,
                jnp.where(is_encoder, gain_one_e, gain_one_d),
                jnp.where(is_encoder, gain_two_e, gain_two_d),
            ]
        )
        slot = lax.broadcasted_iota(jnp.int32, (2, 1, 1), 0)
        gain_slots = jnp.where(slot == section, gain_rows[None], 0.0)
        summed_gains, embedding_grad = lax.psum((gain_slots, table_grad), AXES)
        gains_grad = lax.dynamic_slice_in_dim(summed_gains, section, 1, 0)

        kept_half = jnp.where(is_encoder, summed_e[:widen_half], summed_d[:widen_half])
        sent_half = jnp.where(is_encoder, summed_d[:widen_half], summed_e[:widen_half])
        got_half = cross(sent_half, (0, 1))
        widen_t = jnp.where(
            is_encoder,
            jnp.concatenate([kept_half, got_half], 0),
            jnp.concatenate([got_half, kept_half], 0),
        )
        returned = []
        for own_section, summed in ((0, summed_e), (1, summed_d)):
            returned.append(
                jnp.concatenate(
                    [
                        lax.ppermute(
                            summed[widen_half:], AXES, [(b, a) for a, b in narrow_route(own_section, half)]
                        )
                        for half in range(2)
                    ],
                    0,
                )
            )
        narrow_grad = jnp.where(is_encoder, returned[0], returned[1]).astype(f32)

        block_output = jnp.where(is_encoder, second_e, outputs_d).astype(bf16)
        return (
            block_output.reshape(1, rows, length, width),
            embedding_grad,
            attention_sum[cuts[0] : cuts[1]].T[None],
            attention_sum[cuts[3] : cuts[4]][None],
            widen_t.astype(f32).T[None],
            narrow_grad[None],
            attention_sum[cuts[1] : cuts[2]].T[None],
            attention_sum[cuts[2] : cuts[3]].T[None],
            gains_grad,
        )

    return per_device


def solution(mesh):
    lines = mesh.shape["dp"] // PLANE
    inner_mesh = Mesh(mesh.devices.reshape(2, lines, PLANE), AXES)
    dp = ("line", "plane")
    return jax.shard_map(
        build(lines),
        mesh=inner_mesh,
        in_specs=(
            P("section", dp, None),
            P(dp, None),
            P(dp, None),
            P(),
            P("section", None, dp),
            P("section", dp, None),
            P("section", None, dp),
            P("section", dp, None),
            P("section", None, dp),
            P("section", None, dp),
            P("section", None, None),
            P("section", dp, None, None),
        ),
        out_specs=(
            P("section", dp, None, None),
            P(),
            P("section", None, dp),
            P("section", dp, None),
            P("section", None, dp),
            P("section", dp, None),
            P("section", None, dp),
            P("section", None, dp),
            P("section", None, None),
        ),
        check_vma=False,
    )
```

```python
import functools

import jax
import jax.numpy as jnp
from jax import lax
from jax.experimental import pallas as pl
from jax.experimental.pallas import tpu as pltpu
from jax.sharding import Mesh, PartitionSpec as P

HEADS = 6
HEAD_DIM = 64
PLANE = 4
SCALE = HEAD_DIM ** (-0.5)

epsilon = 1e-06
masked_value = -1000000000.0
AXES = ("section", "line", "plane")
bf16 = jnp.bfloat16
f32 = jnp.float32


def nn(a, b):
    return lax.dot_general(a, b, (((1,), (0,)), ((), ())), preferred_element_type=f32)


def nt(a, b):
    return lax.dot_general(a, b, (((1,), (1,)), ((), ())), preferred_element_type=f32)


def tn(a, b):
    return lax.dot_general(a, b, (((0,), (0,)), ((), ())), preferred_element_type=f32)


def permute(block, axes, route):
    shape = block.shape
    if block.ndim == 2 and shape[0] % 8 == 0:
        block = block.reshape(shape[0] // 8, 8, shape[1])
    return lax.ppermute(block, axes, route).reshape(shape)


def rounded(value):
    return lax.reduce_precision(value, 8, 7).astype(bf16)


def rms_norm(inputs, gain_row):
    return inputs * lax.rsqrt(jnp.mean(inputs * inputs, -1, keepdims=True) + epsilon) * gain_row


def rms_back(inputs, gain_row, upstream):
    scale = lax.rsqrt(jnp.mean(inputs * inputs, -1, keepdims=True) + epsilon)
    normed = inputs * scale
    weighted = upstream * gain_row
    grad = (weighted - normed * jnp.mean(weighted * normed, -1, keepdims=True)) * scale
    return grad, jnp.sum(upstream * normed, 0, keepdims=True)


def gelu_parts(gate):
    slope = (2.0 / jnp.pi) ** 0.5
    cube = 0.044715 * gate * gate
    bent = jnp.tanh(slope * gate * (1.0 + cube))
    half = 0.5 * (1.0 + bent)
    return half * gate, half + 0.5 * gate * (1.0 - bent * bent) * slope * (1.0 + 3.0 * cube)


def whole(shape):
    return pl.BlockSpec(shape, lambda step: (0,) * len(shape))


def call(kernel, outputs, *args, scratch=(), steps=1, specs=None, time_us=5, ties=()):
    specs = specs or {}
    in_specs = [
        specs.get(i)
        or (pl.BlockSpec(memory_space=pltpu.SMEM) if a.dtype == jnp.int32 else whole(a.shape))
        for i, a in enumerate(args)
    ]
    in_specs += [pl.BlockSpec(memory_space=pl.ANY)] * len(ties)
    first, after = len(args), len(args) + len(ties)
    out_shape = tuple(jax.ShapeDtypeStruct(output[0], output[1]) for output in outputs)
    return pl.pallas_call(
        lambda *refs: kernel(*refs[:first], *refs[after:]),
        grid=(steps,),
        out_shape=out_shape,
        in_specs=in_specs,
        out_specs=tuple(output[2] if len(output) > 2 else whole(output[0]) for output in outputs),
        scratch_shapes=list(scratch),
        compiler_params=pltpu.CompilerParams(vmem_limit_bytes=56 * 1024 * 1024),
        cost_estimate=pl.CostEstimate(
            flops=int(time_us * 8e8), bytes_accessed=int(time_us * 2.5e6), transcendentals=0
        ),
    )(*args, *ties)


def chances_of(queries, keys, allowed):
    scores = jnp.where(allowed > 0, tn(queries, keys) * SCALE, masked_value)
    exponent = jnp.exp(scores - jnp.max(scores, -1, keepdims=True))
    return exponent / jnp.sum(exponent, -1, keepdims=True)


def attend_into(context_ref, query_ref, key_ref, value_ref, allowed_ref, starts=(0, 0, 0)):
    rows, length, _ = allowed_ref.shape
    for row in range(rows):
        columns = slice(row * length, (row + 1) * length)
        for head in range(HEADS):
            q, k, v = (
                ref[start + head * HEAD_DIM : start + (head + 1) * HEAD_DIM, columns]
                for ref, start in zip((query_ref, key_ref, value_ref), starts)
            )
            weights = chances_of(q, k, allowed_ref[row]).astype(bf16)
            context_ref[head * HEAD_DIM : (head + 1) * HEAD_DIM, columns] = nt(v, weights).astype(bf16)


def attend_back_into(grads_ref, query_ref, key_ref, value_ref, allowed_ref, upstream, starts=(0, 0, 0)):
    rows, length, _ = allowed_ref.shape
    inner = HEADS * HEAD_DIM
    for row in range(rows):
        columns = slice(row * length, (row + 1) * length)
        for head in range(HEADS):
            first = head * HEAD_DIM
            q, k, v = (
                ref[start + first : start + first + HEAD_DIM, columns]
                for ref, start in zip((query_ref, key_ref, value_ref), starts)
            )
            g = upstream[first : first + HEAD_DIM, columns]
            chances = chances_of(q, k, allowed_ref[row])
            weight_grad = tn(g, v)
            score_grad = (
                chances * (weight_grad - jnp.sum(weight_grad * chances, -1, keepdims=True))
            ).astype(bf16)
            grads = (nt(k, score_grad) * SCALE, nn(q, score_grad) * SCALE, nn(g, chances.astype(bf16)))
            for number, grad in enumerate(grads):
                at = number * inner + first
                grads_ref[at : at + HEAD_DIM, columns] = grad.astype(bf16)


def added(refs):
    total = refs[0][...].astype(f32)
    for ref in refs[1:]:
        total = total + ref[...].astype(f32)
    return total


def split_rows(section, value, kept_ref, sent_ref):
    length = kept_ref.shape[0]
    mine, other = value[:length], value[length:]
    kept_ref[...] = jnp.where(section == 0, mine, other)
    sent_ref[...] = jnp.where(section == 0, other, mine)


def self_forward_kernel(section_ref, projected_ref, allowed_ref, inputs_ref, out_w_ref, context_ref, kept_ref, sent_ref):
    inner = context_ref.shape[0]
    attend_into(context_ref, projected_ref, projected_ref, projected_ref, allowed_ref, (0, inner, 2 * inner))
    first_sum = inputs_ref[...] + tn(context_ref[...], out_w_ref[...])
    split_rows(section_ref[0], first_sum, kept_ref, sent_ref)


def first_norm_kernel(section_ref, kept_ref, got_ref, gains_e_ref, gains_d_ref, first_e_ref, first_d_ref, normed_e_ref, normed_d_ref):
    is_encoder = section_ref[0] == 0
    first_e = jnp.where(is_encoder, kept_ref[...], got_ref[...])
    first_d = jnp.where(is_encoder, got_ref[...], kept_ref[...])
    first_e_ref[...] = first_e
    first_d_ref[...] = first_d
    normed_e_ref[...] = rms_norm(first_e, gains_e_ref[1:2]).astype(bf16)
    normed_d_ref[...] = rms_norm(first_d, gains_d_ref[1:2]).astype(bf16)


def joined(refs, scratch):
    length = refs[0].shape[0]
    for k, ref in enumerate(refs):
        scratch[k * length : (k + 1) * length] = ref[...]
    return scratch[...]


def feed_specs(lines, padded, width):
    half = lines // 2
    return [
        pl.BlockSpec((1, padded, width), lambda step: (step, 0, 0)),
        pl.BlockSpec((1, padded, width), lambda step: (half + step, 0, 0)),
        pl.BlockSpec((2, padded // 2, width), lambda step: (step, 2, 0)),
    ]


def stacked(weights):
    wide = jnp.concatenate([w[0] for pack in weights for w in pack[:2]], 0)
    narrow = jnp.concatenate([half for pack in weights for half in (pack[2][0], pack[2][1])], 0)
    return wide, narrow


def sum_over_steps(total, scratch, out_ref, prior_ref=None):
    step = pl.program_id(0)

    @pl.when(step == 0)
    def _():
        scratch[...] = total if prior_ref is None else total + prior_ref[...].astype(f32)

    @pl.when(step > 0)
    def _():
        scratch[...] += total

    @pl.when(step == pl.num_programs(0) - 1)
    def _():
        out_ref[...] = scratch[...].astype(bf16)


def join_once(refs, scratch):
    @pl.when(pl.program_id(0) == 0)
    def _():
        joined(refs, scratch)


def cut(array, count):
    rows = array.shape[0] // count
    return [array[i * rows : (i + 1) * rows] for i in range(count)]


def feed_forward_kernel(priors, *refs):
    streams, pack, refs = refs[:4], refs[4:7], refs[7:]
    prior_refs, (value_ref, slope_ref, hidden_ref, part_ref, x_ref, part_sum) = refs[:priors], refs[priors:]
    join_once(streams, x_ref)
    wide, narrow = stacked([pack])
    gate, up = cut(nt(wide, x_ref[...]), 2)
    value, slope = gelu_parts(gate)
    value_ref[0, 0] = value.astype(bf16)
    slope_ref[0, 0] = (slope * up).astype(bf16)
    hidden = (value * up).astype(bf16)
    hidden_ref[0, 0] = hidden
    sum_over_steps(tn(hidden, narrow), part_sum, part_ref, *prior_refs)


def feed_back_kernel(*refs):
    outputs, packs, saved = refs[:4], (refs[4:7], refs[7:10]), refs[10:14]
    grads_refs, (back_ref, output_ref, back_sum) = refs[14:16], refs[16:]
    join_once(outputs, output_ref)
    wide, narrow = stacked(packs)
    grads = []
    for core, hidden_grad in enumerate(cut(nt(narrow, output_ref[...]), 2)):
        value_ref, slope_ref = saved[2 * core : 2 * core + 2]
        grads.append((hidden_grad * slope_ref[0, 0].astype(f32)).astype(bf16))
        grads.append((hidden_grad * value_ref[0, 0].astype(f32)).astype(bf16))
        grads_refs[core][0, 0] = grads[-2]
        grads_refs[core][0, 1] = grads[-1]
    sum_over_steps(tn(jnp.concatenate(grads, 0), wide), back_sum, back_ref)


def feed_both_kernel(priors, *refs):
    streams, outputs, pack, refs = refs[:4], refs[4:8], refs[8:11], refs[11:]
    prior_refs, refs = refs[:priors], refs[priors:]
    hidden_ref, grads_ref, part_ref, back_ref, x_ref, output_ref, part_sum, back_sum = refs
    join_once(streams, x_ref)
    join_once(outputs, output_ref)
    wide, narrow = stacked([pack])
    gate, up = cut(nt(wide, x_ref[...]), 2)
    hidden_grad = nt(narrow, output_ref[...])
    value, slope = gelu_parts(gate)
    hidden = (value * up).astype(bf16)
    hidden_ref[0, 0] = hidden
    grads = [(hidden_grad * (slope * up)).astype(bf16), (hidden_grad * value).astype(bf16)]
    grads_ref[0, 0] = grads[0]
    grads_ref[0, 1] = grads[1]
    sum_over_steps(tn(jnp.concatenate(grads, 0), wide), back_sum, back_ref, *prior_refs[1:])
    sum_over_steps(tn(hidden, narrow), part_sum, part_ref, *prior_refs[:1])


def feed_grads_kernel(*refs):
    streams, outputs, grads_refs, hidden_refs = refs[:4], refs[4:8], refs[8:10], refs[10:12]
    own_ref, other_ref, x_ref, output_ref = refs[12:]
    step, steps = pl.program_id(0), pl.num_programs(0)
    padded, rows = grads_refs[0].shape[2:]
    join_once(streams, x_ref)
    join_once(outputs, output_ref)
    for grads_ref, hidden_ref, ref in zip(grads_refs, hidden_refs, (own_ref, other_ref)):
        wide = cut(nn(grads_ref[...].reshape(2 * padded, rows), x_ref[...]), 2)
        narrow = cut(nn(hidden_ref[0, 0], output_ref[...]), 2)
        ref[step, :padded] = wide[0].astype(bf16)
        ref[steps + step, :padded] = wide[1].astype(bf16)
        ref[2 * step, padded:] = narrow[0].astype(bf16)
        ref[2 * step + 1, padded:] = narrow[1].astype(bf16)


def middle_kernel(*refs):
    parts = refs[:4]
    first_e_ref, first_d_ref, normed_d_ref, gains_e_ref, gains_d_ref, cross_e_ref, cross_d_ref, allowed_ref = refs[4:12]
    second_e_ref, normed_e_ref, queries_ref, states_ref, context_ref, second_d_ref, normed_last_ref = refs[12:]
    inner = context_ref.shape[0]
    queries_ref[...] = nt(cross_d_ref[:inner], normed_d_ref[...]).astype(bf16)
    second_e = first_e_ref[...] + added(parts)
    second_e_ref[...] = second_e
    normed = rms_norm(second_e, gains_e_ref[2:3]).astype(bf16)
    normed_e_ref[...] = normed
    states_ref[...] = nt(cross_e_ref[...], normed).astype(bf16)
    attend_into(context_ref, queries_ref, states_ref, states_ref, allowed_ref, (0, 0, inner))
    second_d = first_d_ref[...] + tn(context_ref[...], cross_d_ref[inner:])
    second_d_ref[...] = second_d
    normed_last_ref[...] = rms_norm(second_d, gains_d_ref[2:3]).astype(bf16)


def middle_back_kernel(*refs):
    parts = refs[:4]
    second_d_ref, second_e_ref, cotangent_d_ref, cotangent_e_ref, gains_d_ref, gains_e_ref = refs[4:10]
    cross_d_ref, cross_e_ref, queries_ref, states_ref, allowed_ref = refs[10:15]
    stream_d_ref, branch_ref, grads_ref, stream_e_ref, sent_ref, gain_d_ref, gain_e_ref = refs[15:]
    inner = queries_ref.shape[0]
    input_grad, gain_d_ref[...] = rms_back(second_d_ref[...], gains_d_ref[2:3], added(parts))
    stream_d = cotangent_d_ref[...].astype(f32) + input_grad
    stream_d_ref[...] = stream_d
    branch = stream_d.astype(bf16)
    branch_ref[...] = branch
    context_grad = nt(cross_d_ref[inner:], branch).astype(bf16)
    attend_back_into(grads_ref, queries_ref, states_ref, states_ref, allowed_ref, context_grad, (0, 0, inner))
    final_grad = tn(grads_ref[inner:], cross_e_ref[...])
    input_grad, gain_e_ref[...] = rms_back(second_e_ref[...], gains_e_ref[2:3], final_grad)
    stream_e = cotangent_e_ref[...].astype(f32) + input_grad
    stream_e_ref[...] = stream_e
    sent_ref[...] = stream_e.astype(bf16)


def first_back_d_kernel(grads_ref, cross_d_ref, first_d_ref, gains_d_ref, stream_ref, out_ref, gain_ref):
    inner = cross_d_ref.shape[0] // 2
    upstream = tn(grads_ref[:inner], cross_d_ref[:inner])
    input_grad, gain_ref[...] = rms_back(first_d_ref[...], gains_d_ref[1:2], upstream)
    out_ref[...] = stream_ref[...] + input_grad


def first_back_e_kernel(*refs):
    parts = refs[:4]
    section_ref, first_e_ref, gains_e_ref, stream_ref, stream_d_ref, kept_ref, sent_ref, gain_ref = refs[4:]
    input_grad, gain_ref[...] = rms_back(first_e_ref[...], gains_e_ref[1:2], added(parts))
    stream_e = stream_ref[...] + input_grad
    is_encoder = section_ref[0] == 0
    kept_ref[...] = jnp.where(is_encoder, stream_e, stream_d_ref[...])
    sent_ref[...] = jnp.where(is_encoder, stream_d_ref[...], stream_e)


def self_back_kernel(section_ref, kept_ref, got_ref, out_w_ref, projected_ref, allowed_ref, stream_ref, branch_ref, grads_ref):
    is_encoder = section_ref[0] == 0
    inner, length = out_w_ref.shape[0], kept_ref.shape[0]
    stream_ref[:length] = jnp.where(is_encoder, kept_ref[...], got_ref[...])
    stream_ref[length:] = jnp.where(is_encoder, got_ref[...], kept_ref[...])
    branch = stream_ref[...].astype(bf16)
    branch_ref[...] = branch
    context_grad = nt(out_w_ref[...], branch).astype(bf16)
    attend_back_into(
        grads_ref, projected_ref, projected_ref, projected_ref, allowed_ref, context_grad, (0, inner, 2 * inner)
    )


def table_kernel(grads_ref, in_w_ref, inputs_ref, gain_ref, stream_ref, one_hot_ref, table_ref, gain_grad_ref):
    upstream = tn(grads_ref[...], in_w_ref[...])
    input_grad, gain_grad_ref[...] = rms_back(inputs_ref[...], gain_ref[...], upstream)
    table_ref[...] = tn(one_hot_ref[...], (stream_ref[...] + input_grad).astype(bf16)).astype(bf16)


def in_grad_kernel(*refs):
    grads, streams, out_ref = refs[:4], refs[4:8], refs[8]
    total = nn(grads[0][...], streams[0][...])
    for grad, stream in zip(grads[1:], streams[1:]):
        total = total + nn(grad[...], stream[...])
    out_ref[...] = total.astype(bf16)


def cross_grads_kernel(section_ref, grads_ref, normed_e_ref, normed_d_ref, context_ref, branch_ref, kept_ref, sent_ref):
    inner = context_ref.shape[0]
    is_encoder = section_ref[0] == 0
    grad_e = nn(grads_ref[inner:], normed_e_ref[...])
    grad_first = nn(grads_ref[:inner], normed_d_ref[...])
    grad_second = nn(context_ref[...], branch_ref[...])
    for start, grad_d in ((0, grad_first), (inner, grad_second)):
        part_e = grad_e[start : start + inner]
        kept_ref[start : start + inner] = jnp.where(is_encoder, part_e, grad_d).astype(bf16)
        sent_ref[start : start + inner] = jnp.where(is_encoder, grad_d, part_e).astype(bf16)


def build(lines):
    devices = lines * PLANE

    def place(section, line, plane):
        return section * devices + line * PLANE + plane

    def hop(block, offset):
        route = [
            (place(s, z, j), place(s, z, j ^ offset))
            for s in range(2)
            for z in range(lines)
            for j in range(PLANE)
        ]
        return permute(block, AXES, route)

    def swap(block):
        return permute(block, "section", [(0, 1), (1, 0)])

    narrow_route = []
    for core in range(2):
        for block in range(devices):
            target = (block % 2, 2 * (block // 8) + core, (block % 8) // 2)
            narrow_route.append((core * devices + block, place(*target)))

    def at(array, index, axis=0):
        return lax.dynamic_index_in_dim(array, index, axis, False)

    def ordered(own, others, index, axis=0):
        count = len(others) + 1
        shape = own.shape[:axis] + (count,) + own.shape[axis:]
        out = jnp.zeros(shape, own.dtype)
        for where_to, piece in [(index, own)] + others:
            out = lax.dynamic_update_index_in_dim(out, piece, where_to, axis)
        return out

    def sum_line(block):
        if lines & (lines - 1):
            return rounded(lax.psum(block.astype(f32), "line"))
        distance = 1
        while distance < lines:
            route = [(z, z ^ distance) for z in range(lines)]
            block = rounded(block.astype(f32) + permute(block, "line", route).astype(f32))
            distance *= 2
        return block

    def in_plane(blocks, axis=0):
        j = lax.axis_index("plane")
        return ordered(blocks[0], [(j ^ k, blocks[k]) for k in range(1, PLANE)], j, axis)

    def gather_plane(block, axis=0):
        return in_plane(spread(block), axis)

    def scatter_line(partial):
        if lines > 8:
            return lax.psum_scatter(partial, "line", scatter_dimension=0).astype(f32)
        z = lax.axis_index("line")
        total = at(partial, z).astype(f32)
        for step in range(1, lines):
            for distance in (step, -step):
                route = [(a, a + distance) for a in range(lines) if 0 <= a + distance < lines]
                sent = at(partial, jnp.clip(z + distance, 0, lines - 1))
                total = total + permute(sent, "line", route).astype(f32)
        return total

    def scatter_plane(parts):
        j = lax.axis_index("plane")
        total = at(parts, j).astype(f32)
        for k in range(1, PLANE):
            total = total + hop(at(parts, j ^ k), k).astype(f32)
        return total

    def spread(block):
        return [block] + [hop(block, k) for k in range(1, PLANE)]

    def collected(partial):
        parts = partial.reshape((PLANE, -1) + partial.shape[1:])
        return [parts[0]] + [hop(parts[k], k) for k in range(1, PLANE)]

    def per_device(
        byte_codes,
        encoder_segments,
        target_segments,
        embedding,
        attention_in,
        attention_out,
        widen_weight,
        narrow_weight,
        cross_first,
        cross_second,
        norm_gains,
        cotangent,
    ):
        section = lax.axis_index("section")
        j = lax.axis_index("plane")
        is_encoder = section == 0
        section_scalar = section.astype(jnp.int32).reshape(1)
        inner = cross_first.shape[2] * devices
        vocabulary, width = embedding.shape
        rows, length = encoder_segments.shape
        tokens = rows * length

        def together(*values):
            return lax.optimization_barrier(values)

        def by_section(mine, other):
            return jnp.where(is_encoder, mine, other), jnp.where(is_encoder, other, mine)

        def in_order(mine, other):
            return jnp.concatenate(by_section(mine, other), 0)

        in_cols = attention_in.shape[2]
        cross_cols = cross_first.shape[2]
        column, codes = together(
            jnp.concatenate([attention_in[0].T, attention_out[0], cross_first[0].T, cross_second[0].T], 0),
            byte_codes[0].reshape(tokens),
        )
        column = lax.all_gather(column, "line", axis=0)
        in_column = column[:, :in_cols].reshape(-1, width)

        widen_half = widen_weight.shape[2] // 2
        narrow_half = narrow_weight.shape[1] // 2
        padded_narrow = -(-narrow_half // 16) * 16
        padded_widen = 2 * padded_narrow

        def widened(block):
            return jnp.pad(block, ((0, 0),) * (block.ndim - 2) + ((0, padded_narrow - narrow_half), (0, 0)))

        narrow_parts = widened(narrow_weight[0].reshape(2, narrow_half, width))
        narrow_e, narrow_d = by_section(at(narrow_parts, section), swap(at(narrow_parts, 1 - section)))
        moved = permute(jnp.concatenate([narrow_e, narrow_d], 0), AXES, narrow_route)
        widen_parts = widened(widen_weight[0].T.reshape(2, 2, narrow_half, width)).reshape(
            2, padded_widen, width
        )
        widen_e, widen_d = by_section(at(widen_parts, section), swap(at(widen_parts, 1 - section)))

        one_hot = (
            codes[:, None] == lax.broadcasted_iota(jnp.int32, (tokens, vocabulary), 1)
        ).astype(bf16)
        inputs = nn(one_hot, embedding)
        own_segments = jnp.where(is_encoder, encoder_segments, target_segments)
        earlier = lax.broadcasted_iota(jnp.int32, (length, length), 1) <= lax.broadcasted_iota(
            jnp.int32, (length, length), 0
        )
        allowed = (
            (own_segments[:, :, None] == own_segments[:, None, :]) & (earlier | is_encoder)[None]
        ).astype(f32)
        encoder_row, target_row = at(encoder_segments, section), at(target_segments, section)
        cross_allowed = (target_row[:, None] == encoder_row[None, :]).astype(f32)[None]

        own_gains = norm_gains[0]
        received = swap(jnp.concatenate([at(cotangent[0], 1 - section), own_gains], 0))
        cotangent_e, cotangent_d = by_section(at(cotangent[0], section), received[:length])
        gains_e, gains_d = (g.astype(f32) for g in by_section(own_gains, received[length:]))
        gain_self = own_gains[:1].astype(f32)

        normed_plane = spread(rms_norm(inputs, gain_self).astype(bf16))
        moved, *normed_plane = together(moved, *normed_plane)
        pack_e, pack_d = lax.optimization_barrier(
            (
                jnp.concatenate([widen_e, moved[:padded_narrow]], 0),
                jnp.concatenate([widen_d, moved[padded_narrow:]], 0),
            )
        )
        own_e = lax.all_gather(pack_e, "line", axis=0)
        own_d = lax.all_gather(pack_d, "line", axis=0)

        projected_parts = [
            nt(in_column, block).astype(bf16).reshape(lines, in_cols, tokens) for block in normed_plane
        ]
        projected = ordered(
            projected_parts[0],
            [(j ^ k, hop(projected_parts[k], k)) for k in range(1, PLANE)],
            j,
            1,
        ).reshape(3 * inner, tokens)
        out_w = gather_plane(column[:, in_cols : in_cols + cross_cols], 1).reshape(-1, width)
        row_f32, row_bf16 = ((length, width), f32), ((length, width), bf16)
        context, first_kept, first_sent = call(
            self_forward_kernel,
            (((inner, tokens), bf16), row_f32, row_f32),
            section_scalar,
            projected,
            allowed,
            inputs,
            out_w,
        )

        first_e, first_d, normed_first, normed_cross = call(
            first_norm_kernel,
            (row_f32, row_f32, row_bf16, row_bf16),
            section_scalar,
            first_kept,
            swap(first_sent),
            gains_e,
            gains_d,
        )
        stream_e = spread(normed_first)
        cross_rows, *stream_e = together(column[:, in_cols + cross_cols :], *stream_e)
        cross_pieces = spread(cross_rows)
        group = PLANE * length
        group_bf16 = ((group, width), bf16)
        steps = lines // 2
        pack_shape = (lines, padded_widen + padded_narrow, width)
        pack_specs = feed_specs(lines, padded_widen, width)
        joined_scratch = pltpu.VMEM((group, width), bf16)
        sum_scratch = pltpu.VMEM((group, width), f32)

        def unit(*middle):
            block = (1,) + middle + (padded_widen, group)
            return (
                (steps,) + block[1:],
                bf16,
                pl.BlockSpec(block, lambda step: (step,) + (0,) * (len(block) - 1)),
            )

        def with_packs(first, *packs):
            specs = {first + 3 * i + k: pack_specs[k] for i in range(len(packs)) for k in range(3)}
            return [pack for pack in packs for _ in range(3)], specs

        def feed_forward(stream, pack, *priors):
            packs, specs = with_packs(4, pack)
            return call(
                functools.partial(feed_forward_kernel, len(priors)),
                (unit(1), unit(1), unit(1), group_bf16),
                *stream,
                *packs,
                *priors,
                scratch=(joined_scratch, sum_scratch),
                steps=steps,
                specs=specs,
            )

        def feed_back(output_grad, packs, saved, ties):
            packs, specs = with_packs(4, *packs)
            specs.update({10 + i: unit(1)[2] for i in range(4)})
            return call(
                feed_back_kernel,
                (unit(2), unit(2), group_bf16),
                *output_grad,
                *packs,
                *saved,
                scratch=(joined_scratch, sum_scratch),
                steps=steps,
                specs=specs,
                time_us=8,
                ties=ties,
            )

        def feed_both(stream, output_grad, pack, *priors, ties=()):
            packs, specs = with_packs(8, pack)
            return call(
                functools.partial(feed_both_kernel, len(priors)),
                (unit(1), unit(2), group_bf16, group_bf16),
                *stream,
                *output_grad,
                *packs,
                *priors,
                scratch=(joined_scratch, joined_scratch, sum_scratch, sum_scratch),
                steps=steps,
                specs=specs,
                time_us=8,
                ties=ties,
            )

        def feed_grads(stream, output_grad, grads, hidden):
            specs = {8 + i: unit(2)[2] for i in range(2)}
            specs.update({10 + i: unit(1)[2] for i in range(2)})
            own, other = call(
                feed_grads_kernel,
                ((pack_shape, bf16), (pack_shape, bf16)),
                *stream,
                *output_grad,
                *grads,
                *hidden,
                scratch=(joined_scratch, joined_scratch),
                steps=steps,
                specs=specs,
                time_us=9,
            )
            return (own.astype(f32) + swap(other).astype(f32)).astype(bf16)

        own_e, *stream_e = together(own_e, *stream_e)
        other_e = swap(own_e)
        value_own, slope_own, hidden_own, part_own = feed_forward(stream_e, own_e)
        value_other, slope_other, hidden_other, part_e = feed_forward(stream_e, other_e, part_own)

        part_e, *cross_pieces = together(part_e, *cross_pieces)
        cross_w = in_plane(cross_pieces, 1).reshape(devices, 2, cross_cols, width).swapaxes(0, 1)
        cross_w = cross_w.reshape(-1, width)
        cross_e, cross_d = by_section(cross_w, swap(cross_w))
        cotangent_d, cross_w = together(cotangent_d, cross_w)
        output_grad_d = spread(cotangent_d)

        second_e, normed_final, cross_queries, states, cross_context, second_d, normed_last = call(
            middle_kernel,
            (
                row_f32,
                row_bf16,
                ((inner, length), bf16),
                ((2 * inner, length), bf16),
                ((inner, length), bf16),
                row_f32,
                row_bf16,
            ),
            *collected(part_e),
            first_e,
            first_d,
            normed_cross,
            gains_e,
            gains_d,
            cross_e,
            cross_d,
            cross_allowed,
        )

        stream_d = spread(normed_last)
        own_d, in_rows, *stream_d = together(own_d, column[:, :in_cols], *stream_d)
        in_pieces = [in_rows, hop(in_rows, 1), hop(in_rows, 2)]
        other_d = swap(own_d)
        hidden_own_d, grads_own_d, part_d, back_d = feed_both(stream_d, output_grad_d, own_d)
        hidden_other_d, grads_other_d, part_d, back_d = feed_both(
            stream_d, output_grad_d, other_d, part_d, back_d, ties=in_pieces[1:]
        )
        gain_shape = ((1, width), f32)
        stream_two_d, cross_branch, cross_grads, stream_two_e, sent_e, gain_two_d, gain_two_e = call(
            middle_back_kernel,
            (row_f32, row_bf16, ((3 * inner, length), bf16), row_f32, row_bf16, gain_shape, gain_shape),
            *collected(back_d),
            second_d,
            second_e,
            cotangent_d,
            cotangent_e,
            gains_d,
            gains_e,
            cross_d,
            cross_e,
            cross_queries,
            states,
            cross_allowed,
        )

        output_grad_e = spread(sent_e)
        feed_sum_d = feed_grads(
            stream_d, output_grad_d, (grads_own_d, grads_other_d), (hidden_own_d, hidden_other_d)
        )
        grads_own_e, grads_other_e, back_e = feed_back(
            output_grad_e,
            (own_e, other_e),
            (value_own, slope_own, value_other, slope_other),
            (feed_sum_d,),
        )

        stream_one_d, gain_one_d = call(
            first_back_d_kernel,
            (row_f32, gain_shape),
            cross_grads,
            cross_d,
            first_d,
            gains_d,
            stream_two_d,
        )
        feed_sum_e = feed_grads(
            stream_e, output_grad_e, (grads_own_e, grads_other_e), (hidden_own, hidden_other)
        )
        summed_d = lax.psum_scatter(feed_sum_d, "line", scatter_dimension=0)
        feed_sum_e, summed_d = together(feed_sum_e, summed_d)
        summed_e = lax.psum_scatter(feed_sum_e, "line", scatter_dimension=0)

        cross_kept, cross_sent = call(
            cross_grads_kernel,
            (((2 * inner, width), bf16), ((2 * inner, width), bf16)),
            section_scalar,
            cross_grads,
            normed_final,
            normed_cross,
            cross_context,
            cross_branch,
            ties=(back_e,),
        )

        stream_kept, stream_sent, gain_one_e = call(
            first_back_e_kernel,
            (row_f32, row_f32, gain_shape),
            *collected(back_e),
            section_scalar,
            first_e,
            gains_e,
            stream_two_e,
            stream_one_d,
        )
        in_rows, part_d, stream_kept = together(in_rows, part_d, stream_kept)
        in_pieces.append(hop(in_rows, 3))
        in_w = in_plane(in_pieces, 1).reshape(-1, width)
        stream_got, cross_sent = together(swap(stream_sent), cross_sent)
        stream_one, branch_grad, projected_grad = call(
            self_back_kernel,
            (((tokens, width), f32), ((tokens, width), bf16), ((3 * inner, tokens), bf16)),
            section_scalar,
            stream_kept,
            stream_got,
            out_w,
            projected,
            allowed,
            ties=(feed_sum_e,),
        )
        def scatter_parts(*products):
            parts = [m.astype(bf16).reshape(lines, PLANE, -1, width).swapaxes(0, 1) for m in products]
            return scatter_plane(jnp.concatenate(parts, 2)).astype(bf16)

        cross_grad = (cross_kept.astype(f32) + swap(cross_sent).astype(f32)).astype(bf16)
        cross_part = scatter_parts(cross_grad[:inner], cross_grad[inner:])
        second_out_d = second_d + sum(
            part.astype(f32) for part in collected(part_d)
        )
        out_part = scatter_parts(nn(context, branch_grad))
        parts = projected_grad.reshape(lines, PLANE, in_cols, tokens)
        grad_parts = [at(parts, j, 1)] + [hop(at(parts, j ^ k, 1), k) for k in range(1, PLANE)]
        (in_part,) = call(
            in_grad_kernel,
            (((lines * in_cols, width), bf16),),
            *[part.reshape(lines * in_cols, tokens) for part in grad_parts],
            *normed_plane,
            ties=(cross_part, out_part),
        )
        rest_sum = scatter_line(
            jnp.concatenate([in_part.reshape(lines, in_cols, width), cross_part, out_part], 1)
        )
        table_grad, gain_zero = call(
            table_kernel,
            (((vocabulary, width), bf16), gain_shape),
            projected_grad,
            in_w,
            inputs,
            gain_self,
            stream_one,
            one_hot,
            ties=(in_part,),
        )

        zero_row = jnp.zeros_like(gain_zero)
        gain_rows = jnp.concatenate(
            [
                jnp.where(is_encoder, gain_zero, zero_row),
                gain_one_e,
                gain_two_e,
                jnp.where(is_encoder, zero_row, gain_zero),
                gain_one_d,
                gain_two_d,
            ],
            0,
        ).astype(bf16)
        padded = -(-(vocabulary + 6) // 64) * 64
        padding = jnp.zeros((padded - vocabulary - 6, width), bf16)
        small = jnp.concatenate([table_grad, gain_rows, padding], 0).reshape(2, padded // 2, width)
        chip_sum = at(small, section).astype(f32) + swap(at(small, 1 - section)).astype(f32)
        plane_sum = rounded(scatter_plane(chip_sum.astype(bf16).reshape(PLANE, -1, width)))
        plane_sum, summed_e = together(plane_sum, summed_e)
        rest_sum, summed_e = together(rest_sum, summed_e)
        half_sum = gather_plane(sum_line(plane_sum)).reshape(padded // 2, width)
        small_sum = in_order(half_sum, swap(half_sum)).astype(f32)
        embedding_grad = small_sum[:vocabulary]
        gains_grad = at(small_sum[vocabulary : vocabulary + 6].reshape(2, 3, width), section)[None]

        back = permute(
            jnp.concatenate([summed_e[padded_widen:], summed_d[padded_widen:]], 0),
            AXES,
            [(b, a) for a, b in narrow_route],
        )
        halves_e = jnp.concatenate([summed_e[:padded_widen], back[:padded_narrow]], 0)
        halves_d = jnp.concatenate([summed_d[:padded_widen], back[padded_narrow:]], 0)
        half_kept, half_sent = by_section(halves_e, halves_d)
        both = in_order(half_kept[None], swap(half_sent)[None])
        both = both.reshape(2, 3, padded_narrow, width)[:, :, :narrow_half]
        widen_t = both[:, :2].reshape(2 * widen_half, width)
        narrow_grad = both[:, 2].reshape(2 * narrow_half, width).astype(f32)

        output_kept, output_sent = by_section(second_e.astype(bf16), second_out_d.astype(bf16))
        block_output = in_order(output_kept, swap(output_sent)).reshape(rows, length, width)
        cuts = [0, in_cols, in_cols + cross_cols, in_cols + 2 * cross_cols, in_cols + 3 * cross_cols]
        in_sum, first_cross_sum, second_cross_sum, out_sum = (
            rest_sum[a:b] for a, b in zip(cuts[:-1], cuts[1:])
        )
        return (
            block_output[None],
            embedding_grad,
            in_sum.T[None],
            out_sum[None],
            widen_t.astype(f32).T[None],
            narrow_grad[None],
            first_cross_sum.T[None],
            second_cross_sum.T[None],
            gains_grad,
        )

    return per_device


def solution(mesh):
    lines = mesh.shape["dp"] // PLANE
    inner_mesh = Mesh(mesh.devices.reshape(2, lines, PLANE), AXES)
    dp = ("line", "plane")
    return jax.shard_map(
        build(lines),
        mesh=inner_mesh,
        in_specs=(
            P("section", dp, None),
            P(dp, None),
            P(dp, None),
            P(),
            P("section", None, dp),
            P("section", dp, None),
            P("section", None, dp),
            P("section", dp, None),
            P("section", None, dp),
            P("section", None, dp),
            P("section", None, None),
            P("section", dp, None, None),
        ),
        out_specs=(
            P("section", dp, None, None),
            P(),
            P("section", None, dp),
            P("section", dp, None),
            P("section", None, dp),
            P("section", dp, None),
            P("section", None, dp),
            P("section", None, dp),
            P("section", None, None),
        ),
        check_vma=False,
    )
```

```python
import functools

import jax
import jax.numpy as jnp
from jax import lax
from jax.experimental import pallas as pl
from jax.experimental.pallas import tpu as pltpu
from jax.sharding import Mesh, PartitionSpec as P

HEADS = 6
HEAD_DIM = 64
PLANE = 4
SCALE = HEAD_DIM ** (-0.5)

epsilon = 1e-06
masked_value = -1000000000.0
AXES = ("section", "line", "plane")
bf16 = jnp.bfloat16
f32 = jnp.float32


def nn(a, b):
    return lax.dot_general(a, b, (((1,), (0,)), ((), ())), preferred_element_type=f32)


def nt(a, b):
    return lax.dot_general(a, b, (((1,), (1,)), ((), ())), preferred_element_type=f32)


def tn(a, b):
    return lax.dot_general(a, b, (((0,), (0,)), ((), ())), preferred_element_type=f32)


def permute(block, axes, route):
    shape = block.shape
    if block.ndim == 2 and shape[0] % 8 == 0:
        block = block.reshape(shape[0] // 8, 8, shape[1])
    return lax.ppermute(block, axes, route).reshape(shape)


def rounded(value):
    return lax.reduce_precision(value, 8, 7).astype(bf16)


def rms_norm(inputs, gain_row):
    return inputs * lax.rsqrt(jnp.mean(inputs * inputs, -1, keepdims=True) + epsilon) * gain_row


def rms_back(inputs, gain_row, upstream):
    scale = lax.rsqrt(jnp.mean(inputs * inputs, -1, keepdims=True) + epsilon)
    normed = inputs * scale
    weighted = upstream * gain_row
    grad = (weighted - normed * jnp.mean(weighted * normed, -1, keepdims=True)) * scale
    return grad, jnp.sum(upstream * normed, 0, keepdims=True)


def gelu_parts(gate):
    slope = (2.0 / jnp.pi) ** 0.5
    square = gate * gate
    half = 0.5 + 0.5 * jnp.tanh(gate * (slope + (slope * 0.044715) * square))
    bend = gate * (slope + (slope * 0.134145) * square)
    return gate * half, half + (2.0 * half) * ((1.0 - half) * bend)


def whole(shape):
    return pl.BlockSpec(shape, lambda step: (0,) * len(shape))


def call(kernel, outputs, *args, scratch=(), specs=None, time_us=0.3, ties=(), vmem=56):
    specs = specs or {}
    in_specs = [
        specs.get(i)
        or (pl.BlockSpec(memory_space=pltpu.SMEM) if a.dtype == jnp.int32 else whole(a.shape))
        for i, a in enumerate(args)
    ]
    in_specs += [pl.BlockSpec(memory_space=pl.ANY)] * len(ties)
    first, after = len(args), len(args) + len(ties)
    out_shape = tuple(jax.ShapeDtypeStruct(output[0], output[1]) for output in outputs)
    return pl.pallas_call(
        lambda *refs: kernel(*refs[:first], *refs[after:]),
        grid=(1,),
        out_shape=out_shape,
        in_specs=in_specs,
        out_specs=tuple(output[2] if len(output) > 2 else whole(output[0]) for output in outputs),
        scratch_shapes=list(scratch),
        compiler_params=pltpu.CompilerParams(vmem_limit_bytes=vmem * 1024 * 1024),
        cost_estimate=pl.CostEstimate(
            flops=int(time_us * 8e8), bytes_accessed=int(time_us * 2.5e6), transcendentals=0
        ),
    )(*args, *ties)


def chances_of(queries, keys, allowed):
    scores = jnp.where(allowed > 0, tn(queries, keys) * SCALE, masked_value)
    exponent = jnp.exp(scores - jnp.max(scores, -1, keepdims=True))
    return exponent / jnp.sum(exponent, -1, keepdims=True)


def attend_into(context_ref, query_ref, key_ref, value_ref, allowed_ref, starts=(0, 0, 0)):
    rows, length, _ = allowed_ref.shape
    for row in range(rows):
        columns = slice(row * length, (row + 1) * length)
        for head in range(HEADS):
            q, k, v = (
                ref[start + head * HEAD_DIM : start + (head + 1) * HEAD_DIM, columns]
                for ref, start in zip((query_ref, key_ref, value_ref), starts)
            )
            weights = chances_of(q, k, allowed_ref[row]).astype(bf16)
            context_ref[head * HEAD_DIM : (head + 1) * HEAD_DIM, columns] = nt(v, weights).astype(bf16)


def attend_back_into(grads_ref, query_ref, key_ref, value_ref, allowed_ref, upstream, starts=(0, 0, 0)):
    rows, length, _ = allowed_ref.shape
    inner = HEADS * HEAD_DIM
    for row in range(rows):
        columns = slice(row * length, (row + 1) * length)
        for head in range(HEADS):
            first = head * HEAD_DIM
            q, k, v = (
                ref[start + first : start + first + HEAD_DIM, columns]
                for ref, start in zip((query_ref, key_ref, value_ref), starts)
            )
            g = upstream[first : first + HEAD_DIM, columns]
            chances = chances_of(q, k, allowed_ref[row])
            weight_grad = tn(g, v)
            score_grad = (
                chances * (weight_grad - jnp.sum(weight_grad * chances, -1, keepdims=True))
            ).astype(bf16)
            grads = (nt(k, score_grad) * SCALE, nn(q, score_grad) * SCALE, nn(g, chances.astype(bf16)))
            for number, grad in enumerate(grads):
                at = number * inner + first
                grads_ref[at : at + HEAD_DIM, columns] = grad.astype(bf16)


def added(refs):
    total = refs[0][...].astype(f32)
    for ref in refs[1:]:
        total = total + ref[...].astype(f32)
    return total


def split_rows(section, value, kept_ref, sent_ref):
    length = kept_ref.shape[0]
    mine, other = value[:length], value[length:]
    kept_ref[...] = jnp.where(section == 0, mine, other)
    sent_ref[...] = jnp.where(section == 0, other, mine)


def self_forward_kernel(section_ref, projected_ref, allowed_ref, inputs_ref, out_w_ref, context_ref, kept_ref, sent_ref):
    inner = context_ref.shape[0]
    attend_into(context_ref, projected_ref, projected_ref, projected_ref, allowed_ref, (0, inner, 2 * inner))
    first_sum = inputs_ref[...] + tn(context_ref[...], out_w_ref[...])
    split_rows(section_ref[0], first_sum, kept_ref, sent_ref)


def first_norm_kernel(section_ref, kept_ref, got_ref, gains_e_ref, gains_d_ref, first_e_ref, first_d_ref, normed_e_ref, normed_d_ref):
    is_encoder = section_ref[0] == 0
    first_e = jnp.where(is_encoder, kept_ref[...], got_ref[...])
    first_d = jnp.where(is_encoder, got_ref[...], kept_ref[...])
    first_e_ref[...] = first_e
    first_d_ref[...] = first_d
    normed_e_ref[...] = rms_norm(first_e, gains_e_ref[1:2]).astype(bf16)
    normed_d_ref[...] = rms_norm(first_d, gains_d_ref[1:2]).astype(bf16)


def joined(refs, out_ref):
    length = refs[0].shape[0]
    for k, ref in enumerate(refs):
        out_ref[k * length : (k + 1) * length] = ref[...]
    return out_ref[...]


def apart(value, refs):
    length = refs[0].shape[0]
    for k, ref in enumerate(refs):
        ref[...] = value[k * length : (k + 1) * length].astype(bf16)


def pack_specs(lines, padded, width):
    return [
        pl.BlockSpec((lines, padded, width), lambda step: (0, 0, 0)),
        pl.BlockSpec((lines, padded // 2, width), lambda step: (0, 2, 0)),
    ]


def rows_of(ref):
    return ref[...].reshape(ref.shape[0] * ref.shape[1], ref.shape[2])


def feed_forward(x, wide, narrow, value_ref, slope_ref, hidden_ref):
    both = nt(wide, x)
    units = both.shape[0] // 2
    value, slope = gelu_parts(both[:units])
    value_ref[...] = value.astype(bf16)
    slope_ref[...] = (slope * both[units:]).astype(bf16)
    hidden_ref[...] = (value * both[units:]).astype(bf16)
    return tn(hidden_ref[...], narrow)


def feed_forward_own_kernel(*refs):
    streams, wide_ref, narrow_ref, value_ref, slope_ref, hidden_ref, part_ref, x_ref = refs[:4], *refs[4:]
    x = joined(streams, x_ref)
    part = feed_forward(x, rows_of(wide_ref), rows_of(narrow_ref), value_ref, slope_ref, hidden_ref)
    part_ref[...] = part.astype(bf16)


def feed_forward_other_kernel(x_ref, prior_ref, wide_ref, narrow_ref, value_ref, slope_ref, hidden_ref, *part_refs):
    part = feed_forward(
        x_ref[...], rows_of(wide_ref), rows_of(narrow_ref), value_ref, slope_ref, hidden_ref
    )
    apart(part + prior_ref[...].astype(f32), part_refs)


def feed_back_kernel(*refs):
    outputs, packs, saved = refs[:4], (refs[4:6], refs[6:8]), refs[8:12]
    grads_refs, output_ref, back_refs = refs[12:14], refs[14], refs[15:]
    output_grad = joined(outputs, output_ref)
    back = None
    for core, (wide_ref, narrow_ref) in enumerate(packs):
        hidden_grad = nt(rows_of(narrow_ref), output_grad)
        units = hidden_grad.shape[0]
        value_ref, slope_ref = saved[2 * core : 2 * core + 2]
        grads_refs[core][:units] = (hidden_grad * slope_ref[...].astype(f32)).astype(bf16)
        grads_refs[core][units:] = (hidden_grad * value_ref[...].astype(f32)).astype(bf16)
        term = tn(grads_refs[core][...], rows_of(wide_ref))
        back = term if back is None else back + term
    apart(back, back_refs)


def feed_both(x, output_grad, wide, narrow, grads_ref):
    both = nt(wide, x)
    hidden_grad = nt(narrow, output_grad)
    units = hidden_grad.shape[0]
    value, slope = gelu_parts(both[:units])
    grads_ref[:units] = (hidden_grad * (slope * both[units:])).astype(bf16)
    grads_ref[units : 2 * units] = (hidden_grad * value).astype(bf16)
    grads_ref[2 * units :] = (value * both[units:]).astype(bf16)
    return tn(grads_ref[2 * units :], narrow), tn(grads_ref[: 2 * units], wide)


def feed_both_own_kernel(*refs):
    streams, outputs, wide_ref, narrow_ref, grads_ref, part_ref, back_ref, x_ref, output_ref = (
        refs[:4],
        refs[4:8],
        *refs[8:],
    )
    x, output_grad = joined(streams, x_ref), joined(outputs, output_ref)
    part, back = feed_both(x, output_grad, rows_of(wide_ref), rows_of(narrow_ref), grads_ref)
    part_ref[...] = part.astype(bf16)
    back_ref[...] = back.astype(bf16)


def feed_both_other_kernel(x_ref, output_ref, part_prior, back_prior, wide_ref, narrow_ref, grads_ref, *refs):
    part, back = feed_both(x_ref[...], output_ref[...], rows_of(wide_ref), rows_of(narrow_ref), grads_ref)
    apart(back + back_prior[...].astype(f32), refs[:4])
    apart(part + part_prior[...].astype(f32), refs[4:])


def feed_grads_kernel(*refs):
    cores, pack_ref = (refs[: len(refs) // 2], refs[len(refs) // 2 : -1]), refs[-1]
    lines = pack_ref.shape[0]
    wide = narrow = 0.0
    for x_ref, output_ref, *factors in cores:
        if len(factors) == 1:
            units = factors[0].shape[0] // 3
            grads, hidden = factors[0][: 2 * units], factors[0][2 * units :]
        else:
            grads, hidden = factors[0][...], factors[1][...]
        wide = wide + nn(grads, x_ref[...])
        narrow = narrow + nn(hidden, output_ref[...])
    padded = wide.shape[0] // lines
    pack_ref[:, :padded] = wide.astype(bf16).reshape(lines, padded, wide.shape[1])
    pack_ref[:, padded:] = narrow.astype(bf16).reshape(lines, padded // 2, wide.shape[1])


def middle_kernel(*refs):
    parts = refs[:4]
    first_e_ref, first_d_ref, normed_d_ref, gains_e_ref, gains_d_ref, cross_e_ref, cross_d_ref, allowed_ref = refs[4:12]
    second_e_ref, normed_e_ref, queries_ref, states_ref, context_ref, second_d_ref, normed_last_ref = refs[12:]
    inner = context_ref.shape[0]
    queries_ref[...] = nt(cross_d_ref[:inner], normed_d_ref[...]).astype(bf16)
    second_e = first_e_ref[...] + added(parts)
    second_e_ref[...] = second_e
    normed = rms_norm(second_e, gains_e_ref[2:3]).astype(bf16)
    normed_e_ref[...] = normed
    states_ref[...] = nt(cross_e_ref[...], normed).astype(bf16)
    attend_into(context_ref, queries_ref, states_ref, states_ref, allowed_ref, (0, 0, inner))
    second_d = first_d_ref[...] + tn(context_ref[...], cross_d_ref[inner:])
    second_d_ref[...] = second_d
    normed_last_ref[...] = rms_norm(second_d, gains_d_ref[2:3]).astype(bf16)


def middle_back_kernel(*refs):
    parts = refs[:4]
    second_d_ref, second_e_ref, cotangent_d_ref, cotangent_e_ref, gains_d_ref, gains_e_ref = refs[4:10]
    cross_d_ref, cross_e_ref, queries_ref, states_ref, allowed_ref = refs[10:15]
    stream_d_ref, branch_ref, grads_ref, stream_e_ref, sent_ref, gain_d_ref, gain_e_ref = refs[15:]
    inner = queries_ref.shape[0]
    input_grad, gain_d_ref[...] = rms_back(second_d_ref[...], gains_d_ref[2:3], added(parts))
    stream_d = cotangent_d_ref[...].astype(f32) + input_grad
    stream_d_ref[...] = stream_d
    branch = stream_d.astype(bf16)
    branch_ref[...] = branch
    context_grad = nt(cross_d_ref[inner:], branch).astype(bf16)
    attend_back_into(grads_ref, queries_ref, states_ref, states_ref, allowed_ref, context_grad, (0, 0, inner))
    final_grad = tn(grads_ref[inner:], cross_e_ref[...])
    input_grad, gain_e_ref[...] = rms_back(second_e_ref[...], gains_e_ref[2:3], final_grad)
    stream_e = cotangent_e_ref[...].astype(f32) + input_grad
    stream_e_ref[...] = stream_e
    sent_ref[...] = stream_e.astype(bf16)


def first_back_d_kernel(grads_ref, cross_d_ref, first_d_ref, gains_d_ref, stream_ref, out_ref, gain_ref):
    inner = cross_d_ref.shape[0] // 2
    upstream = tn(grads_ref[:inner], cross_d_ref[:inner])
    input_grad, gain_ref[...] = rms_back(first_d_ref[...], gains_d_ref[1:2], upstream)
    out_ref[...] = stream_ref[...] + input_grad


def first_back_e_kernel(*refs):
    parts = refs[:4]
    section_ref, first_e_ref, gains_e_ref, stream_ref, stream_d_ref, kept_ref, sent_ref, gain_ref = refs[4:]
    input_grad, gain_ref[...] = rms_back(first_e_ref[...], gains_e_ref[1:2], added(parts))
    stream_e = stream_ref[...] + input_grad
    is_encoder = section_ref[0] == 0
    kept_ref[...] = jnp.where(is_encoder, stream_e, stream_d_ref[...])
    sent_ref[...] = jnp.where(is_encoder, stream_d_ref[...], stream_e)


def self_back_kernel(section_ref, kept_ref, got_ref, out_w_ref, projected_ref, allowed_ref, stream_ref, branch_ref, grads_ref):
    is_encoder = section_ref[0] == 0
    inner, length = out_w_ref.shape[0], kept_ref.shape[0]
    stream_ref[:length] = jnp.where(is_encoder, kept_ref[...], got_ref[...])
    stream_ref[length:] = jnp.where(is_encoder, got_ref[...], kept_ref[...])
    branch = stream_ref[...].astype(bf16)
    branch_ref[...] = branch
    context_grad = nt(out_w_ref[...], branch).astype(bf16)
    attend_back_into(
        grads_ref, projected_ref, projected_ref, projected_ref, allowed_ref, context_grad, (0, inner, 2 * inner)
    )


def table_kernel(*refs):
    grads, codes, gain_refs, (section_ref, in_ref, embedding_ref, gain_ref, stream_ref, out_ref) = (
        refs[:4],
        refs[4:8],
        refs[8:12],
        refs[12:],
    )
    table = gain_grad = 0.0
    for k, (grad, code_ref) in enumerate(zip(grads, codes)):
        shape = (embedding_ref.shape[0], code_ref.shape[1])
        one_hot = (lax.broadcasted_iota(jnp.int32, shape, 0) == code_ref[...]).astype(bf16)
        inputs = tn(one_hot, embedding_ref[...])
        input_grad, gain_part = rms_back(inputs, gain_ref[...], tn(grad[...], in_ref[...]))
        if k == 0:
            input_grad = input_grad + stream_ref[...]
        gain_grad = gain_grad + gain_part
        table = table + nn(one_hot, input_grad.astype(bf16))
    vocabulary = embedding_ref.shape[0]
    out_ref[:vocabulary] = table.astype(bf16)
    nothing, is_encoder = jnp.zeros_like(gain_grad), section_ref[0] == 0
    rows = [jnp.where(is_encoder, gain_grad, nothing), gain_refs[0][...], gain_refs[1][...]]
    rows += [jnp.where(is_encoder, nothing, gain_grad), gain_refs[2][...], gain_refs[3][...]]
    rows.append(jnp.zeros((out_ref.shape[0] - vocabulary - 6, out_ref.shape[1]), f32))
    out_ref[vocabulary:] = jnp.concatenate(rows, 0).astype(bf16)


def assemble_kernel(section_ref, plane_ref, *refs):
    pieces, (table_ref, gains_ref, rows_ref) = refs[:PLANE], refs[PLANE:]
    count = pieces[0].shape[0]
    for k, piece in enumerate(pieces):
        rows_ref[pl.ds(pl.multiple_of((plane_ref[0] ^ k) * count, 8), count)] = piece[...].astype(f32)
    vocabulary = table_ref.shape[0]
    table_ref[...] = rows_ref[:vocabulary]
    gains = rows_ref[vocabulary : vocabulary + 8]
    gains_ref[0] = jnp.where(section_ref[0] == 0, gains[:3], gains[3:6])


def in_grad_kernel(*refs):
    grads, streams, out_ref = refs[:4], refs[4:8], refs[8]
    total = nn(grads[0][...], streams[0][...])
    for grad, stream in zip(grads[1:], streams[1:]):
        total = total + nn(grad[...], stream[...])
    out_ref[...] = total.astype(bf16)


def cross_grads_kernel(section_ref, grads_ref, normed_e_ref, normed_d_ref, context_ref, branch_ref, kept_ref, sent_ref):
    inner = context_ref.shape[0]
    is_encoder = section_ref[0] == 0
    grad_e = nn(grads_ref[inner:], normed_e_ref[...])
    grad_first = nn(grads_ref[:inner], normed_d_ref[...])
    grad_second = nn(context_ref[...], branch_ref[...])
    for start, grad_d in ((0, grad_first), (inner, grad_second)):
        part_e = grad_e[start : start + inner]
        kept_ref[start : start + inner] = jnp.where(is_encoder, part_e, grad_d).astype(bf16)
        sent_ref[start : start + inner] = jnp.where(is_encoder, grad_d, part_e).astype(bf16)


def build(lines):
    devices = lines * PLANE

    def place(section, line, plane):
        return section * devices + line * PLANE + plane

    def hop(block, offset):
        route = [
            (place(s, z, j), place(s, z, j ^ offset))
            for s in range(2)
            for z in range(lines)
            for j in range(PLANE)
        ]
        return permute(block, AXES, route)

    def swap(block):
        return permute(block, "section", [(0, 1), (1, 0)])

    narrow_route = []
    for core in range(2):
        for block in range(devices):
            target = (block % 2, 2 * (block // 8) + core, (block % 8) // 2)
            narrow_route.append((core * devices + block, place(*target)))

    def at(array, index, axis=0):
        return lax.dynamic_index_in_dim(array, index, axis, False)

    def ordered(own, others, index, axis=0):
        count = len(others) + 1
        shape = own.shape[:axis] + (count,) + own.shape[axis:]
        out = jnp.zeros(shape, own.dtype)
        for where_to, piece in [(index, own)] + others:
            out = lax.dynamic_update_index_in_dim(out, piece, where_to, axis)
        return out

    def sum_line(block):
        if lines & (lines - 1):
            return rounded(lax.psum(block.astype(f32), "line"))
        distance = 1
        while distance < lines:
            route = [(z, z ^ distance) for z in range(lines)]
            block = rounded(block.astype(f32) + permute(block, "line", route).astype(f32))
            distance *= 2
        return block

    def in_plane(blocks, axis=0):
        j = lax.axis_index("plane")
        return ordered(blocks[0], [(j ^ k, blocks[k]) for k in range(1, PLANE)], j, axis)

    def gather_plane(block, axis=0):
        return in_plane(spread(block), axis)

    def scattered(parts):
        j = lax.axis_index("plane")
        return [at(parts, j)] + [hop(at(parts, j ^ k), k) for k in range(1, PLANE)]

    def total_of(terms):
        return sum((term.astype(f32) for term in terms[1:]), terms[0].astype(f32))

    def spread(block):
        return [block] + [hop(block, k) for k in range(1, PLANE)]

    def collected(parts):
        return [parts[0]] + [hop(parts[k], k) for k in range(1, PLANE)]

    def per_device(
        byte_codes,
        encoder_segments,
        target_segments,
        embedding,
        attention_in,
        attention_out,
        widen_weight,
        narrow_weight,
        cross_first,
        cross_second,
        norm_gains,
        cotangent,
    ):
        section = lax.axis_index("section")
        j = lax.axis_index("plane")
        is_encoder = section == 0
        section_scalar = section.astype(jnp.int32).reshape(1)
        inner = cross_first.shape[2] * devices
        vocabulary, width = embedding.shape
        rows, length = encoder_segments.shape
        tokens = rows * length

        def together(*values):
            return list(lax.optimization_barrier(values))

        def by_section(mine, other):
            return jnp.where(is_encoder, mine, other), jnp.where(is_encoder, other, mine)

        def in_order(mine, other):
            return jnp.concatenate(by_section(mine, other), 0)

        in_cols = attention_in.shape[2]
        cross_cols = cross_first.shape[2]
        column, codes = together(
            jnp.concatenate([attention_in[0].T, attention_out[0], cross_first[0].T, cross_second[0].T], 0),
            byte_codes[0],
        )
        column = lax.all_gather(column, "line", axis=0)
        in_column = column[:, :in_cols].reshape(-1, width)

        widen_half = widen_weight.shape[2] // 2
        narrow_half = narrow_weight.shape[1] // 2
        padded_narrow = -(-narrow_half // 16) * 16
        padded_widen = 2 * padded_narrow

        def widened(block):
            return jnp.pad(block, ((0, 0),) * (block.ndim - 2) + ((0, padded_narrow - narrow_half), (0, 0)))

        narrow_parts = widened(narrow_weight[0].reshape(2, narrow_half, width))
        narrow_e, narrow_d = by_section(at(narrow_parts, section), swap(at(narrow_parts, 1 - section)))
        moved = permute(jnp.concatenate([narrow_e, narrow_d], 0), AXES, narrow_route)
        widen_parts = widened(widen_weight[0].T.reshape(2, 2, narrow_half, width)).reshape(
            2, padded_widen, width
        )
        widen_e, widen_d = by_section(at(widen_parts, section), swap(at(widen_parts, 1 - section)))

        columns = lax.broadcasted_iota(jnp.int32, (tokens, vocabulary), 1)
        inputs = nn((codes.reshape(tokens, 1) == columns).astype(bf16), embedding)
        codes_plane = spread(codes.reshape(1, tokens))
        own_segments = jnp.where(is_encoder, encoder_segments, target_segments)
        earlier = lax.broadcasted_iota(jnp.int32, (length, length), 1) <= lax.broadcasted_iota(
            jnp.int32, (length, length), 0
        )
        allowed = (
            (own_segments[:, :, None] == own_segments[:, None, :]) & (earlier | is_encoder)[None]
        ).astype(f32)
        encoder_row, target_row = at(encoder_segments, section), at(target_segments, section)
        cross_allowed = (target_row[:, None] == encoder_row[None, :]).astype(f32)[None]

        own_gains = norm_gains[0]
        received = swap(jnp.concatenate([at(cotangent[0], 1 - section), own_gains], 0))
        cotangent_e, cotangent_d = by_section(at(cotangent[0], section), received[:length])
        gains_e, gains_d = (g.astype(f32) for g in by_section(own_gains, received[length:]))
        gain_self = own_gains[:1].astype(f32)

        normed_plane = spread(rms_norm(inputs, gain_self).astype(bf16))
        moved, *planes = together(moved, *normed_plane, *codes_plane)
        normed_plane, codes_plane = planes[:PLANE], planes[PLANE:]
        pack_e, pack_d = lax.optimization_barrier(
            (
                jnp.concatenate([widen_e, moved[:padded_narrow]], 0),
                jnp.concatenate([widen_d, moved[padded_narrow:]], 0),
            )
        )
        own_e = lax.all_gather(pack_e, "line", axis=0)
        own_d = lax.all_gather(pack_d, "line", axis=0)

        projected_parts = [
            nt(in_column, block).astype(bf16).reshape(lines, in_cols, tokens) for block in normed_plane
        ]
        hopped = together(*[hop(projected_parts[k], k) for k in range(1, PLANE)], column)
        column = hopped[-1]
        projected = in_plane([projected_parts[0], *hopped[:-1]], 1).reshape(3 * inner, tokens)
        out_pieces = together(*spread(column[:, in_cols : in_cols + cross_cols]), column)
        column = out_pieces[-1]
        out_w = in_plane(out_pieces[:-1], 1).reshape(inner, width)
        cross_pieces = spread(column[:, in_cols + cross_cols :])
        row_f32, row_bf16 = ((length, width), f32), ((length, width), bf16)
        context, first_kept, first_sent = call(
            self_forward_kernel,
            (((inner, tokens), bf16), row_f32, row_f32),
            section_scalar,
            projected,
            allowed,
            inputs,
            out_w,
        )

        first_e, first_d, normed_first, normed_cross = call(
            first_norm_kernel,
            (row_f32, row_f32, row_bf16, row_bf16),
            section_scalar,
            first_kept,
            swap(first_sent),
            gains_e,
            gains_d,
        )
        normed_first, *cross_pieces = together(normed_first, *cross_pieces)
        stream_e = spread(normed_first)
        group = PLANE * length
        group_bf16 = ((group, width), bf16)
        pack_shape = (lines, padded_widen + padded_narrow, width)
        halves_of = pack_specs(lines, padded_widen, width)
        units = lines * padded_narrow
        unit_bf16, pair_bf16, trio_bf16 = (((n * units, group), bf16) for n in (1, 2, 3))
        blocks_bf16 = (row_bf16,) * PLANE

        def with_packs(first, *packs):
            specs = {first + 2 * i + k: halves_of[k] for i in range(len(packs)) for k in range(2)}
            return dict(specs=specs), [pack for pack in packs for _ in range(2)]

        def feed_grads(own, other, *ties):
            (pack,) = call(feed_grads_kernel, ((pack_shape, bf16),), *own, *other, time_us=0.3, ties=ties)
            return pack

        own_e, *stream_e = together(own_e, *stream_e)
        other_e = swap(own_e)
        cotangent_d, *stream_e = together(cotangent_d, *stream_e)
        options, packs = with_packs(4, own_e)
        value_own, slope_own, hidden_own, part_own, x_e = call(
            feed_forward_own_kernel,
            (unit_bf16, unit_bf16, unit_bf16, group_bf16, group_bf16),
            *stream_e,
            *packs,
            **options,
        )
        output_grad_d = spread(cotangent_d)
        x_e, *cross_pieces = together(x_e, *cross_pieces)
        cross_w = in_plane(cross_pieces, 1).reshape(devices, 2, cross_cols, width).swapaxes(0, 1)
        cross_w = cross_w.reshape(2 * inner, width)
        cross_e, cross_d = by_section(cross_w, swap(cross_w))
        options, packs = with_packs(2, other_e)
        value_other, slope_other, hidden_other, *part_e = call(
            feed_forward_other_kernel,
            (unit_bf16, unit_bf16, unit_bf16, *blocks_bf16),
            x_e,
            part_own,
            *packs,
            **options,
        )
        *part_e, output_grad_d[1], output_grad_d[2], output_grad_d[3] = together(
            *part_e, *output_grad_d[1:]
        )

        second_e, normed_final, cross_queries, states, cross_context, second_d, normed_last = call(
            middle_kernel,
            (
                row_f32,
                row_bf16,
                ((inner, length), bf16),
                ((2 * inner, length), bf16),
                ((inner, length), bf16),
                row_f32,
                row_bf16,
            ),
            *collected(part_e),
            first_e,
            first_d,
            normed_cross,
            gains_e,
            gains_d,
            cross_e,
            cross_d,
            cross_allowed,
        )

        stream_d = spread(normed_last)
        own_d, *stream_d = together(own_d, *stream_d)
        other_d = swap(own_d)
        options, packs = with_packs(8, own_d)
        factors_d, part_own, back_own, x_d, joined_grad_d = call(
            feed_both_own_kernel,
            (trio_bf16, group_bf16, group_bf16, group_bf16, group_bf16),
            *stream_d,
            *output_grad_d,
            *packs,
            **options,
        )
        options, packs = with_packs(4, other_d)
        factors_other_d, *blocks = call(
            feed_both_other_kernel,
            (trio_bf16, *blocks_bf16, *blocks_bf16),
            x_d,
            joined_grad_d,
            part_own,
            back_own,
            *packs,
            **options,
        )
        feed_sum_d = feed_grads(
            (x_d, joined_grad_d, factors_d),
            (swap(x_d), swap(joined_grad_d), swap(factors_other_d)),
        )
        feed_sum_d, *blocks = together(feed_sum_d, *blocks)
        back_d, part_d = collected(blocks[:PLANE]), blocks[PLANE:]
        gain_shape = ((1, width), f32)
        stream_two_d, cross_branch, cross_grads, stream_two_e, sent_e, gain_two_d, gain_two_e = call(
            middle_back_kernel,
            (row_f32, row_bf16, ((3 * inner, length), bf16), row_f32, row_bf16, gain_shape, gain_shape),
            *back_d,
            second_d,
            second_e,
            cotangent_d,
            cotangent_e,
            gains_d,
            gains_e,
            cross_d,
            cross_e,
            cross_queries,
            states,
            cross_allowed,
        )

        stream_one_d, gain_one_d = call(
            first_back_d_kernel,
            (row_f32, gain_shape),
            cross_grads,
            cross_d,
            first_d,
            gains_d,
            stream_two_d,
        )
        output_grad_e = together(*spread(sent_e))
        cross_kept, cross_sent = call(
            cross_grads_kernel,
            (((2 * inner, width), bf16), ((2 * inner, width), bf16)),
            section_scalar,
            cross_grads,
            normed_final,
            normed_cross,
            cross_context,
            cross_branch,
        )
        cross_grad = (cross_kept.astype(f32) + swap(cross_sent).astype(f32)).astype(bf16)
        options, packs = with_packs(4, own_e, other_e)
        grads_own, grads_other, joined_grad_e, *back_e = call(
            feed_back_kernel,
            (pair_bf16, pair_bf16, group_bf16, *blocks_bf16),
            *output_grad_e,
            *packs,
            value_own,
            slope_own,
            value_other,
            slope_other,
            ties=(stream_one_d, cross_kept),
            time_us=0.3,
            **options,
        )
        def by_plane(*products):
            parts = [m.astype(bf16).reshape(lines, PLANE, -1, width).swapaxes(0, 1) for m in products]
            return jnp.concatenate(parts, 2)

        cross_terms = scattered(by_plane(cross_grad[:inner], cross_grad[inner:]))
        feed_sum_e = feed_grads(
            (x_e, joined_grad_e, grads_own, hidden_own),
            (swap(x_e), swap(joined_grad_e), swap(grads_other), swap(hidden_other)),
        )
        feed_sum_e, *blocks = together(feed_sum_e, *back_e, *cross_terms)
        back_e, cross_terms = blocks[:PLANE], blocks[PLANE:]
        back_e = collected(back_e)

        summed_d = lax.psum_scatter(feed_sum_d, "line", scatter_dimension=0)
        feed_sum_e, summed_d = together(feed_sum_e, summed_d)
        summed_e = lax.psum_scatter(feed_sum_e, "line", scatter_dimension=0)

        stream_kept, stream_sent, gain_one_e = call(
            first_back_e_kernel,
            (row_f32, row_f32, gain_shape),
            *back_e,
            section_scalar,
            first_e,
            gains_e,
            stream_two_e,
            stream_one_d,
            ties=(feed_sum_e,),
        )
        stream_got = swap(stream_sent)
        stream_one, branch_grad, projected_grad = call(
            self_back_kernel,
            (((tokens, width), f32), ((tokens, width), bf16), ((3 * inner, tokens), bf16)),
            section_scalar,
            stream_kept,
            stream_got,
            out_w,
            projected,
            allowed,
        )
        parts = projected_grad.reshape(lines, PLANE, in_cols, tokens)
        grad_parts = [at(parts, j, 1)] + [hop(at(parts, j ^ k, 1), k) for k in range(1, PLANE)]
        branch_grad, *grad_parts = together(
            branch_grad, *[part.reshape(lines * in_cols, tokens) for part in grad_parts]
        )
        out_part = total_of(scattered(by_plane(nn(context, branch_grad)))).astype(bf16)
        cross_part = total_of(cross_terms).astype(bf16)
        (in_part,) = call(
            in_grad_kernel,
            (((lines * in_cols, width), bf16),),
            *grad_parts,
            *normed_plane,
        )
        padded = -(-(vocabulary + 6) // 64) * 64
        (small,) = call(
            table_kernel,
            (((padded, width), bf16),),
            *grad_parts,
            *codes_plane,
            gain_one_e,
            gain_two_e,
            gain_one_d,
            gain_two_d,
            section_scalar,
            in_column,
            embedding,
            gain_self,
            stream_one,
            specs={4 + k: whole((1, tokens)) for k in range(PLANE)},
        )
        plane_sum = rounded(total_of(scattered(small.reshape(PLANE, -1, width))))
        plane_sum, summed_e = together(plane_sum, summed_e)
        chip_sum = rounded(plane_sum.astype(f32) + swap(plane_sum).astype(f32))
        rest_pack = jnp.concatenate([in_part.reshape(lines, in_cols, width), cross_part, out_part], 1)
        rest_pack, line_sum = together(rest_pack, sum_line(chip_sum))
        rest_sum = lax.psum_scatter(rest_pack, "line", scatter_dimension=0).astype(f32)
        pieces = together(*spread(line_sum), *part_d)
        pieces[PLANE:] = collected(pieces[PLANE:])
        second_out_d = second_d + sum(part.astype(f32) for part in pieces[PLANE:])
        embedding_grad, gains_grad = call(
            assemble_kernel,
            (((vocabulary, width), f32), ((1, 3, width), f32)),
            section_scalar,
            j.astype(jnp.int32).reshape(1),
            *pieces[:PLANE],
            scratch=(pltpu.VMEM((padded, width), f32),),
        )

        def returned(summed, receiver):
            narrow = permute(summed[padded_widen:], AXES, [(b, a) for a, b in narrow_route])
            half = jnp.concatenate([summed[:padded_widen], narrow], 0)
            return half, permute(half, "section", [(1 - receiver, receiver)])

        half_d, got_d = returned(summed_d, 1)
        half_e, got_e = returned(summed_e, 0)
        both = jnp.where(is_encoder, jnp.stack([half_e, got_e]), jnp.stack([got_d, half_d]))
        both = both.reshape(2, 3, padded_narrow, width)[:, :, :narrow_half]
        widen_t = both[:, :2].reshape(2 * widen_half, width)
        narrow_grad = both[:, 2].reshape(2 * narrow_half, width).astype(f32)

        output_kept, output_sent = by_section(second_e.astype(bf16), second_out_d.astype(bf16))
        block_output = in_order(output_kept, swap(output_sent)).reshape(rows, length, width)
        cuts = [0, in_cols, in_cols + cross_cols, in_cols + 2 * cross_cols, in_cols + 3 * cross_cols]
        in_sum, first_cross_sum, second_cross_sum, out_sum = (
            rest_sum[a:b] for a, b in zip(cuts[:-1], cuts[1:])
        )
        return (
            block_output[None],
            embedding_grad,
            in_sum.T[None],
            out_sum[None],
            widen_t.astype(f32).T[None],
            narrow_grad[None],
            first_cross_sum.T[None],
            second_cross_sum.T[None],
            gains_grad,
        )

    return per_device


def solution(mesh):
    lines = mesh.shape["dp"] // PLANE
    inner_mesh = Mesh(mesh.devices.reshape(2, lines, PLANE), AXES)
    dp = ("line", "plane")
    return jax.shard_map(
        build(lines),
        mesh=inner_mesh,
        in_specs=(
            P("section", dp, None),
            P(dp, None),
            P(dp, None),
            P(),
            P("section", None, dp),
            P("section", dp, None),
            P("section", None, dp),
            P("section", dp, None),
            P("section", None, dp),
            P("section", None, dp),
            P("section", None, None),
            P("section", dp, None, None),
        ),
        out_specs=(
            P("section", dp, None, None),
            P(),
            P("section", None, dp),
            P("section", dp, None),
            P("section", None, dp),
            P("section", dp, None),
            P("section", None, dp),
            P("section", None, dp),
            P("section", None, None),
        ),
        check_vma=False,
    )
```

```python
import functools

import jax
import jax.numpy as jnp
from jax import lax
from jax.experimental import pallas as pl
from jax.experimental.pallas import tpu as pltpu
from jax.sharding import Mesh, PartitionSpec as P

HEADS = 6
HEAD_DIM = 64
PLANE = 4
SCALE = HEAD_DIM ** (-0.5)

epsilon = 1e-06
masked_value = -1000000000.0
AXES = ("section", "line", "plane")
bf16 = jnp.bfloat16
f32 = jnp.float32


def nn(a, b):
    return lax.dot_general(a, b, (((1,), (0,)), ((), ())), preferred_element_type=f32)


def nt(a, b):
    return lax.dot_general(a, b, (((1,), (1,)), ((), ())), preferred_element_type=f32)


def tn(a, b):
    return lax.dot_general(a, b, (((0,), (0,)), ((), ())), preferred_element_type=f32)


def permute(block, axes, route):
    shape = block.shape
    if block.ndim == 2 and shape[0] % 8 == 0:
        block = block.reshape(shape[0] // 8, 8, shape[1])
    return lax.ppermute(block, axes, route).reshape(shape)


def rounded(value):
    return lax.reduce_precision(value, 8, 7).astype(bf16)


def rms_norm(inputs, gain_row):
    return inputs * lax.rsqrt(jnp.mean(inputs * inputs, -1, keepdims=True) + epsilon) * gain_row


def rms_back(inputs, gain_row, upstream):
    scale = lax.rsqrt(jnp.mean(inputs * inputs, -1, keepdims=True) + epsilon)
    normed = inputs * scale
    weighted = upstream * gain_row
    grad = (weighted - normed * jnp.mean(weighted * normed, -1, keepdims=True)) * scale
    return grad, jnp.sum(upstream * normed, 0, keepdims=True)


def gelu_parts(gate):
    slope = (2.0 / jnp.pi) ** 0.5
    square = gate * gate
    half = 0.5 + 0.5 * jnp.tanh(gate * (slope + (slope * 0.044715) * square))
    bend = gate * (slope + (slope * 0.134145) * square)
    return gate * half, half + (2.0 * half) * ((1.0 - half) * bend)


def whole(shape):
    return pl.BlockSpec(shape, lambda step: (0,) * len(shape))


def call(kernel, outputs, *args, scratch=(), specs=None, time_us=0.3, ties=(), vmem=56):
    specs = specs or {}
    in_specs = [
        specs.get(i)
        or (pl.BlockSpec(memory_space=pltpu.SMEM) if a.dtype == jnp.int32 else whole(a.shape))
        for i, a in enumerate(args)
    ]
    in_specs += [pl.BlockSpec(memory_space=pl.ANY)] * len(ties)
    first, after = len(args), len(args) + len(ties)
    out_shape = tuple(jax.ShapeDtypeStruct(output[0], output[1]) for output in outputs)
    return pl.pallas_call(
        lambda *refs: kernel(*refs[:first], *refs[after:]),
        grid=(1,),
        out_shape=out_shape,
        in_specs=in_specs,
        out_specs=tuple(output[2] if len(output) > 2 else whole(output[0]) for output in outputs),
        scratch_shapes=list(scratch),
        compiler_params=pltpu.CompilerParams(vmem_limit_bytes=vmem * 1024 * 1024),
        cost_estimate=pl.CostEstimate(
            flops=int(time_us * 8e8), bytes_accessed=int(time_us * 2.5e6), transcendentals=0
        ),
    )(*args, *ties)


def chances_of(queries, keys, allowed):
    scores = jnp.where(allowed > 0, tn(queries, keys) * SCALE, masked_value)
    exponent = jnp.exp(scores - jnp.max(scores, -1, keepdims=True))
    return exponent / jnp.sum(exponent, -1, keepdims=True)


def attend_into(context_ref, query_ref, key_ref, value_ref, allowed_ref, starts=(0, 0, 0)):
    rows, length, _ = allowed_ref.shape
    for row in range(rows):
        columns = slice(row * length, (row + 1) * length)
        for head in range(HEADS):
            q, k, v = (
                ref[start + head * HEAD_DIM : start + (head + 1) * HEAD_DIM, columns]
                for ref, start in zip((query_ref, key_ref, value_ref), starts)
            )
            weights = chances_of(q, k, allowed_ref[row]).astype(bf16)
            context_ref[head * HEAD_DIM : (head + 1) * HEAD_DIM, columns] = nt(v, weights).astype(bf16)


def attend_back_into(grads_ref, query_ref, key_ref, value_ref, allowed_ref, upstream, starts=(0, 0, 0)):
    rows, length, _ = allowed_ref.shape
    inner = HEADS * HEAD_DIM
    for row in range(rows):
        columns = slice(row * length, (row + 1) * length)
        for head in range(HEADS):
            first = head * HEAD_DIM
            q, k, v = (
                ref[start + first : start + first + HEAD_DIM, columns]
                for ref, start in zip((query_ref, key_ref, value_ref), starts)
            )
            g = upstream[first : first + HEAD_DIM, columns]
            chances = chances_of(q, k, allowed_ref[row])
            weight_grad = tn(g, v)
            score_grad = (
                chances * (weight_grad - jnp.sum(weight_grad * chances, -1, keepdims=True))
            ).astype(bf16)
            grads = (nt(k, score_grad) * SCALE, nn(q, score_grad) * SCALE, nn(g, chances.astype(bf16)))
            for number, grad in enumerate(grads):
                at = number * inner + first
                grads_ref[at : at + HEAD_DIM, columns] = grad.astype(bf16)


def added(refs):
    total = refs[0][...].astype(f32)
    for ref in refs[1:]:
        total = total + ref[...].astype(f32)
    return total


def split_rows(section, value, kept_ref, sent_ref):
    length = kept_ref.shape[0]
    mine, other = value[:length], value[length:]
    kept_ref[...] = jnp.where(section == 0, mine, other)
    sent_ref[...] = jnp.where(section == 0, other, mine)


def self_forward_kernel(section_ref, projected_ref, allowed_ref, inputs_ref, out_w_ref, context_ref, kept_ref, sent_ref):
    inner = context_ref.shape[0]
    attend_into(context_ref, projected_ref, projected_ref, projected_ref, allowed_ref, (0, inner, 2 * inner))
    first_sum = inputs_ref[...] + tn(context_ref[...], out_w_ref[...])
    split_rows(section_ref[0], first_sum, kept_ref, sent_ref)


def first_norm_kernel(section_ref, kept_ref, got_ref, gains_e_ref, gains_d_ref, first_e_ref, first_d_ref, normed_e_ref, normed_d_ref):
    is_encoder = section_ref[0] == 0
    first_e = jnp.where(is_encoder, kept_ref[...], got_ref[...])
    first_d = jnp.where(is_encoder, got_ref[...], kept_ref[...])
    first_e_ref[...] = first_e
    first_d_ref[...] = first_d
    normed_e_ref[...] = rms_norm(first_e, gains_e_ref[1:2]).astype(bf16)
    normed_d_ref[...] = rms_norm(first_d, gains_d_ref[1:2]).astype(bf16)


def joined(refs, out_ref):
    length = refs[0].shape[0]
    for k, ref in enumerate(refs):
        out_ref[k * length : (k + 1) * length] = ref[...]
    return out_ref[...]


def apart(value, refs):
    length = refs[0].shape[0]
    for k, ref in enumerate(refs):
        ref[...] = value[k * length : (k + 1) * length].astype(bf16)


def pack_specs(lines, padded, width):
    return [
        pl.BlockSpec((lines, padded, width), lambda step: (0, 0, 0)),
        pl.BlockSpec((lines, padded // 2, width), lambda step: (0, 2, 0)),
    ]


def rows_of(ref):
    return ref[...].reshape(ref.shape[0] * ref.shape[1], ref.shape[2])


def feed_forward(x, wide, narrow, value_ref, slope_ref, hidden_ref):
    both = nt(wide, x)
    units = both.shape[0] // 2
    value, slope = gelu_parts(both[:units])
    value_ref[...] = value.astype(bf16)
    slope_ref[...] = (slope * both[units:]).astype(bf16)
    hidden_ref[...] = (value * both[units:]).astype(bf16)
    return tn(hidden_ref[...], narrow)


def feed_forward_own_kernel(*refs):
    streams, wide_ref, narrow_ref, value_ref, slope_ref, hidden_ref, part_ref, x_ref = refs[:4], *refs[4:]
    x = joined(streams, x_ref)
    part = feed_forward(x, rows_of(wide_ref), rows_of(narrow_ref), value_ref, slope_ref, hidden_ref)
    part_ref[...] = part.astype(bf16)


def feed_forward_other_kernel(x_ref, prior_ref, wide_ref, narrow_ref, value_ref, slope_ref, hidden_ref, *part_refs):
    part = feed_forward(
        x_ref[...], rows_of(wide_ref), rows_of(narrow_ref), value_ref, slope_ref, hidden_ref
    )
    apart(part + prior_ref[...].astype(f32), part_refs)


def feed_back_kernel(*refs):
    outputs, packs, saved = refs[:4], (refs[4:6], refs[6:8]), refs[8:12]
    grads_refs, output_ref, back_refs = refs[12:14], refs[14], refs[15:]
    output_grad = joined(outputs, output_ref)
    back = None
    for core, (wide_ref, narrow_ref) in enumerate(packs):
        hidden_grad = nt(rows_of(narrow_ref), output_grad)
        units = hidden_grad.shape[0]
        value_ref, slope_ref = saved[2 * core : 2 * core + 2]
        grads_refs[core][:units] = (hidden_grad * slope_ref[...].astype(f32)).astype(bf16)
        grads_refs[core][units:] = (hidden_grad * value_ref[...].astype(f32)).astype(bf16)
        term = tn(grads_refs[core][...], rows_of(wide_ref))
        back = term if back is None else back + term
    apart(back, back_refs)


def feed_both(x, output_grad, wide, narrow, grads_ref):
    both = nt(wide, x)
    hidden_grad = nt(narrow, output_grad)
    units = hidden_grad.shape[0]
    value, slope = gelu_parts(both[:units])
    grads_ref[:units] = (hidden_grad * (slope * both[units:])).astype(bf16)
    grads_ref[units : 2 * units] = (hidden_grad * value).astype(bf16)
    grads_ref[2 * units :] = (value * both[units:]).astype(bf16)
    return tn(grads_ref[2 * units :], narrow), tn(grads_ref[: 2 * units], wide)


def feed_both_own_kernel(*refs):
    streams, outputs, wide_ref, narrow_ref, grads_ref, part_ref, back_ref, x_ref, output_ref = (
        refs[:4],
        refs[4:8],
        *refs[8:],
    )
    x, output_grad = joined(streams, x_ref), joined(outputs, output_ref)
    part, back = feed_both(x, output_grad, rows_of(wide_ref), rows_of(narrow_ref), grads_ref)
    part_ref[...] = part.astype(bf16)
    back_ref[...] = back.astype(bf16)


def feed_both_other_kernel(x_ref, output_ref, part_prior, back_prior, wide_ref, narrow_ref, grads_ref, *refs):
    part, back = feed_both(x_ref[...], output_ref[...], rows_of(wide_ref), rows_of(narrow_ref), grads_ref)
    apart(back + back_prior[...].astype(f32), refs[:4])
    apart(part + part_prior[...].astype(f32), refs[4:])


def feed_grads_kernel(*refs):
    cores, pack_ref = (refs[: len(refs) // 2], refs[len(refs) // 2 : -1]), refs[-1]
    lines = pack_ref.shape[0]
    wide = narrow = 0.0
    for x_ref, output_ref, *factors in cores:
        if len(factors) == 1:
            units = factors[0].shape[0] // 3
            grads, hidden = factors[0][: 2 * units], factors[0][2 * units :]
        else:
            grads, hidden = factors[0][...], factors[1][...]
        wide = wide + nn(grads, x_ref[...])
        narrow = narrow + nn(hidden, output_ref[...])
    padded = wide.shape[0] // lines
    pack_ref[:, :padded] = wide.astype(bf16).reshape(lines, padded, wide.shape[1])
    pack_ref[:, padded:] = narrow.astype(bf16).reshape(lines, padded // 2, wide.shape[1])


def middle_kernel(*refs):
    parts = refs[:4]
    first_e_ref, first_d_ref, normed_d_ref, gains_e_ref, gains_d_ref, cross_e_ref, cross_d_ref, allowed_ref = refs[4:12]
    second_e_ref, normed_e_ref, queries_ref, states_ref, context_ref, second_d_ref, normed_last_ref = refs[12:]
    inner = context_ref.shape[0]
    queries_ref[...] = nt(cross_d_ref[:inner], normed_d_ref[...]).astype(bf16)
    second_e = first_e_ref[...] + added(parts)
    second_e_ref[...] = second_e
    normed = rms_norm(second_e, gains_e_ref[2:3]).astype(bf16)
    normed_e_ref[...] = normed
    states_ref[...] = nt(cross_e_ref[...], normed).astype(bf16)
    attend_into(context_ref, queries_ref, states_ref, states_ref, allowed_ref, (0, 0, inner))
    second_d = first_d_ref[...] + tn(context_ref[...], cross_d_ref[inner:])
    second_d_ref[...] = second_d
    normed_last_ref[...] = rms_norm(second_d, gains_d_ref[2:3]).astype(bf16)


def middle_back_kernel(*refs):
    parts = refs[:4]
    second_d_ref, second_e_ref, cotangent_d_ref, cotangent_e_ref, gains_d_ref, gains_e_ref = refs[4:10]
    cross_d_ref, cross_e_ref, queries_ref, states_ref, allowed_ref = refs[10:15]
    stream_d_ref, branch_ref, grads_ref, stream_e_ref, sent_ref, gain_d_ref, gain_e_ref = refs[15:]
    inner = queries_ref.shape[0]
    input_grad, gain_d_ref[...] = rms_back(second_d_ref[...], gains_d_ref[2:3], added(parts))
    stream_d = cotangent_d_ref[...].astype(f32) + input_grad
    stream_d_ref[...] = stream_d
    branch = stream_d.astype(bf16)
    branch_ref[...] = branch
    context_grad = nt(cross_d_ref[inner:], branch).astype(bf16)
    attend_back_into(grads_ref, queries_ref, states_ref, states_ref, allowed_ref, context_grad, (0, 0, inner))
    final_grad = tn(grads_ref[inner:], cross_e_ref[...])
    input_grad, gain_e_ref[...] = rms_back(second_e_ref[...], gains_e_ref[2:3], final_grad)
    stream_e = cotangent_e_ref[...].astype(f32) + input_grad
    stream_e_ref[...] = stream_e
    sent_ref[...] = stream_e.astype(bf16)


def first_back_d_kernel(grads_ref, cross_d_ref, first_d_ref, gains_d_ref, stream_ref, out_ref, gain_ref):
    inner = cross_d_ref.shape[0] // 2
    upstream = tn(grads_ref[:inner], cross_d_ref[:inner])
    input_grad, gain_ref[...] = rms_back(first_d_ref[...], gains_d_ref[1:2], upstream)
    out_ref[...] = stream_ref[...] + input_grad


def first_back_e_kernel(*refs):
    parts = refs[:4]
    section_ref, first_e_ref, gains_e_ref, stream_ref, stream_d_ref, kept_ref, sent_ref, gain_ref = refs[4:]
    input_grad, gain_ref[...] = rms_back(first_e_ref[...], gains_e_ref[1:2], added(parts))
    stream_e = stream_ref[...] + input_grad
    is_encoder = section_ref[0] == 0
    kept_ref[...] = jnp.where(is_encoder, stream_e, stream_d_ref[...])
    sent_ref[...] = jnp.where(is_encoder, stream_d_ref[...], stream_e)


def self_back_kernel(section_ref, kept_ref, got_ref, out_w_ref, projected_ref, allowed_ref, stream_ref, branch_ref, grads_ref):
    is_encoder = section_ref[0] == 0
    inner, length = out_w_ref.shape[0], kept_ref.shape[0]
    stream_ref[:length] = jnp.where(is_encoder, kept_ref[...], got_ref[...])
    stream_ref[length:] = jnp.where(is_encoder, got_ref[...], kept_ref[...])
    branch = stream_ref[...].astype(bf16)
    branch_ref[...] = branch
    context_grad = nt(out_w_ref[...], branch).astype(bf16)
    attend_back_into(
        grads_ref, projected_ref, projected_ref, projected_ref, allowed_ref, context_grad, (0, inner, 2 * inner)
    )


def table_kernel(*refs):
    grads, codes, gain_refs, (section_ref, in_ref, embedding_ref, gain_ref, stream_ref, out_ref) = (
        refs[:4],
        refs[4:8],
        refs[8:12],
        refs[12:],
    )
    table = gain_grad = 0.0
    for k, (grad, code_ref) in enumerate(zip(grads, codes)):
        shape = (embedding_ref.shape[0], code_ref.shape[1])
        one_hot = (lax.broadcasted_iota(jnp.int32, shape, 0) == code_ref[...]).astype(bf16)
        inputs = tn(one_hot, embedding_ref[...])
        input_grad, gain_part = rms_back(inputs, gain_ref[...], tn(grad[...], in_ref[...]))
        if k == 0:
            input_grad = input_grad + stream_ref[...]
        gain_grad = gain_grad + gain_part
        table = table + nn(one_hot, input_grad.astype(bf16))
    vocabulary = embedding_ref.shape[0]
    out_ref[:vocabulary] = table.astype(bf16)
    nothing, is_encoder = jnp.zeros_like(gain_grad), section_ref[0] == 0
    rows = [jnp.where(is_encoder, gain_grad, nothing), gain_refs[0][...], gain_refs[1][...]]
    rows += [jnp.where(is_encoder, nothing, gain_grad), gain_refs[2][...], gain_refs[3][...]]
    rows.append(jnp.zeros((out_ref.shape[0] - vocabulary - 6, out_ref.shape[1]), f32))
    out_ref[vocabulary:] = jnp.concatenate(rows, 0).astype(bf16)


def assemble_kernel(section_ref, plane_ref, *refs):
    pieces, (table_ref, gains_ref, rows_ref) = refs[:PLANE], refs[PLANE:]
    count = pieces[0].shape[0]
    for k, piece in enumerate(pieces):
        rows_ref[pl.ds(pl.multiple_of((plane_ref[0] ^ k) * count, 8), count)] = piece[...].astype(f32)
    vocabulary = table_ref.shape[0]
    table_ref[...] = rows_ref[:vocabulary]
    gains = rows_ref[vocabulary : vocabulary + 8]
    gains_ref[0] = jnp.where(section_ref[0] == 0, gains[:3], gains[3:6])


def in_grad_kernel(*refs):
    grads, streams, out_ref = refs[:4], refs[4:8], refs[8]
    total = nn(grads[0][...], streams[0][...])
    for grad, stream in zip(grads[1:], streams[1:]):
        total = total + nn(grad[...], stream[...])
    out_ref[...] = total.astype(bf16)


def cross_grads_kernel(section_ref, grads_ref, normed_e_ref, normed_d_ref, context_ref, branch_ref, kept_ref, sent_ref):
    inner = context_ref.shape[0]
    is_encoder = section_ref[0] == 0
    grad_e = nn(grads_ref[inner:], normed_e_ref[...])
    grad_first = nn(grads_ref[:inner], normed_d_ref[...])
    grad_second = nn(context_ref[...], branch_ref[...])
    for start, grad_d in ((0, grad_first), (inner, grad_second)):
        part_e = grad_e[start : start + inner]
        kept_ref[start : start + inner] = jnp.where(is_encoder, part_e, grad_d).astype(bf16)
        sent_ref[start : start + inner] = jnp.where(is_encoder, grad_d, part_e).astype(bf16)


def build(lines):
    devices = lines * PLANE

    def place(section, line, plane):
        return section * devices + line * PLANE + plane

    def hop(block, offset):
        route = [
            (place(s, z, j), place(s, z, j ^ offset))
            for s in range(2)
            for z in range(lines)
            for j in range(PLANE)
        ]
        return permute(block, AXES, route)

    def swap(block):
        return permute(block, "section", [(0, 1), (1, 0)])

    narrow_route = []
    for core in range(2):
        for block in range(devices):
            target = (block % 2, 2 * (block // 8) + core, (block % 8) // 2)
            narrow_route.append((core * devices + block, place(*target)))

    def at(array, index, axis=0):
        return lax.dynamic_index_in_dim(array, index, axis, False)

    def ordered(own, others, index, axis=0):
        count = len(others) + 1
        shape = own.shape[:axis] + (count,) + own.shape[axis:]
        out = jnp.zeros(shape, own.dtype)
        for where_to, piece in [(index, own)] + others:
            out = lax.dynamic_update_index_in_dim(out, piece, where_to, axis)
        return out

    def sum_line(block):
        if lines & (lines - 1):
            return rounded(lax.psum(block.astype(f32), "line"))
        distance = 1
        while distance < lines:
            route = [(z, z ^ distance) for z in range(lines)]
            block = rounded(block.astype(f32) + permute(block, "line", route).astype(f32))
            distance *= 2
        return block

    def in_plane(blocks, axis=0):
        j = lax.axis_index("plane")
        return ordered(blocks[0], [(j ^ k, blocks[k]) for k in range(1, PLANE)], j, axis)

    def gather_plane(block, axis=0):
        return in_plane(spread(block), axis)

    def scattered(parts):
        j = lax.axis_index("plane")
        return [at(parts, j)] + [hop(at(parts, j ^ k), k) for k in range(1, PLANE)]

    def total_of(terms):
        return sum((term.astype(f32) for term in terms[1:]), terms[0].astype(f32))

    def spread(block):
        return [block] + [hop(block, k) for k in range(1, PLANE)]

    def collected(parts):
        return [parts[0]] + [hop(parts[k], k) for k in range(1, PLANE)]

    def per_device(
        byte_codes,
        encoder_segments,
        target_segments,
        embedding,
        attention_in,
        attention_out,
        widen_weight,
        narrow_weight,
        cross_first,
        cross_second,
        norm_gains,
        cotangent,
    ):
        section = lax.axis_index("section")
        j = lax.axis_index("plane")
        is_encoder = section == 0
        section_scalar = section.astype(jnp.int32).reshape(1)
        inner = cross_first.shape[2] * devices
        vocabulary, width = embedding.shape
        rows, length = encoder_segments.shape
        tokens = rows * length

        def together(*values):
            return list(lax.optimization_barrier(values))

        def by_section(mine, other):
            return jnp.where(is_encoder, mine, other), jnp.where(is_encoder, other, mine)

        def in_order(mine, other):
            return jnp.concatenate(by_section(mine, other), 0)

        in_cols = attention_in.shape[2]
        cross_cols = cross_first.shape[2]
        column, codes = together(
            jnp.concatenate([attention_in[0].T, attention_out[0], cross_first[0].T, cross_second[0].T], 0),
            byte_codes[0],
        )
        column = lax.all_gather(column, "line", axis=0)
        in_column = column[:, :in_cols].reshape(-1, width)

        widen_half = widen_weight.shape[2] // 2
        narrow_half = narrow_weight.shape[1] // 2
        padded_narrow = -(-narrow_half // 16) * 16
        padded_widen = 2 * padded_narrow

        def widened(block):
            return jnp.pad(block, ((0, 0),) * (block.ndim - 2) + ((0, padded_narrow - narrow_half), (0, 0)))

        narrow_parts = widened(narrow_weight[0].reshape(2, narrow_half, width))
        narrow_e, narrow_d = by_section(at(narrow_parts, section), swap(at(narrow_parts, 1 - section)))
        moved = permute(jnp.concatenate([narrow_e, narrow_d], 0), AXES, narrow_route)
        widen_parts = widened(widen_weight[0].T.reshape(2, 2, narrow_half, width)).reshape(
            2, padded_widen, width
        )
        widen_e, widen_d = by_section(at(widen_parts, section), swap(at(widen_parts, 1 - section)))

        columns = lax.broadcasted_iota(jnp.int32, (tokens, vocabulary), 1)
        inputs = nn((codes.reshape(tokens, 1) == columns).astype(bf16), embedding)
        codes_plane = spread(codes.reshape(1, tokens))
        own_segments = jnp.where(is_encoder, encoder_segments, target_segments)
        earlier = lax.broadcasted_iota(jnp.int32, (length, length), 1) <= lax.broadcasted_iota(
            jnp.int32, (length, length), 0
        )
        allowed = (
            (own_segments[:, :, None] == own_segments[:, None, :]) & (earlier | is_encoder)[None]
        ).astype(f32)
        encoder_row, target_row = at(encoder_segments, section), at(target_segments, section)
        cross_allowed = (target_row[:, None] == encoder_row[None, :]).astype(f32)[None]

        own_gains = norm_gains[0]
        received = swap(jnp.concatenate([at(cotangent[0], 1 - section), own_gains], 0))
        cotangent_e, cotangent_d = by_section(at(cotangent[0], section), received[:length])
        gains_e, gains_d = (g.astype(f32) for g in by_section(own_gains, received[length:]))
        gain_self = own_gains[:1].astype(f32)

        normed_plane = spread(rms_norm(inputs, gain_self).astype(bf16))
        moved, *planes = together(moved, *normed_plane, *codes_plane)
        normed_plane, codes_plane = planes[:PLANE], planes[PLANE:]
        pack_e, pack_d = lax.optimization_barrier(
            (
                jnp.concatenate([widen_e, moved[:padded_narrow]], 0),
                jnp.concatenate([widen_d, moved[padded_narrow:]], 0),
            )
        )
        own_e = lax.all_gather(pack_e, "line", axis=0)
        own_d = lax.all_gather(pack_d, "line", axis=0)

        projected_parts = [
            nt(in_column, block).astype(bf16).reshape(lines, in_cols, tokens) for block in normed_plane
        ]
        hopped = together(*[hop(projected_parts[k], k) for k in range(1, PLANE)], column)
        column = hopped[-1]
        projected = in_plane([projected_parts[0], *hopped[:-1]], 1).reshape(3 * inner, tokens)
        out_pieces = together(*spread(column[:, in_cols : in_cols + cross_cols]), column)
        column = out_pieces[-1]
        out_w = in_plane(out_pieces[:-1], 1).reshape(inner, width)
        row_f32, row_bf16 = ((length, width), f32), ((length, width), bf16)
        context, first_kept, first_sent = call(
            self_forward_kernel,
            (((inner, tokens), bf16), row_f32, row_f32),
            section_scalar,
            projected,
            allowed,
            inputs,
            out_w,
        )

        first_e, first_d, normed_first, normed_cross = call(
            first_norm_kernel,
            (row_f32, row_f32, row_bf16, row_bf16),
            section_scalar,
            first_kept,
            swap(first_sent),
            gains_e,
            gains_d,
        )
        stream_e = spread(normed_first)
        column, *stream_e = together(column, *stream_e)
        cross_pieces = spread(column[:, in_cols + cross_cols :])
        group = PLANE * length
        group_bf16 = ((group, width), bf16)
        pack_shape = (lines, padded_widen + padded_narrow, width)
        halves_of = pack_specs(lines, padded_widen, width)
        units = lines * padded_narrow
        unit_bf16, pair_bf16, trio_bf16 = (((n * units, group), bf16) for n in (1, 2, 3))
        blocks_bf16 = (row_bf16,) * PLANE

        def with_packs(first, *packs):
            specs = {first + 2 * i + k: halves_of[k] for i in range(len(packs)) for k in range(2)}
            return dict(specs=specs), [pack for pack in packs for _ in range(2)]

        def feed_grads(own, other, *ties):
            (pack,) = call(feed_grads_kernel, ((pack_shape, bf16),), *own, *other, time_us=0.3, ties=ties)
            return pack

        own_e, *stream_e = together(own_e, *stream_e)
        other_e = swap(own_e)
        cotangent_d, *stream_e = together(cotangent_d, *stream_e)
        options, packs = with_packs(4, own_e)
        value_own, slope_own, hidden_own, part_own, x_e = call(
            feed_forward_own_kernel,
            (unit_bf16, unit_bf16, unit_bf16, group_bf16, group_bf16),
            *stream_e,
            *packs,
            **options,
        )
        output_grad_d = spread(cotangent_d)
        x_e, *cross_pieces = together(x_e, *cross_pieces)
        cross_w = in_plane(cross_pieces, 1).reshape(devices, 2, cross_cols, width).swapaxes(0, 1)
        cross_w = cross_w.reshape(2 * inner, width)
        cross_e, cross_d = by_section(cross_w, swap(cross_w))
        options, packs = with_packs(2, other_e)
        value_other, slope_other, hidden_other, *part_e = call(
            feed_forward_other_kernel,
            (unit_bf16, unit_bf16, unit_bf16, *blocks_bf16),
            x_e,
            part_own,
            *packs,
            **options,
        )
        *part_e, output_grad_d[1], output_grad_d[2], output_grad_d[3] = together(
            *part_e, *output_grad_d[1:]
        )

        second_e, normed_final, cross_queries, states, cross_context, second_d, normed_last = call(
            middle_kernel,
            (
                row_f32,
                row_bf16,
                ((inner, length), bf16),
                ((2 * inner, length), bf16),
                ((inner, length), bf16),
                row_f32,
                row_bf16,
            ),
            *collected(part_e),
            first_e,
            first_d,
            normed_cross,
            gains_e,
            gains_d,
            cross_e,
            cross_d,
            cross_allowed,
        )

        stream_d = spread(normed_last)
        own_d, *stream_d = together(own_d, *stream_d)
        other_d = swap(own_d)
        options, packs = with_packs(8, own_d)
        factors_d, part_own, back_own, x_d, joined_grad_d = call(
            feed_both_own_kernel,
            (trio_bf16, group_bf16, group_bf16, group_bf16, group_bf16),
            *stream_d,
            *output_grad_d,
            *packs,
            **options,
        )
        options, packs = with_packs(4, other_d)
        factors_other_d, *blocks = call(
            feed_both_other_kernel,
            (trio_bf16, *blocks_bf16, *blocks_bf16),
            x_d,
            joined_grad_d,
            part_own,
            back_own,
            *packs,
            **options,
        )
        feed_sum_d = feed_grads(
            (x_d, joined_grad_d, factors_d),
            (swap(x_d), swap(joined_grad_d), swap(factors_other_d)),
        )
        back_d, part_d = collected(blocks[:PLANE]), blocks[PLANE:]
        gain_shape = ((1, width), f32)
        stream_two_d, cross_branch, cross_grads, stream_two_e, sent_e, gain_two_d, gain_two_e = call(
            middle_back_kernel,
            (row_f32, row_bf16, ((3 * inner, length), bf16), row_f32, row_bf16, gain_shape, gain_shape),
            *back_d,
            second_d,
            second_e,
            cotangent_d,
            cotangent_e,
            gains_d,
            gains_e,
            cross_d,
            cross_e,
            cross_queries,
            states,
            cross_allowed,
            ties=(feed_sum_d,),
        )

        stream_one_d, gain_one_d = call(
            first_back_d_kernel,
            (row_f32, gain_shape),
            cross_grads,
            cross_d,
            first_d,
            gains_d,
            stream_two_d,
        )
        output_grad_e = together(*spread(sent_e))
        cross_kept, cross_sent = call(
            cross_grads_kernel,
            (((2 * inner, width), bf16), ((2 * inner, width), bf16)),
            section_scalar,
            cross_grads,
            normed_final,
            normed_cross,
            cross_context,
            cross_branch,
        )
        cross_grad = (cross_kept.astype(f32) + swap(cross_sent).astype(f32)).astype(bf16)
        options, packs = with_packs(4, own_e, other_e)
        grads_own, grads_other, joined_grad_e, *back_e = call(
            feed_back_kernel,
            (pair_bf16, pair_bf16, group_bf16, *blocks_bf16),
            *output_grad_e,
            *packs,
            value_own,
            slope_own,
            value_other,
            slope_other,
            ties=(stream_one_d, cross_kept),
            time_us=0.3,
            **options,
        )
        def by_plane(*products):
            parts = [m.astype(bf16).reshape(lines, PLANE, -1, width).swapaxes(0, 1) for m in products]
            return jnp.concatenate(parts, 2)

        cross_terms = scattered(by_plane(cross_grad[:inner], cross_grad[inner:]))
        feed_sum_e = feed_grads(
            (x_e, joined_grad_e, grads_own, hidden_own),
            (swap(x_e), swap(joined_grad_e), swap(grads_other), swap(hidden_other)),
        )
        back_e = collected(back_e)

        summed_d = lax.psum_scatter(feed_sum_d, "line", scatter_dimension=0)
        feed_sum_e, summed_d = together(feed_sum_e, summed_d)
        summed_e = lax.psum_scatter(feed_sum_e, "line", scatter_dimension=0)

        stream_kept, stream_sent, gain_one_e = call(
            first_back_e_kernel,
            (row_f32, row_f32, gain_shape),
            *back_e,
            section_scalar,
            first_e,
            gains_e,
            stream_two_e,
            stream_one_d,
            ties=(feed_sum_e,),
        )
        stream_got = swap(stream_sent)
        stream_one, branch_grad, projected_grad = call(
            self_back_kernel,
            (((tokens, width), f32), ((tokens, width), bf16), ((3 * inner, tokens), bf16)),
            section_scalar,
            stream_kept,
            stream_got,
            out_w,
            projected,
            allowed,
        )
        projected_grad, *cross_terms = together(projected_grad, *cross_terms)
        parts = projected_grad.reshape(lines, PLANE, in_cols, tokens)
        grad_parts = [at(parts, j, 1)] + [hop(at(parts, j ^ k, 1), k) for k in range(1, PLANE)]
        branch_grad, *grad_parts = together(
            branch_grad, *[part.reshape(lines * in_cols, tokens) for part in grad_parts]
        )
        out_part = total_of(scattered(by_plane(nn(context, branch_grad)))).astype(bf16)
        cross_part = total_of(cross_terms).astype(bf16)
        (in_part,) = call(
            in_grad_kernel,
            (((lines * in_cols, width), bf16),),
            *grad_parts,
            *normed_plane,
        )
        padded = -(-(vocabulary + 6) // 64) * 64
        (small,) = call(
            table_kernel,
            (((padded, width), bf16),),
            *grad_parts,
            *codes_plane,
            gain_one_e,
            gain_two_e,
            gain_one_d,
            gain_two_d,
            section_scalar,
            in_column,
            embedding,
            gain_self,
            stream_one,
            specs={4 + k: whole((1, tokens)) for k in range(PLANE)},
        )
        plane_sum = rounded(total_of(scattered(small.reshape(PLANE, -1, width))))
        plane_sum, summed_e, *part_d = together(plane_sum, summed_e, *part_d)
        part_d = collected(part_d)
        halves = plane_sum.reshape(2, padded // 8, width)
        chip_sum = rounded(at(halves, section).astype(f32) + swap(at(halves, 1 - section)).astype(f32))
        rest_pack = jnp.concatenate([in_part.reshape(lines, in_cols, width), cross_part, out_part], 1)
        rest_pack, line_sum, summed_d, summed_e = together(
            rest_pack, sum_line(chip_sum), summed_d, summed_e
        )
        rest_sum = lax.psum_scatter(rest_pack, "line", scatter_dimension=0).astype(f32)
        pieces = together(*spread(in_order(line_sum, swap(line_sum))), *part_d)
        second_out_d = second_d + sum(part.astype(f32) for part in pieces[PLANE:])
        embedding_grad, gains_grad = call(
            assemble_kernel,
            (((vocabulary, width), f32), ((1, 3, width), f32)),
            section_scalar,
            j.astype(jnp.int32).reshape(1),
            *pieces[:PLANE],
            scratch=(pltpu.VMEM((padded, width), f32),),
        )

        narrow = permute(
            jnp.concatenate([summed_e[padded_widen:], summed_d[padded_widen:]], 0),
            AXES,
            [(b, a) for a, b in narrow_route],
        )
        half_e = jnp.concatenate([summed_e[:padded_widen], narrow[:padded_narrow]], 0)
        half_d = jnp.concatenate([summed_d[:padded_widen], narrow[padded_narrow:]], 0)
        half_kept, half_sent = by_section(half_e, half_d)
        both = in_order(half_kept[None], swap(half_sent)[None])
        both = both.reshape(2, 3, padded_narrow, width)[:, :, :narrow_half]
        widen_t = both[:, :2].reshape(2 * widen_half, width)
        narrow_grad = both[:, 2].reshape(2 * narrow_half, width).astype(f32)

        output_kept, output_sent = by_section(second_e.astype(bf16), second_out_d.astype(bf16))
        block_output = in_order(output_kept, swap(output_sent)).reshape(rows, length, width)
        cuts = [0, in_cols, in_cols + cross_cols, in_cols + 2 * cross_cols, in_cols + 3 * cross_cols]
        in_sum, first_cross_sum, second_cross_sum, out_sum = (
            rest_sum[a:b] for a, b in zip(cuts[:-1], cuts[1:])
        )
        return (
            block_output[None],
            embedding_grad,
            in_sum.T[None],
            out_sum[None],
            widen_t.astype(f32).T[None],
            narrow_grad[None],
            first_cross_sum.T[None],
            second_cross_sum.T[None],
            gains_grad,
        )

    return per_device


def solution(mesh):
    lines = mesh.shape["dp"] // PLANE
    inner_mesh = Mesh(mesh.devices.reshape(2, lines, PLANE), AXES)
    dp = ("line", "plane")
    return jax.shard_map(
        build(lines),
        mesh=inner_mesh,
        in_specs=(
            P("section", dp, None),
            P(dp, None),
            P(dp, None),
            P(),
            P("section", None, dp),
            P("section", dp, None),
            P("section", None, dp),
            P("section", dp, None),
            P("section", None, dp),
            P("section", None, dp),
            P("section", None, None),
            P("section", dp, None, None),
        ),
        out_specs=(
            P("section", dp, None, None),
            P(),
            P("section", None, dp),
            P("section", dp, None),
            P("section", None, dp),
            P("section", dp, None),
            P("section", None, dp),
            P("section", None, dp),
            P("section", None, None),
        ),
        check_vma=False,
    )
```

```python
import functools

import jax
import jax.numpy as jnp
from jax import lax
from jax.experimental import pallas as pl
from jax.experimental.pallas import tpu as pltpu
from jax.sharding import Mesh, PartitionSpec as P

HEADS = 6
HEAD_DIM = 64
PLANE = 4
SCALE = HEAD_DIM ** (-0.5)

epsilon = 1e-06
masked_value = -1000000000.0
AXES = ("section", "line", "plane")
bf16 = jnp.bfloat16
f32 = jnp.float32


def nn(a, b):
    return lax.dot_general(a, b, (((1,), (0,)), ((), ())), preferred_element_type=f32)


def nt(a, b):
    return lax.dot_general(a, b, (((1,), (1,)), ((), ())), preferred_element_type=f32)


def tn(a, b):
    return lax.dot_general(a, b, (((0,), (0,)), ((), ())), preferred_element_type=f32)


def permute(block, axes, route):
    shape = block.shape
    if block.ndim == 2 and shape[0] % 8 == 0:
        block = block.reshape(shape[0] // 8, 8, shape[1])
    return lax.ppermute(block, axes, route).reshape(shape)


def rounded(value):
    return lax.reduce_precision(value, 8, 7).astype(bf16)


def rms_norm(inputs, gain_row):
    return inputs * lax.rsqrt(jnp.mean(inputs * inputs, -1, keepdims=True) + epsilon) * gain_row


def rms_back(inputs, gain_row, upstream):
    scale = lax.rsqrt(jnp.mean(inputs * inputs, -1, keepdims=True) + epsilon)
    normed = inputs * scale
    weighted = upstream * gain_row
    grad = (weighted - normed * jnp.mean(weighted * normed, -1, keepdims=True)) * scale
    return grad, jnp.sum(upstream * normed, 0, keepdims=True)


def gelu_parts(gate):
    slope = (2.0 / jnp.pi) ** 0.5
    square = gate * gate
    half = 0.5 + 0.5 * jnp.tanh(gate * (slope + (slope * 0.044715) * square))
    bend = gate * (slope + (slope * 0.134145) * square)
    return gate * half, half + (2.0 * half) * ((1.0 - half) * bend)


def whole(shape):
    return pl.BlockSpec(shape, lambda step: (0,) * len(shape))


def call(kernel, outputs, *args, scratch=(), specs=None, time_us=1, ties=(), vmem=56):
    specs = specs or {}
    in_specs = [
        specs.get(i)
        or (pl.BlockSpec(memory_space=pltpu.SMEM) if a.dtype == jnp.int32 else whole(a.shape))
        for i, a in enumerate(args)
    ]
    in_specs += [pl.BlockSpec(memory_space=pl.ANY)] * len(ties)
    first, after = len(args), len(args) + len(ties)
    out_shape = tuple(jax.ShapeDtypeStruct(output[0], output[1]) for output in outputs)
    return pl.pallas_call(
        lambda *refs: kernel(*refs[:first], *refs[after:]),
        grid=(1,),
        out_shape=out_shape,
        in_specs=in_specs,
        out_specs=tuple(output[2] if len(output) > 2 else whole(output[0]) for output in outputs),
        scratch_shapes=list(scratch),
        compiler_params=pltpu.CompilerParams(vmem_limit_bytes=vmem * 1024 * 1024),
        cost_estimate=pl.CostEstimate(
            flops=int(time_us * 8e8), bytes_accessed=int(time_us * 2.5e6), transcendentals=0
        ),
    )(*args, *ties)


def chances_of(queries, keys, allowed):
    scores = jnp.where(allowed > 0, tn(queries, keys) * SCALE, masked_value)
    exponent = jnp.exp(scores - jnp.max(scores, -1, keepdims=True))
    return exponent / jnp.sum(exponent, -1, keepdims=True)


def attend_into(context_ref, query_ref, key_ref, value_ref, allowed_ref, starts=(0, 0, 0)):
    rows, length, _ = allowed_ref.shape
    for row in range(rows):
        columns = slice(row * length, (row + 1) * length)
        for head in range(HEADS):
            q, k, v = (
                ref[start + head * HEAD_DIM : start + (head + 1) * HEAD_DIM, columns]
                for ref, start in zip((query_ref, key_ref, value_ref), starts)
            )
            weights = chances_of(q, k, allowed_ref[row]).astype(bf16)
            context_ref[head * HEAD_DIM : (head + 1) * HEAD_DIM, columns] = nt(v, weights).astype(bf16)


def attend_back_into(grads_ref, query_ref, key_ref, value_ref, allowed_ref, upstream, starts=(0, 0, 0)):
    rows, length, _ = allowed_ref.shape
    inner = HEADS * HEAD_DIM
    for row in range(rows):
        columns = slice(row * length, (row + 1) * length)
        for head in range(HEADS):
            first = head * HEAD_DIM
            q, k, v = (
                ref[start + first : start + first + HEAD_DIM, columns]
                for ref, start in zip((query_ref, key_ref, value_ref), starts)
            )
            g = upstream[first : first + HEAD_DIM, columns]
            chances = chances_of(q, k, allowed_ref[row])
            weight_grad = tn(g, v)
            score_grad = (
                chances * (weight_grad - jnp.sum(weight_grad * chances, -1, keepdims=True))
            ).astype(bf16)
            grads = (nt(k, score_grad) * SCALE, nn(q, score_grad) * SCALE, nn(g, chances.astype(bf16)))
            for number, grad in enumerate(grads):
                at = number * inner + first
                grads_ref[at : at + HEAD_DIM, columns] = grad.astype(bf16)


def added(refs):
    total = refs[0][...].astype(f32)
    for ref in refs[1:]:
        total = total + ref[...].astype(f32)
    return total


def split_rows(section, value, kept_ref, sent_ref):
    length = kept_ref.shape[0]
    mine, other = value[:length], value[length:]
    kept_ref[...] = jnp.where(section == 0, mine, other)
    sent_ref[...] = jnp.where(section == 0, other, mine)


def self_forward_kernel(section_ref, projected_ref, allowed_ref, inputs_ref, out_w_ref, context_ref, kept_ref, sent_ref):
    inner = context_ref.shape[0]
    attend_into(context_ref, projected_ref, projected_ref, projected_ref, allowed_ref, (0, inner, 2 * inner))
    first_sum = inputs_ref[...] + tn(context_ref[...], out_w_ref[...])
    split_rows(section_ref[0], first_sum, kept_ref, sent_ref)


def first_norm_kernel(section_ref, kept_ref, got_ref, gains_e_ref, gains_d_ref, first_e_ref, first_d_ref, normed_e_ref, normed_d_ref):
    is_encoder = section_ref[0] == 0
    first_e = jnp.where(is_encoder, kept_ref[...], got_ref[...])
    first_d = jnp.where(is_encoder, got_ref[...], kept_ref[...])
    first_e_ref[...] = first_e
    first_d_ref[...] = first_d
    normed_e_ref[...] = rms_norm(first_e, gains_e_ref[1:2]).astype(bf16)
    normed_d_ref[...] = rms_norm(first_d, gains_d_ref[1:2]).astype(bf16)


def joined(refs, out_ref):
    length = refs[0].shape[0]
    for k, ref in enumerate(refs):
        out_ref[k * length : (k + 1) * length] = ref[...]
    return out_ref[...]


def apart(value, refs):
    length = refs[0].shape[0]
    for k, ref in enumerate(refs):
        ref[...] = value[k * length : (k + 1) * length].astype(bf16)


def pack_specs(lines, padded, width):
    return [
        pl.BlockSpec((lines, padded, width), lambda step: (0, 0, 0)),
        pl.BlockSpec((lines, padded // 2, width), lambda step: (0, 2, 0)),
    ]


def rows_of(ref):
    return ref[...].reshape(ref.shape[0] * ref.shape[1], ref.shape[2])


def feed_forward(x, wide, narrow, value_ref, slope_ref, hidden_ref):
    both = nt(wide, x)
    units = both.shape[0] // 2
    value, slope = gelu_parts(both[:units])
    value_ref[...] = value.astype(bf16)
    slope_ref[...] = (slope * both[units:]).astype(bf16)
    hidden_ref[...] = (value * both[units:]).astype(bf16)
    return tn(hidden_ref[...], narrow)


def feed_forward_own_kernel(*refs):
    streams, wide_ref, narrow_ref, value_ref, slope_ref, hidden_ref, part_ref, x_ref = refs[:4], *refs[4:]
    x = joined(streams, x_ref)
    part = feed_forward(x, rows_of(wide_ref), rows_of(narrow_ref), value_ref, slope_ref, hidden_ref)
    part_ref[...] = part.astype(bf16)


def feed_forward_other_kernel(x_ref, prior_ref, wide_ref, narrow_ref, value_ref, slope_ref, hidden_ref, *part_refs):
    part = feed_forward(
        x_ref[...], rows_of(wide_ref), rows_of(narrow_ref), value_ref, slope_ref, hidden_ref
    )
    apart(part + prior_ref[...].astype(f32), part_refs)


def feed_back_kernel(*refs):
    outputs, packs, saved = refs[:4], (refs[4:6], refs[6:8]), refs[8:12]
    grads_refs, output_ref, back_refs = refs[12:14], refs[14], refs[15:]
    output_grad = joined(outputs, output_ref)
    back = None
    for core, (wide_ref, narrow_ref) in enumerate(packs):
        hidden_grad = nt(rows_of(narrow_ref), output_grad)
        units = hidden_grad.shape[0]
        value_ref, slope_ref = saved[2 * core : 2 * core + 2]
        grads_refs[core][:units] = (hidden_grad * slope_ref[...].astype(f32)).astype(bf16)
        grads_refs[core][units:] = (hidden_grad * value_ref[...].astype(f32)).astype(bf16)
        term = tn(grads_refs[core][...], rows_of(wide_ref))
        back = term if back is None else back + term
    apart(back, back_refs)


def feed_both(x, output_grad, wide, narrow, grads_ref):
    both = nt(wide, x)
    hidden_grad = nt(narrow, output_grad)
    units = hidden_grad.shape[0]
    value, slope = gelu_parts(both[:units])
    grads_ref[:units] = (hidden_grad * (slope * both[units:])).astype(bf16)
    grads_ref[units : 2 * units] = (hidden_grad * value).astype(bf16)
    grads_ref[2 * units :] = (value * both[units:]).astype(bf16)
    return tn(grads_ref[2 * units :], narrow), tn(grads_ref[: 2 * units], wide)


def feed_both_own_kernel(*refs):
    streams, outputs, wide_ref, narrow_ref, grads_ref, part_ref, back_ref, x_ref, output_ref = (
        refs[:4],
        refs[4:8],
        *refs[8:],
    )
    x, output_grad = joined(streams, x_ref), joined(outputs, output_ref)
    part, back = feed_both(x, output_grad, rows_of(wide_ref), rows_of(narrow_ref), grads_ref)
    part_ref[...] = part.astype(bf16)
    back_ref[...] = back.astype(bf16)


def feed_both_other_kernel(x_ref, output_ref, part_prior, back_prior, wide_ref, narrow_ref, grads_ref, *refs):
    part, back = feed_both(x_ref[...], output_ref[...], rows_of(wide_ref), rows_of(narrow_ref), grads_ref)
    apart(back + back_prior[...].astype(f32), refs[:4])
    apart(part + part_prior[...].astype(f32), refs[4:])


def feed_grads_kernel(*refs):
    cores, pack_ref = (refs[: len(refs) // 2], refs[len(refs) // 2 : -1]), refs[-1]
    lines = pack_ref.shape[0]
    wide = narrow = 0.0
    for x_ref, output_ref, *factors in cores:
        if len(factors) == 1:
            units = factors[0].shape[0] // 3
            grads, hidden = factors[0][: 2 * units], factors[0][2 * units :]
        else:
            grads, hidden = factors[0][...], factors[1][...]
        wide = wide + nn(grads, x_ref[...])
        narrow = narrow + nn(hidden, output_ref[...])
    padded = wide.shape[0] // lines
    pack_ref[:, :padded] = wide.astype(bf16).reshape(lines, padded, wide.shape[1])
    pack_ref[:, padded:] = narrow.astype(bf16).reshape(lines, padded // 2, wide.shape[1])


def middle_kernel(*refs):
    parts = refs[:4]
    first_e_ref, first_d_ref, normed_d_ref, gains_e_ref, gains_d_ref, cross_e_ref, cross_d_ref, allowed_ref = refs[4:12]
    second_e_ref, normed_e_ref, queries_ref, states_ref, context_ref, second_d_ref, normed_last_ref = refs[12:]
    inner = context_ref.shape[0]
    queries_ref[...] = nt(cross_d_ref[:inner], normed_d_ref[...]).astype(bf16)
    second_e = first_e_ref[...] + added(parts)
    second_e_ref[...] = second_e
    normed = rms_norm(second_e, gains_e_ref[2:3]).astype(bf16)
    normed_e_ref[...] = normed
    states_ref[...] = nt(cross_e_ref[...], normed).astype(bf16)
    attend_into(context_ref, queries_ref, states_ref, states_ref, allowed_ref, (0, 0, inner))
    second_d = first_d_ref[...] + tn(context_ref[...], cross_d_ref[inner:])
    second_d_ref[...] = second_d
    normed_last_ref[...] = rms_norm(second_d, gains_d_ref[2:3]).astype(bf16)


def middle_back_kernel(*refs):
    parts = refs[:4]
    second_d_ref, second_e_ref, cotangent_d_ref, cotangent_e_ref, gains_d_ref, gains_e_ref = refs[4:10]
    cross_d_ref, cross_e_ref, queries_ref, states_ref, allowed_ref = refs[10:15]
    stream_d_ref, branch_ref, grads_ref, stream_e_ref, sent_ref, gain_d_ref, gain_e_ref = refs[15:]
    inner = queries_ref.shape[0]
    input_grad, gain_d_ref[...] = rms_back(second_d_ref[...], gains_d_ref[2:3], added(parts))
    stream_d = cotangent_d_ref[...].astype(f32) + input_grad
    stream_d_ref[...] = stream_d
    branch = stream_d.astype(bf16)
    branch_ref[...] = branch
    context_grad = nt(cross_d_ref[inner:], branch).astype(bf16)
    attend_back_into(grads_ref, queries_ref, states_ref, states_ref, allowed_ref, context_grad, (0, 0, inner))
    final_grad = tn(grads_ref[inner:], cross_e_ref[...])
    input_grad, gain_e_ref[...] = rms_back(second_e_ref[...], gains_e_ref[2:3], final_grad)
    stream_e = cotangent_e_ref[...].astype(f32) + input_grad
    stream_e_ref[...] = stream_e
    sent_ref[...] = stream_e.astype(bf16)


def first_back_d_kernel(grads_ref, cross_d_ref, first_d_ref, gains_d_ref, stream_ref, out_ref, gain_ref):
    inner = cross_d_ref.shape[0] // 2
    upstream = tn(grads_ref[:inner], cross_d_ref[:inner])
    input_grad, gain_ref[...] = rms_back(first_d_ref[...], gains_d_ref[1:2], upstream)
    out_ref[...] = stream_ref[...] + input_grad


def first_back_e_kernel(*refs):
    parts = refs[:4]
    section_ref, first_e_ref, gains_e_ref, stream_ref, stream_d_ref, kept_ref, sent_ref, gain_ref = refs[4:]
    input_grad, gain_ref[...] = rms_back(first_e_ref[...], gains_e_ref[1:2], added(parts))
    stream_e = stream_ref[...] + input_grad
    is_encoder = section_ref[0] == 0
    kept_ref[...] = jnp.where(is_encoder, stream_e, stream_d_ref[...])
    sent_ref[...] = jnp.where(is_encoder, stream_d_ref[...], stream_e)


def self_back_kernel(section_ref, kept_ref, got_ref, out_w_ref, projected_ref, allowed_ref, stream_ref, branch_ref, grads_ref):
    is_encoder = section_ref[0] == 0
    inner, length = out_w_ref.shape[0], kept_ref.shape[0]
    stream_ref[:length] = jnp.where(is_encoder, kept_ref[...], got_ref[...])
    stream_ref[length:] = jnp.where(is_encoder, got_ref[...], kept_ref[...])
    branch = stream_ref[...].astype(bf16)
    branch_ref[...] = branch
    context_grad = nt(out_w_ref[...], branch).astype(bf16)
    attend_back_into(
        grads_ref, projected_ref, projected_ref, projected_ref, allowed_ref, context_grad, (0, inner, 2 * inner)
    )


def table_kernel(*refs):
    grads, codes, gain_refs, (section_ref, in_ref, embedding_ref, gain_ref, stream_ref, out_ref) = (
        refs[:4],
        refs[4:8],
        refs[8:12],
        refs[12:],
    )
    table = gain_grad = 0.0
    for k, (grad, code_ref) in enumerate(zip(grads, codes)):
        shape = (embedding_ref.shape[0], code_ref.shape[1])
        one_hot = (lax.broadcasted_iota(jnp.int32, shape, 0) == code_ref[...]).astype(bf16)
        inputs = tn(one_hot, embedding_ref[...])
        input_grad, gain_part = rms_back(inputs, gain_ref[...], tn(grad[...], in_ref[...]))
        if k == 0:
            input_grad = input_grad + stream_ref[...]
        gain_grad = gain_grad + gain_part
        table = table + nn(one_hot, input_grad.astype(bf16))
    vocabulary = embedding_ref.shape[0]
    out_ref[:vocabulary] = table.astype(bf16)
    nothing, is_encoder = jnp.zeros_like(gain_grad), section_ref[0] == 0
    rows = [jnp.where(is_encoder, gain_grad, nothing), gain_refs[0][...], gain_refs[1][...]]
    rows += [jnp.where(is_encoder, nothing, gain_grad), gain_refs[2][...], gain_refs[3][...]]
    rows.append(jnp.zeros((out_ref.shape[0] - vocabulary - 6, out_ref.shape[1]), f32))
    out_ref[vocabulary:] = jnp.concatenate(rows, 0).astype(bf16)


def assemble_kernel(section_ref, plane_ref, *refs):
    pieces, (table_ref, gains_ref, rows_ref) = refs[:PLANE], refs[PLANE:]
    count = pieces[0].shape[0]
    for k, piece in enumerate(pieces):
        rows_ref[pl.ds(pl.multiple_of((plane_ref[0] ^ k) * count, 8), count)] = piece[...].astype(f32)
    vocabulary = table_ref.shape[0]
    table_ref[...] = rows_ref[:vocabulary]
    gains = rows_ref[vocabulary : vocabulary + 8]
    gains_ref[0] = jnp.where(section_ref[0] == 0, gains[:3], gains[3:6])


def in_grad_kernel(*refs):
    grads, streams, out_ref = refs[:4], refs[4:8], refs[8]
    total = nn(grads[0][...], streams[0][...])
    for grad, stream in zip(grads[1:], streams[1:]):
        total = total + nn(grad[...], stream[...])
    out_ref[...] = total.astype(bf16)


def cross_grads_kernel(section_ref, grads_ref, normed_e_ref, normed_d_ref, context_ref, branch_ref, kept_ref, sent_ref):
    inner = context_ref.shape[0]
    is_encoder = section_ref[0] == 0
    grad_e = nn(grads_ref[inner:], normed_e_ref[...])
    grad_first = nn(grads_ref[:inner], normed_d_ref[...])
    grad_second = nn(context_ref[...], branch_ref[...])
    for start, grad_d in ((0, grad_first), (inner, grad_second)):
        part_e = grad_e[start : start + inner]
        kept_ref[start : start + inner] = jnp.where(is_encoder, part_e, grad_d).astype(bf16)
        sent_ref[start : start + inner] = jnp.where(is_encoder, grad_d, part_e).astype(bf16)


def build(lines):
    devices = lines * PLANE

    def place(section, line, plane):
        return section * devices + line * PLANE + plane

    def hop(block, offset):
        route = [
            (place(s, z, j), place(s, z, j ^ offset))
            for s in range(2)
            for z in range(lines)
            for j in range(PLANE)
        ]
        return permute(block, AXES, route)

    def swap(block):
        return permute(block, "section", [(0, 1), (1, 0)])

    narrow_route = []
    for core in range(2):
        for block in range(devices):
            target = (block % 2, 2 * (block // 8) + core, (block % 8) // 2)
            narrow_route.append((core * devices + block, place(*target)))

    def at(array, index, axis=0):
        return lax.dynamic_index_in_dim(array, index, axis, False)

    def ordered(own, others, index, axis=0):
        count = len(others) + 1
        shape = own.shape[:axis] + (count,) + own.shape[axis:]
        out = jnp.zeros(shape, own.dtype)
        for where_to, piece in [(index, own)] + others:
            out = lax.dynamic_update_index_in_dim(out, piece, where_to, axis)
        return out

    def sum_line(block):
        if lines & (lines - 1):
            return rounded(lax.psum(block.astype(f32), "line"))
        distance = 1
        while distance < lines:
            route = [(z, z ^ distance) for z in range(lines)]
            block = rounded(block.astype(f32) + permute(block, "line", route).astype(f32))
            distance *= 2
        return block

    def in_plane(blocks, axis=0):
        j = lax.axis_index("plane")
        return ordered(blocks[0], [(j ^ k, blocks[k]) for k in range(1, PLANE)], j, axis)

    def gather_plane(block, axis=0):
        return in_plane(spread(block), axis)

    def scattered(parts):
        j = lax.axis_index("plane")
        return [at(parts, j)] + [hop(at(parts, j ^ k), k) for k in range(1, PLANE)]

    def total_of(terms):
        return sum((term.astype(f32) for term in terms[1:]), terms[0].astype(f32))

    def spread(block):
        return [block] + [hop(block, k) for k in range(1, PLANE)]

    def collected(parts):
        return [parts[0]] + [hop(parts[k], k) for k in range(1, PLANE)]

    def per_device(
        byte_codes,
        encoder_segments,
        target_segments,
        embedding,
        attention_in,
        attention_out,
        widen_weight,
        narrow_weight,
        cross_first,
        cross_second,
        norm_gains,
        cotangent,
    ):
        section = lax.axis_index("section")
        j = lax.axis_index("plane")
        is_encoder = section == 0
        section_scalar = section.astype(jnp.int32).reshape(1)
        inner = cross_first.shape[2] * devices
        vocabulary, width = embedding.shape
        rows, length = encoder_segments.shape
        tokens = rows * length

        def together(*values):
            return list(lax.optimization_barrier(values))

        def by_section(mine, other):
            return jnp.where(is_encoder, mine, other), jnp.where(is_encoder, other, mine)

        def in_order(mine, other):
            return jnp.concatenate(by_section(mine, other), 0)

        in_cols = attention_in.shape[2]
        cross_cols = cross_first.shape[2]
        column, codes = together(
            jnp.concatenate([attention_in[0].T, attention_out[0], cross_first[0].T, cross_second[0].T], 0),
            byte_codes[0],
        )
        column = lax.all_gather(column, "line", axis=0)
        in_column = column[:, :in_cols].reshape(-1, width)

        widen_half = widen_weight.shape[2] // 2
        narrow_half = narrow_weight.shape[1] // 2
        padded_narrow = -(-narrow_half // 16) * 16
        padded_widen = 2 * padded_narrow

        def widened(block):
            return jnp.pad(block, ((0, 0),) * (block.ndim - 2) + ((0, padded_narrow - narrow_half), (0, 0)))

        narrow_parts = widened(narrow_weight[0].reshape(2, narrow_half, width))
        narrow_e, narrow_d = by_section(at(narrow_parts, section), swap(at(narrow_parts, 1 - section)))
        moved = permute(jnp.concatenate([narrow_e, narrow_d], 0), AXES, narrow_route)
        widen_parts = widened(widen_weight[0].T.reshape(2, 2, narrow_half, width)).reshape(
            2, padded_widen, width
        )
        widen_e, widen_d = by_section(at(widen_parts, section), swap(at(widen_parts, 1 - section)))

        columns = lax.broadcasted_iota(jnp.int32, (tokens, vocabulary), 1)
        inputs = nn((codes.reshape(tokens, 1) == columns).astype(bf16), embedding)
        own_segments = jnp.where(is_encoder, encoder_segments, target_segments)
        earlier = lax.broadcasted_iota(jnp.int32, (length, length), 1) <= lax.broadcasted_iota(
            jnp.int32, (length, length), 0
        )
        allowed = (
            (own_segments[:, :, None] == own_segments[:, None, :]) & (earlier | is_encoder)[None]
        ).astype(f32)
        encoder_row, target_row = at(encoder_segments, section), at(target_segments, section)
        cross_allowed = (target_row[:, None] == encoder_row[None, :]).astype(f32)[None]

        own_gains = norm_gains[0]
        received = swap(jnp.concatenate([at(cotangent[0], 1 - section), own_gains], 0))
        cotangent_e, cotangent_d = by_section(at(cotangent[0], section), received[:length])
        gains_e, gains_d = (g.astype(f32) for g in by_section(own_gains, received[length:]))
        gain_self = own_gains[:1].astype(f32)

        normed_plane = spread(rms_norm(inputs, gain_self).astype(bf16))
        moved, *normed_plane = together(moved, *normed_plane)
        pack_e, pack_d = lax.optimization_barrier(
            (
                jnp.concatenate([widen_e, moved[:padded_narrow]], 0),
                jnp.concatenate([widen_d, moved[padded_narrow:]], 0),
            )
        )
        own_e = lax.all_gather(pack_e, "line", axis=0)
        own_d = lax.all_gather(pack_d, "line", axis=0)

        projected_parts = [
            nt(in_column, block).astype(bf16).reshape(lines, in_cols, tokens) for block in normed_plane
        ]
        codes_row, *projected_parts = together(codes.reshape(1, tokens), *projected_parts)
        hopped = together(
            *spread(codes_row), *[hop(projected_parts[k], k) for k in range(1, PLANE)], column
        )
        codes_plane, hopped = hopped[:PLANE], hopped[PLANE:]
        column = hopped[-1]
        projected = in_plane([projected_parts[0], *hopped[:-1]], 1).reshape(3 * inner, tokens)
        out_pieces = together(*spread(column[:, in_cols : in_cols + cross_cols]), column)
        column = out_pieces[-1]
        out_w = in_plane(out_pieces[:-1], 1).reshape(inner, width)
        row_f32, row_bf16 = ((length, width), f32), ((length, width), bf16)
        context, first_kept, first_sent = call(
            self_forward_kernel,
            (((inner, tokens), bf16), row_f32, row_f32),
            section_scalar,
            projected,
            allowed,
            inputs,
            out_w,
        )

        first_e, first_d, normed_first, normed_cross = call(
            first_norm_kernel,
            (row_f32, row_f32, row_bf16, row_bf16),
            section_scalar,
            first_kept,
            swap(first_sent),
            gains_e,
            gains_d,
        )
        stream_e = spread(normed_first)
        column, *stream_e = together(column, *stream_e)
        cross_pieces = spread(column[:, in_cols + cross_cols :])
        group = PLANE * length
        group_bf16 = ((group, width), bf16)
        pack_shape = (lines, padded_widen + padded_narrow, width)
        halves_of = pack_specs(lines, padded_widen, width)
        units = lines * padded_narrow
        unit_bf16, pair_bf16, trio_bf16 = (((n * units, group), bf16) for n in (1, 2, 3))
        blocks_bf16 = (row_bf16,) * PLANE

        def with_packs(first, *packs):
            specs = {first + 2 * i + k: halves_of[k] for i in range(len(packs)) for k in range(2)}
            return dict(specs=specs), [pack for pack in packs for _ in range(2)]

        def feed_grads(own, other, *ties):
            (pack,) = call(feed_grads_kernel, ((pack_shape, bf16),), *own, *other, time_us=1, ties=ties)
            return pack

        own_e, *stream_e = together(own_e, *stream_e)
        other_e = swap(own_e)
        cotangent_d, *stream_e = together(cotangent_d, *stream_e)
        options, packs = with_packs(4, own_e)
        value_own, slope_own, hidden_own, part_own, x_e = call(
            feed_forward_own_kernel,
            (unit_bf16, unit_bf16, unit_bf16, group_bf16, group_bf16),
            *stream_e,
            *packs,
            **options,
        )
        output_grad_d = spread(cotangent_d)
        x_e, *cross_pieces = together(x_e, *cross_pieces)
        cross_w = in_plane(cross_pieces, 1).reshape(devices, 2, cross_cols, width).swapaxes(0, 1)
        cross_w = cross_w.reshape(2 * inner, width)
        cross_e, cross_d = by_section(cross_w, swap(cross_w))
        options, packs = with_packs(2, other_e)
        value_other, slope_other, hidden_other, *part_e = call(
            feed_forward_other_kernel,
            (unit_bf16, unit_bf16, unit_bf16, *blocks_bf16),
            x_e,
            part_own,
            *packs,
            **options,
        )
        *part_e, output_grad_d[1], output_grad_d[2], output_grad_d[3] = together(
            *part_e, *output_grad_d[1:]
        )

        second_e, normed_final, cross_queries, states, cross_context, second_d, normed_last = call(
            middle_kernel,
            (
                row_f32,
                row_bf16,
                ((inner, length), bf16),
                ((2 * inner, length), bf16),
                ((inner, length), bf16),
                row_f32,
                row_bf16,
            ),
            *collected(part_e),
            first_e,
            first_d,
            normed_cross,
            gains_e,
            gains_d,
            cross_e,
            cross_d,
            cross_allowed,
        )

        stream_d = spread(normed_last)
        own_d, *stream_d = together(own_d, *stream_d)
        other_d = swap(own_d)
        options, packs = with_packs(8, own_d)
        factors_d, part_own, back_own, x_d, joined_grad_d = call(
            feed_both_own_kernel,
            (trio_bf16, group_bf16, group_bf16, group_bf16, group_bf16),
            *stream_d,
            *output_grad_d,
            *packs,
            **options,
        )
        options, packs = with_packs(4, other_d)
        factors_other_d, *blocks = call(
            feed_both_other_kernel,
            (trio_bf16, *blocks_bf16, *blocks_bf16),
            x_d,
            joined_grad_d,
            part_own,
            back_own,
            *packs,
            **options,
        )
        feed_sum_d = feed_grads(
            (x_d, joined_grad_d, factors_d),
            (swap(x_d), swap(joined_grad_d), swap(factors_other_d)),
        )
        back_d, part_d = collected(blocks[:PLANE]), blocks[PLANE:]
        gain_shape = ((1, width), f32)
        stream_two_d, cross_branch, cross_grads, stream_two_e, sent_e, gain_two_d, gain_two_e = call(
            middle_back_kernel,
            (row_f32, row_bf16, ((3 * inner, length), bf16), row_f32, row_bf16, gain_shape, gain_shape),
            *back_d,
            second_d,
            second_e,
            cotangent_d,
            cotangent_e,
            gains_d,
            gains_e,
            cross_d,
            cross_e,
            cross_queries,
            states,
            cross_allowed,
            ties=(feed_sum_d,),
        )

        stream_one_d, gain_one_d = call(
            first_back_d_kernel,
            (row_f32, gain_shape),
            cross_grads,
            cross_d,
            first_d,
            gains_d,
            stream_two_d,
        )
        output_grad_e = together(*spread(sent_e))
        cross_kept, cross_sent = call(
            cross_grads_kernel,
            (((2 * inner, width), bf16), ((2 * inner, width), bf16)),
            section_scalar,
            cross_grads,
            normed_final,
            normed_cross,
            cross_context,
            cross_branch,
        )
        cross_grad = (cross_kept.astype(f32) + swap(cross_sent).astype(f32)).astype(bf16)
        options, packs = with_packs(4, own_e, other_e)
        grads_own, grads_other, joined_grad_e, *back_e = call(
            feed_back_kernel,
            (pair_bf16, pair_bf16, group_bf16, *blocks_bf16),
            *output_grad_e,
            *packs,
            value_own,
            slope_own,
            value_other,
            slope_other,
            ties=(stream_one_d, cross_kept),
            time_us=1,
            **options,
        )
        def by_plane(*products):
            parts = [m.astype(bf16).reshape(lines, PLANE, -1, width).swapaxes(0, 1) for m in products]
            return jnp.concatenate(parts, 2)

        cross_terms = scattered(by_plane(cross_grad[:inner], cross_grad[inner:]))
        feed_sum_e = feed_grads(
            (x_e, joined_grad_e, grads_own, hidden_own),
            (swap(x_e), swap(joined_grad_e), swap(grads_other), swap(hidden_other)),
        )
        back_e = collected(back_e)

        summed_d = lax.psum_scatter(feed_sum_d, "line", scatter_dimension=0)
        feed_sum_e, summed_d = together(feed_sum_e, summed_d)
        summed_e = lax.psum_scatter(feed_sum_e, "line", scatter_dimension=0)

        stream_kept, stream_sent, gain_one_e = call(
            first_back_e_kernel,
            (row_f32, row_f32, gain_shape),
            *back_e,
            section_scalar,
            first_e,
            gains_e,
            stream_two_e,
            stream_one_d,
            ties=(feed_sum_e,),
        )
        stream_got = swap(stream_sent)
        stream_one, branch_grad, projected_grad = call(
            self_back_kernel,
            (((tokens, width), f32), ((tokens, width), bf16), ((3 * inner, tokens), bf16)),
            section_scalar,
            stream_kept,
            stream_got,
            out_w,
            projected,
            allowed,
        )
        projected_grad, *cross_terms = together(projected_grad, *cross_terms)
        parts = projected_grad.reshape(lines, PLANE, in_cols, tokens)
        grad_parts = [at(parts, j, 1)] + [hop(at(parts, j ^ k, 1), k) for k in range(1, PLANE)]
        branch_grad, *grad_parts = together(
            branch_grad, *[part.reshape(lines * in_cols, tokens) for part in grad_parts]
        )
        out_part = total_of(scattered(by_plane(nn(context, branch_grad)))).astype(bf16)
        cross_part = total_of(cross_terms).astype(bf16)
        (in_part,) = call(
            in_grad_kernel,
            (((lines * in_cols, width), bf16),),
            *grad_parts,
            *normed_plane,
        )
        padded = -(-(vocabulary + 6) // 64) * 64
        (small,) = call(
            table_kernel,
            (((padded, width), bf16),),
            *grad_parts,
            *codes_plane,
            gain_one_e,
            gain_two_e,
            gain_one_d,
            gain_two_d,
            section_scalar,
            in_column,
            embedding,
            gain_self,
            stream_one,
            specs={4 + k: whole((1, tokens)) for k in range(PLANE)},
        )
        plane_sum = rounded(total_of(scattered(small.reshape(PLANE, -1, width))))
        plane_sum, summed_e, *part_d = together(plane_sum, summed_e, *part_d)
        part_d = collected(part_d)
        halves = plane_sum.reshape(2, padded // 8, width)
        chip_sum = rounded(at(halves, section).astype(f32) + swap(at(halves, 1 - section)).astype(f32))
        rest_pack = jnp.concatenate([in_part.reshape(lines, in_cols, width), cross_part, out_part], 1)
        rest_pack, line_sum, summed_d, summed_e = together(
            rest_pack, sum_line(chip_sum), summed_d, summed_e
        )
        rest_sum = lax.psum_scatter(rest_pack, "line", scatter_dimension=0).astype(f32)
        pieces = together(*spread(in_order(line_sum, swap(line_sum))), *part_d)
        second_out_d = second_d + sum(part.astype(f32) for part in pieces[PLANE:])
        embedding_grad, gains_grad = call(
            assemble_kernel,
            (((vocabulary, width), f32), ((1, 3, width), f32)),
            section_scalar,
            j.astype(jnp.int32).reshape(1),
            *pieces[:PLANE],
            scratch=(pltpu.VMEM((padded, width), f32),),
        )

        narrow = permute(
            jnp.concatenate([summed_e[padded_widen:], summed_d[padded_widen:]], 0),
            AXES,
            [(b, a) for a, b in narrow_route],
        )
        half_e = jnp.concatenate([summed_e[:padded_widen], narrow[:padded_narrow]], 0)
        half_d = jnp.concatenate([summed_d[:padded_widen], narrow[padded_narrow:]], 0)
        half_kept, half_sent = by_section(half_e, half_d)
        both = in_order(half_kept[None], swap(half_sent)[None])
        both = both.reshape(2, 3, padded_narrow, width)[:, :, :narrow_half]
        widen_t = both[:, :2].reshape(2 * widen_half, width)
        narrow_grad = both[:, 2].reshape(2 * narrow_half, width).astype(f32)

        output_kept, output_sent = by_section(second_e.astype(bf16), second_out_d.astype(bf16))
        block_output = in_order(output_kept, swap(output_sent)).reshape(rows, length, width)
        cuts = [0, in_cols, in_cols + cross_cols, in_cols + 2 * cross_cols, in_cols + 3 * cross_cols]
        in_sum, first_cross_sum, second_cross_sum, out_sum = (
            rest_sum[a:b] for a, b in zip(cuts[:-1], cuts[1:])
        )
        return (
            block_output[None],
            embedding_grad,
            in_sum.T[None],
            out_sum[None],
            widen_t.astype(f32).T[None],
            narrow_grad[None],
            first_cross_sum.T[None],
            second_cross_sum.T[None],
            gains_grad,
        )

    return per_device


def solution(mesh):
    lines = mesh.shape["dp"] // PLANE
    inner_mesh = Mesh(mesh.devices.reshape(2, lines, PLANE), AXES)
    dp = ("line", "plane")
    return jax.shard_map(
        build(lines),
        mesh=inner_mesh,
        in_specs=(
            P("section", dp, None),
            P(dp, None),
            P(dp, None),
            P(),
            P("section", None, dp),
            P("section", dp, None),
            P("section", None, dp),
            P("section", dp, None),
            P("section", None, dp),
            P("section", None, dp),
            P("section", None, None),
            P("section", dp, None, None),
        ),
        out_specs=(
            P("section", dp, None, None),
            P(),
            P("section", None, dp),
            P("section", dp, None),
            P("section", None, dp),
            P("section", dp, None),
            P("section", None, dp),
            P("section", None, dp),
            P("section", None, None),
        ),
        check_vma=False,
    )
```

```python
import functools

import jax
import jax.numpy as jnp
from jax import lax
from jax.experimental import pallas as pl
from jax.experimental.pallas import tpu as pltpu
from jax.sharding import Mesh, PartitionSpec as P

HEADS = 6
HEAD_DIM = 64
PLANE = 4
SCALE = HEAD_DIM ** (-0.5)

epsilon = 1e-06
masked_value = -1000000000.0
AXES = ("section", "line", "plane")
bf16 = jnp.bfloat16
f32 = jnp.float32


def nn(a, b):
    return lax.dot_general(a, b, (((1,), (0,)), ((), ())), preferred_element_type=f32)


def nt(a, b):
    return lax.dot_general(a, b, (((1,), (1,)), ((), ())), preferred_element_type=f32)


def tn(a, b):
    return lax.dot_general(a, b, (((0,), (0,)), ((), ())), preferred_element_type=f32)


def permute(block, axes, route):
    shape = block.shape
    if block.ndim == 2 and shape[0] % 8 == 0:
        block = block.reshape(shape[0] // 8, 8, shape[1])
    return lax.ppermute(block, axes, route).reshape(shape)


def rounded(value):
    return lax.reduce_precision(value, 8, 7).astype(bf16)


def rms_norm(inputs, gain_row):
    return inputs * lax.rsqrt(jnp.mean(inputs * inputs, -1, keepdims=True) + epsilon) * gain_row


def rms_back(inputs, gain_row, upstream):
    scale = lax.rsqrt(jnp.mean(inputs * inputs, -1, keepdims=True) + epsilon)
    normed = inputs * scale
    weighted = upstream * gain_row
    grad = (weighted - normed * jnp.mean(weighted * normed, -1, keepdims=True)) * scale
    return grad, jnp.sum(upstream * normed, 0, keepdims=True)


def gelu_parts(gate):
    slope = (2.0 / jnp.pi) ** 0.5
    square = gate * gate
    half = 0.5 + 0.5 * jnp.tanh(gate * (slope + (slope * 0.044715) * square))
    bend = gate * (slope + (slope * 0.134145) * square)
    return gate * half, half + (2.0 * half) * ((1.0 - half) * bend)


def whole(shape):
    return pl.BlockSpec(shape, lambda step: (0,) * len(shape))


def call(kernel, outputs, *args, scratch=(), specs=None, time_us=1, ties=(), vmem=56):
    specs = specs or {}
    in_specs = [
        specs.get(i)
        or (pl.BlockSpec(memory_space=pltpu.SMEM) if a.dtype == jnp.int32 else whole(a.shape))
        for i, a in enumerate(args)
    ]
    in_specs += [pl.BlockSpec(memory_space=pl.ANY)] * len(ties)
    first, after = len(args), len(args) + len(ties)
    out_shape = tuple(jax.ShapeDtypeStruct(output[0], output[1]) for output in outputs)
    return pl.pallas_call(
        lambda *refs: kernel(*refs[:first], *refs[after:]),
        grid=(1,),
        out_shape=out_shape,
        in_specs=in_specs,
        out_specs=tuple(output[2] if len(output) > 2 else whole(output[0]) for output in outputs),
        scratch_shapes=list(scratch),
        compiler_params=pltpu.CompilerParams(vmem_limit_bytes=vmem * 1024 * 1024),
        cost_estimate=pl.CostEstimate(
            flops=int(time_us * 8e8), bytes_accessed=int(time_us * 2.5e6), transcendentals=0
        ),
    )(*args, *ties)


def chances_of(queries, keys, allowed):
    scores = jnp.where(allowed > 0, tn(queries, keys) * SCALE, masked_value)
    exponent = jnp.exp(scores - jnp.max(scores, -1, keepdims=True))
    return exponent / jnp.sum(exponent, -1, keepdims=True)


def attend_into(context_ref, query_ref, key_ref, value_ref, allowed_ref, starts=(0, 0, 0)):
    rows, length, _ = allowed_ref.shape
    for row in range(rows):
        columns = slice(row * length, (row + 1) * length)
        for head in range(HEADS):
            q, k, v = (
                ref[start + head * HEAD_DIM : start + (head + 1) * HEAD_DIM, columns]
                for ref, start in zip((query_ref, key_ref, value_ref), starts)
            )
            weights = chances_of(q, k, allowed_ref[row]).astype(bf16)
            context_ref[head * HEAD_DIM : (head + 1) * HEAD_DIM, columns] = nt(v, weights).astype(bf16)


def attend_back_into(grads_ref, query_ref, key_ref, value_ref, allowed_ref, upstream, starts=(0, 0, 0)):
    rows, length, _ = allowed_ref.shape
    inner = HEADS * HEAD_DIM
    for row in range(rows):
        columns = slice(row * length, (row + 1) * length)
        for head in range(HEADS):
            first = head * HEAD_DIM
            q, k, v = (
                ref[start + first : start + first + HEAD_DIM, columns]
                for ref, start in zip((query_ref, key_ref, value_ref), starts)
            )
            g = upstream[first : first + HEAD_DIM, columns]
            chances = chances_of(q, k, allowed_ref[row])
            weight_grad = tn(g, v)
            score_grad = (
                chances * (weight_grad - jnp.sum(weight_grad * chances, -1, keepdims=True))
            ).astype(bf16)
            grads = (nt(k, score_grad) * SCALE, nn(q, score_grad) * SCALE, nn(g, chances.astype(bf16)))
            for number, grad in enumerate(grads):
                at = number * inner + first
                grads_ref[at : at + HEAD_DIM, columns] = grad.astype(bf16)


def added(refs):
    total = refs[0][...].astype(f32)
    for ref in refs[1:]:
        total = total + ref[...].astype(f32)
    return total


def split_rows(section, value, kept_ref, sent_ref):
    length = kept_ref.shape[0]
    mine, other = value[:length], value[length:]
    kept_ref[...] = jnp.where(section == 0, mine, other)
    sent_ref[...] = jnp.where(section == 0, other, mine)


def self_forward_kernel(section_ref, projected_ref, allowed_ref, inputs_ref, out_w_ref, context_ref, kept_ref, sent_ref):
    inner = context_ref.shape[0]
    attend_into(context_ref, projected_ref, projected_ref, projected_ref, allowed_ref, (0, inner, 2 * inner))
    first_sum = inputs_ref[...] + tn(context_ref[...], out_w_ref[...])
    split_rows(section_ref[0], first_sum, kept_ref, sent_ref)


def first_norm_kernel(section_ref, kept_ref, got_ref, gains_e_ref, gains_d_ref, first_e_ref, first_d_ref, normed_e_ref, normed_d_ref):
    is_encoder = section_ref[0] == 0
    first_e = jnp.where(is_encoder, kept_ref[...], got_ref[...])
    first_d = jnp.where(is_encoder, got_ref[...], kept_ref[...])
    first_e_ref[...] = first_e
    first_d_ref[...] = first_d
    normed_e_ref[...] = rms_norm(first_e, gains_e_ref[1:2]).astype(bf16)
    normed_d_ref[...] = rms_norm(first_d, gains_d_ref[1:2]).astype(bf16)


def joined(refs, out_ref):
    length = refs[0].shape[0]
    for k, ref in enumerate(refs):
        out_ref[k * length : (k + 1) * length] = ref[...]
    return out_ref[...]


def apart(value, refs):
    length = refs[0].shape[0]
    for k, ref in enumerate(refs):
        ref[...] = value[k * length : (k + 1) * length].astype(bf16)


def pack_specs(lines, padded, width):
    return [
        pl.BlockSpec((lines, padded, width), lambda step: (0, 0, 0)),
        pl.BlockSpec((lines, padded // 2, width), lambda step: (0, 2, 0)),
    ]


def rows_of(ref):
    return ref[...].reshape(ref.shape[0] * ref.shape[1], ref.shape[2])


def feed_forward(x, wide, narrow, value_ref, slope_ref, hidden_ref):
    both = nt(wide, x)
    units = both.shape[0] // 2
    value, slope = gelu_parts(both[:units])
    value_ref[...] = value.astype(bf16)
    slope_ref[...] = (slope * both[units:]).astype(bf16)
    hidden_ref[...] = (value * both[units:]).astype(bf16)
    return tn(hidden_ref[...], narrow)


def feed_forward_own_kernel(*refs):
    streams, wide_ref, narrow_ref, value_ref, slope_ref, hidden_ref, part_ref, x_ref = refs[:4], *refs[4:]
    x = joined(streams, x_ref)
    part = feed_forward(x, rows_of(wide_ref), rows_of(narrow_ref), value_ref, slope_ref, hidden_ref)
    part_ref[...] = part.astype(bf16)


def feed_forward_other_kernel(x_ref, prior_ref, wide_ref, narrow_ref, value_ref, slope_ref, hidden_ref, *part_refs):
    part = feed_forward(
        x_ref[...], rows_of(wide_ref), rows_of(narrow_ref), value_ref, slope_ref, hidden_ref
    )
    apart(part + prior_ref[...].astype(f32), part_refs)


def feed_back_kernel(*refs):
    outputs, packs, saved = refs[:4], (refs[4:6], refs[6:8]), refs[8:12]
    grads_refs, output_ref, back_refs = refs[12:14], refs[14], refs[15:]
    output_grad = joined(outputs, output_ref)
    back = None
    for core, (wide_ref, narrow_ref) in enumerate(packs):
        hidden_grad = nt(rows_of(narrow_ref), output_grad)
        units = hidden_grad.shape[0]
        value_ref, slope_ref = saved[2 * core : 2 * core + 2]
        grads_refs[core][:units] = (hidden_grad * slope_ref[...].astype(f32)).astype(bf16)
        grads_refs[core][units:] = (hidden_grad * value_ref[...].astype(f32)).astype(bf16)
        term = tn(grads_refs[core][...], rows_of(wide_ref))
        back = term if back is None else back + term
    apart(back, back_refs)


def feed_both(x, output_grad, wide, narrow, grads_ref):
    both = nt(wide, x)
    hidden_grad = nt(narrow, output_grad)
    units = hidden_grad.shape[0]
    value, slope = gelu_parts(both[:units])
    grads_ref[:units] = (hidden_grad * (slope * both[units:])).astype(bf16)
    grads_ref[units : 2 * units] = (hidden_grad * value).astype(bf16)
    grads_ref[2 * units :] = (value * both[units:]).astype(bf16)
    return tn(grads_ref[2 * units :], narrow), tn(grads_ref[: 2 * units], wide)


def feed_both_own_kernel(*refs):
    streams, outputs, wide_ref, narrow_ref, grads_ref, part_ref, back_ref, x_ref, output_ref = (
        refs[:4],
        refs[4:8],
        *refs[8:],
    )
    x, output_grad = joined(streams, x_ref), joined(outputs, output_ref)
    part, back = feed_both(x, output_grad, rows_of(wide_ref), rows_of(narrow_ref), grads_ref)
    part_ref[...] = part.astype(bf16)
    back_ref[...] = back.astype(bf16)


def feed_both_other_kernel(x_ref, output_ref, part_prior, back_prior, wide_ref, narrow_ref, grads_ref, *refs):
    part, back = feed_both(x_ref[...], output_ref[...], rows_of(wide_ref), rows_of(narrow_ref), grads_ref)
    apart(back + back_prior[...].astype(f32), refs[:4])
    apart(part + part_prior[...].astype(f32), refs[4:])


def feed_grads_kernel(*refs):
    cores, pack_ref = (refs[: len(refs) // 2], refs[len(refs) // 2 : -1]), refs[-1]
    lines = pack_ref.shape[0]
    wide = narrow = 0.0
    for x_ref, output_ref, *factors in cores:
        if len(factors) == 1:
            units = factors[0].shape[0] // 3
            grads, hidden = factors[0][: 2 * units], factors[0][2 * units :]
        else:
            grads, hidden = factors[0][...], factors[1][...]
        wide = wide + nn(grads, x_ref[...])
        narrow = narrow + nn(hidden, output_ref[...])
    padded = wide.shape[0] // lines
    pack_ref[:, :padded] = wide.astype(bf16).reshape(lines, padded, wide.shape[1])
    pack_ref[:, padded:] = narrow.astype(bf16).reshape(lines, padded // 2, wide.shape[1])


def middle_kernel(*refs):
    parts = refs[:4]
    first_e_ref, first_d_ref, normed_d_ref, gains_e_ref, gains_d_ref, cross_e_ref, cross_d_ref, allowed_ref = refs[4:12]
    second_e_ref, normed_e_ref, queries_ref, states_ref, context_ref, second_d_ref, normed_last_ref = refs[12:]
    inner = context_ref.shape[0]
    queries_ref[...] = nt(cross_d_ref[:inner], normed_d_ref[...]).astype(bf16)
    second_e = first_e_ref[...] + added(parts)
    second_e_ref[...] = second_e
    normed = rms_norm(second_e, gains_e_ref[2:3]).astype(bf16)
    normed_e_ref[...] = normed
    states_ref[...] = nt(cross_e_ref[...], normed).astype(bf16)
    attend_into(context_ref, queries_ref, states_ref, states_ref, allowed_ref, (0, 0, inner))
    second_d = first_d_ref[...] + tn(context_ref[...], cross_d_ref[inner:])
    second_d_ref[...] = second_d
    normed_last_ref[...] = rms_norm(second_d, gains_d_ref[2:3]).astype(bf16)


def middle_back_kernel(*refs):
    parts = refs[:4]
    second_d_ref, second_e_ref, cotangent_d_ref, cotangent_e_ref, gains_d_ref, gains_e_ref = refs[4:10]
    cross_d_ref, cross_e_ref, queries_ref, states_ref, allowed_ref = refs[10:15]
    stream_d_ref, branch_ref, grads_ref, stream_e_ref, sent_ref, gain_d_ref, gain_e_ref = refs[15:]
    inner = queries_ref.shape[0]
    input_grad, gain_d_ref[...] = rms_back(second_d_ref[...], gains_d_ref[2:3], added(parts))
    stream_d = cotangent_d_ref[...].astype(f32) + input_grad
    stream_d_ref[...] = stream_d
    branch = stream_d.astype(bf16)
    branch_ref[...] = branch
    context_grad = nt(cross_d_ref[inner:], branch).astype(bf16)
    attend_back_into(grads_ref, queries_ref, states_ref, states_ref, allowed_ref, context_grad, (0, 0, inner))
    final_grad = tn(grads_ref[inner:], cross_e_ref[...])
    input_grad, gain_e_ref[...] = rms_back(second_e_ref[...], gains_e_ref[2:3], final_grad)
    stream_e = cotangent_e_ref[...].astype(f32) + input_grad
    stream_e_ref[...] = stream_e
    sent_ref[...] = stream_e.astype(bf16)


def first_back_d_kernel(grads_ref, cross_d_ref, first_d_ref, gains_d_ref, stream_ref, out_ref, gain_ref):
    inner = cross_d_ref.shape[0] // 2
    upstream = tn(grads_ref[:inner], cross_d_ref[:inner])
    input_grad, gain_ref[...] = rms_back(first_d_ref[...], gains_d_ref[1:2], upstream)
    out_ref[...] = stream_ref[...] + input_grad


def first_back_e_kernel(*refs):
    parts = refs[:4]
    section_ref, first_e_ref, gains_e_ref, stream_ref, stream_d_ref, kept_ref, sent_ref, gain_ref = refs[4:]
    input_grad, gain_ref[...] = rms_back(first_e_ref[...], gains_e_ref[1:2], added(parts))
    stream_e = stream_ref[...] + input_grad
    is_encoder = section_ref[0] == 0
    kept_ref[...] = jnp.where(is_encoder, stream_e, stream_d_ref[...])
    sent_ref[...] = jnp.where(is_encoder, stream_d_ref[...], stream_e)


def self_back_kernel(section_ref, kept_ref, got_ref, out_w_ref, projected_ref, allowed_ref, stream_ref, branch_ref, grads_ref):
    is_encoder = section_ref[0] == 0
    inner, length = out_w_ref.shape[0], kept_ref.shape[0]
    stream_ref[:length] = jnp.where(is_encoder, kept_ref[...], got_ref[...])
    stream_ref[length:] = jnp.where(is_encoder, got_ref[...], kept_ref[...])
    branch = stream_ref[...].astype(bf16)
    branch_ref[...] = branch
    context_grad = nt(out_w_ref[...], branch).astype(bf16)
    attend_back_into(
        grads_ref, projected_ref, projected_ref, projected_ref, allowed_ref, context_grad, (0, inner, 2 * inner)
    )


def table_kernel(*refs):
    grads, codes, gain_refs, (section_ref, in_ref, embedding_ref, gain_ref, stream_ref, out_ref) = (
        refs[:4],
        refs[4:8],
        refs[8:12],
        refs[12:],
    )
    table = gain_grad = 0.0
    for k, (grad, code_ref) in enumerate(zip(grads, codes)):
        shape = (embedding_ref.shape[0], code_ref.shape[1])
        one_hot = (lax.broadcasted_iota(jnp.int32, shape, 0) == code_ref[...]).astype(bf16)
        inputs = tn(one_hot, embedding_ref[...])
        input_grad, gain_part = rms_back(inputs, gain_ref[...], tn(grad[...], in_ref[...]))
        if k == 0:
            input_grad = input_grad + stream_ref[...]
        gain_grad = gain_grad + gain_part
        table = table + nn(one_hot, input_grad.astype(bf16))
    vocabulary = embedding_ref.shape[0]
    out_ref[:vocabulary] = table.astype(bf16)
    nothing, is_encoder = jnp.zeros_like(gain_grad), section_ref[0] == 0
    rows = [jnp.where(is_encoder, gain_grad, nothing), gain_refs[0][...], gain_refs[1][...]]
    rows += [jnp.where(is_encoder, nothing, gain_grad), gain_refs[2][...], gain_refs[3][...]]
    rows.append(jnp.zeros((out_ref.shape[0] - vocabulary - 6, out_ref.shape[1]), f32))
    out_ref[vocabulary:] = jnp.concatenate(rows, 0).astype(bf16)


def assemble_kernel(section_ref, plane_ref, *refs):
    pieces, (table_ref, gains_ref, rows_ref) = refs[:PLANE], refs[PLANE:]
    count = pieces[0].shape[0]
    for k, piece in enumerate(pieces):
        rows_ref[pl.ds(pl.multiple_of((plane_ref[0] ^ k) * count, 8), count)] = piece[...].astype(f32)
    vocabulary = table_ref.shape[0]
    table_ref[...] = rows_ref[:vocabulary]
    gains = rows_ref[vocabulary : vocabulary + 8]
    gains_ref[0] = jnp.where(section_ref[0] == 0, gains[:3], gains[3:6])


def in_grad_kernel(*refs):
    grads, streams, out_ref = refs[:4], refs[4:8], refs[8]
    total = nn(grads[0][...], streams[0][...])
    for grad, stream in zip(grads[1:], streams[1:]):
        total = total + nn(grad[...], stream[...])
    out_ref[...] = total.astype(bf16)


def cross_grads_kernel(section_ref, grads_ref, normed_e_ref, normed_d_ref, context_ref, branch_ref, kept_ref, sent_ref):
    inner = context_ref.shape[0]
    is_encoder = section_ref[0] == 0
    grad_e = nn(grads_ref[inner:], normed_e_ref[...])
    grad_first = nn(grads_ref[:inner], normed_d_ref[...])
    grad_second = nn(context_ref[...], branch_ref[...])
    for start, grad_d in ((0, grad_first), (inner, grad_second)):
        part_e = grad_e[start : start + inner]
        kept_ref[start : start + inner] = jnp.where(is_encoder, part_e, grad_d).astype(bf16)
        sent_ref[start : start + inner] = jnp.where(is_encoder, grad_d, part_e).astype(bf16)


def build(lines):
    devices = lines * PLANE

    def place(section, line, plane):
        return section * devices + line * PLANE + plane

    def hop(block, offset):
        route = [
            (place(s, z, j), place(s, z, j ^ offset))
            for s in range(2)
            for z in range(lines)
            for j in range(PLANE)
        ]
        return permute(block, AXES, route)

    def swap(block):
        return permute(block, "section", [(0, 1), (1, 0)])

    narrow_route = []
    for core in range(2):
        for block in range(devices):
            target = (block % 2, 2 * (block // 8) + core, (block % 8) // 2)
            narrow_route.append((core * devices + block, place(*target)))

    def at(array, index, axis=0):
        return lax.dynamic_index_in_dim(array, index, axis, False)

    def ordered(own, others, index, axis=0):
        count = len(others) + 1
        shape = own.shape[:axis] + (count,) + own.shape[axis:]
        out = jnp.zeros(shape, own.dtype)
        for where_to, piece in [(index, own)] + others:
            out = lax.dynamic_update_index_in_dim(out, piece, where_to, axis)
        return out

    def sum_line(block):
        if lines & (lines - 1):
            return rounded(lax.psum(block.astype(f32), "line"))
        distance = 1
        while distance < lines:
            route = [(z, z ^ distance) for z in range(lines)]
            block = rounded(block.astype(f32) + permute(block, "line", route).astype(f32))
            distance *= 2
        return block

    def in_plane(blocks, axis=0):
        j = lax.axis_index("plane")
        return ordered(blocks[0], [(j ^ k, blocks[k]) for k in range(1, PLANE)], j, axis)

    def gather_plane(block, axis=0):
        return in_plane(spread(block), axis)

    def scattered(parts):
        j = lax.axis_index("plane")
        return [at(parts, j)] + [hop(at(parts, j ^ k), k) for k in range(1, PLANE)]

    def total_of(terms):
        return sum((term.astype(f32) for term in terms[1:]), terms[0].astype(f32))

    def spread(block):
        return [block] + [hop(block, k) for k in range(1, PLANE)]

    def collected(parts):
        return [parts[0]] + [hop(parts[k], k) for k in range(1, PLANE)]

    def per_device(
        byte_codes,
        encoder_segments,
        target_segments,
        embedding,
        attention_in,
        attention_out,
        widen_weight,
        narrow_weight,
        cross_first,
        cross_second,
        norm_gains,
        cotangent,
    ):
        section = lax.axis_index("section")
        j = lax.axis_index("plane")
        is_encoder = section == 0
        section_scalar = section.astype(jnp.int32).reshape(1)
        inner = cross_first.shape[2] * devices
        vocabulary, width = embedding.shape
        rows, length = encoder_segments.shape
        tokens = rows * length

        def together(*values):
            return list(lax.optimization_barrier(values))

        def by_section(mine, other):
            return jnp.where(is_encoder, mine, other), jnp.where(is_encoder, other, mine)

        def in_order(mine, other):
            return jnp.concatenate(by_section(mine, other), 0)

        in_cols = attention_in.shape[2]
        cross_cols = cross_first.shape[2]
        column, codes = together(
            jnp.concatenate([attention_in[0].T, attention_out[0], cross_first[0].T, cross_second[0].T], 0),
            byte_codes[0],
        )
        column = lax.all_gather(column, "line", axis=0)
        in_column = column[:, :in_cols].reshape(-1, width)

        widen_half = widen_weight.shape[2] // 2
        narrow_half = narrow_weight.shape[1] // 2
        padded_narrow = -(-narrow_half // 16) * 16
        padded_widen = 2 * padded_narrow

        def widened(block):
            return jnp.pad(block, ((0, 0),) * (block.ndim - 2) + ((0, padded_narrow - narrow_half), (0, 0)))

        narrow_parts = widened(narrow_weight[0].reshape(2, narrow_half, width))
        narrow_e, narrow_d = by_section(at(narrow_parts, section), swap(at(narrow_parts, 1 - section)))
        moved = permute(jnp.concatenate([narrow_e, narrow_d], 0), AXES, narrow_route)
        widen_parts = widened(widen_weight[0].T.reshape(2, 2, narrow_half, width)).reshape(
            2, padded_widen, width
        )
        widen_e, widen_d = by_section(at(widen_parts, section), swap(at(widen_parts, 1 - section)))

        columns = lax.broadcasted_iota(jnp.int32, (tokens, vocabulary), 1)
        inputs = nn((codes.reshape(tokens, 1) == columns).astype(bf16), embedding)
        own_segments = jnp.where(is_encoder, encoder_segments, target_segments)
        earlier = lax.broadcasted_iota(jnp.int32, (length, length), 1) <= lax.broadcasted_iota(
            jnp.int32, (length, length), 0
        )
        allowed = (
            (own_segments[:, :, None] == own_segments[:, None, :]) & (earlier | is_encoder)[None]
        ).astype(f32)
        encoder_row, target_row = at(encoder_segments, section), at(target_segments, section)
        cross_allowed = (target_row[:, None] == encoder_row[None, :]).astype(f32)[None]

        own_gains = norm_gains[0]
        received = swap(jnp.concatenate([at(cotangent[0], 1 - section), own_gains], 0))
        cotangent_e, cotangent_d = by_section(at(cotangent[0], section), received[:length])
        gains_e, gains_d = (g.astype(f32) for g in by_section(own_gains, received[length:]))
        gain_self = own_gains[:1].astype(f32)

        normed_plane = spread(rms_norm(inputs, gain_self).astype(bf16))
        moved, *normed_plane = together(moved, *normed_plane)
        pack_e, pack_d = lax.optimization_barrier(
            (
                jnp.concatenate([widen_e, moved[:padded_narrow]], 0),
                jnp.concatenate([widen_d, moved[padded_narrow:]], 0),
            )
        )
        own_e = lax.all_gather(pack_e, "line", axis=0)
        own_d = lax.all_gather(pack_d, "line", axis=0)

        projected_parts = [
            nt(in_column, block).astype(bf16).reshape(lines, in_cols, tokens) for block in normed_plane
        ]
        codes_row, *projected_parts = together(codes.reshape(1, tokens), *projected_parts)
        hopped = together(
            *spread(codes_row), *[hop(projected_parts[k], k) for k in range(1, PLANE)], column
        )
        codes_plane, hopped = hopped[:PLANE], hopped[PLANE:]
        column = hopped[-1]
        projected = in_plane([projected_parts[0], *hopped[:-1]], 1).reshape(3 * inner, tokens)
        out_pieces = together(*spread(column[:, in_cols : in_cols + cross_cols]), column)
        column = out_pieces[-1]
        out_w = in_plane(out_pieces[:-1], 1).reshape(inner, width)
        row_f32, row_bf16 = ((length, width), f32), ((length, width), bf16)
        context, first_kept, first_sent = call(
            self_forward_kernel,
            (((inner, tokens), bf16), row_f32, row_f32),
            section_scalar,
            projected,
            allowed,
            inputs,
            out_w,
        )

        first_e, first_d, normed_first, normed_cross = call(
            first_norm_kernel,
            (row_f32, row_f32, row_bf16, row_bf16),
            section_scalar,
            first_kept,
            swap(first_sent),
            gains_e,
            gains_d,
        )
        stream_e = spread(normed_first)
        column, *stream_e = together(column, *stream_e)
        cross_pieces = spread(column[:, in_cols + cross_cols :])
        group = PLANE * length
        group_bf16 = ((group, width), bf16)
        pack_shape = (lines, padded_widen + padded_narrow, width)
        halves_of = pack_specs(lines, padded_widen, width)
        units = lines * padded_narrow
        unit_bf16, pair_bf16, trio_bf16 = (((n * units, group), bf16) for n in (1, 2, 3))
        blocks_bf16 = (row_bf16,) * PLANE

        def with_packs(first, *packs):
            specs = {first + 2 * i + k: halves_of[k] for i in range(len(packs)) for k in range(2)}
            return dict(specs=specs), [pack for pack in packs for _ in range(2)]

        def feed_grads(own, other, *ties):
            (pack,) = call(feed_grads_kernel, ((pack_shape, bf16),), *own, *other, time_us=1, ties=ties)
            return pack

        own_e, *stream_e = together(own_e, *stream_e)
        other_e = swap(own_e)
        cotangent_d, *stream_e = together(cotangent_d, *stream_e)
        options, packs = with_packs(4, own_e)
        value_own, slope_own, hidden_own, part_own, x_e = call(
            feed_forward_own_kernel,
            (unit_bf16, unit_bf16, unit_bf16, group_bf16, group_bf16),
            *stream_e,
            *packs,
            **options,
        )
        output_grad_d = spread(cotangent_d)
        x_e, *cross_pieces = together(x_e, *cross_pieces)
        cross_w = in_plane(cross_pieces, 1).reshape(devices, 2, cross_cols, width).swapaxes(0, 1)
        cross_w = cross_w.reshape(2 * inner, width)
        cross_e, cross_d = by_section(cross_w, swap(cross_w))
        options, packs = with_packs(2, other_e)
        value_other, slope_other, hidden_other, *part_e = call(
            feed_forward_other_kernel,
            (unit_bf16, unit_bf16, unit_bf16, *blocks_bf16),
            x_e,
            part_own,
            *packs,
            **options,
        )
        *part_e, output_grad_d[1], output_grad_d[2], output_grad_d[3] = together(
            *part_e, *output_grad_d[1:]
        )

        second_e, normed_final, cross_queries, states, cross_context, second_d, normed_last = call(
            middle_kernel,
            (
                row_f32,
                row_bf16,
                ((inner, length), bf16),
                ((2 * inner, length), bf16),
                ((inner, length), bf16),
                row_f32,
                row_bf16,
            ),
            *collected(part_e),
            first_e,
            first_d,
            normed_cross,
            gains_e,
            gains_d,
            cross_e,
            cross_d,
            cross_allowed,
        )

        stream_d = spread(normed_last)
        own_d, *stream_d = together(own_d, *stream_d)
        other_d = swap(own_d)
        options, packs = with_packs(8, own_d)
        factors_d, part_own, back_own, x_d, joined_grad_d = call(
            feed_both_own_kernel,
            (trio_bf16, group_bf16, group_bf16, group_bf16, group_bf16),
            *stream_d,
            *output_grad_d,
            *packs,
            **options,
        )
        options, packs = with_packs(4, other_d)
        factors_other_d, *blocks = call(
            feed_both_other_kernel,
            (trio_bf16, *blocks_bf16, *blocks_bf16),
            x_d,
            joined_grad_d,
            part_own,
            back_own,
            *packs,
            **options,
        )
        feed_sum_d = feed_grads(
            (x_d, joined_grad_d, factors_d),
            (swap(x_d), swap(joined_grad_d), swap(factors_other_d)),
        )
        back_d, part_d = collected(blocks[:PLANE]), blocks[PLANE:]
        gain_shape = ((1, width), f32)
        stream_two_d, cross_branch, cross_grads, stream_two_e, sent_e, gain_two_d, gain_two_e = call(
            middle_back_kernel,
            (row_f32, row_bf16, ((3 * inner, length), bf16), row_f32, row_bf16, gain_shape, gain_shape),
            *back_d,
            second_d,
            second_e,
            cotangent_d,
            cotangent_e,
            gains_d,
            gains_e,
            cross_d,
            cross_e,
            cross_queries,
            states,
            cross_allowed,
            ties=(feed_sum_d,),
        )

        stream_one_d, gain_one_d = call(
            first_back_d_kernel,
            (row_f32, gain_shape),
            cross_grads,
            cross_d,
            first_d,
            gains_d,
            stream_two_d,
        )
        output_grad_e = together(*spread(sent_e))
        cross_kept, cross_sent = call(
            cross_grads_kernel,
            (((2 * inner, width), bf16), ((2 * inner, width), bf16)),
            section_scalar,
            cross_grads,
            normed_final,
            normed_cross,
            cross_context,
            cross_branch,
        )
        cross_grad = (cross_kept.astype(f32) + swap(cross_sent).astype(f32)).astype(bf16)
        options, packs = with_packs(4, own_e, other_e)
        grads_own, grads_other, joined_grad_e, *back_e = call(
            feed_back_kernel,
            (pair_bf16, pair_bf16, group_bf16, *blocks_bf16),
            *output_grad_e,
            *packs,
            value_own,
            slope_own,
            value_other,
            slope_other,
            ties=(stream_one_d, cross_kept),
            time_us=1,
            **options,
        )
        def by_plane(*products):
            parts = [m.astype(bf16).reshape(lines, PLANE, -1, width).swapaxes(0, 1) for m in products]
            return jnp.concatenate(parts, 2)

        cross_terms = scattered(by_plane(cross_grad[:inner], cross_grad[inner:]))
        feed_sum_e = feed_grads(
            (x_e, joined_grad_e, grads_own, hidden_own),
            (swap(x_e), swap(joined_grad_e), swap(grads_other), swap(hidden_other)),
        )
        back_e = collected(back_e)

        summed_d = lax.psum_scatter(feed_sum_d, "line", scatter_dimension=0)
        feed_sum_e, summed_d = together(feed_sum_e, summed_d)
        summed_e = lax.psum_scatter(feed_sum_e, "line", scatter_dimension=0)

        stream_kept, stream_sent, gain_one_e = call(
            first_back_e_kernel,
            (row_f32, row_f32, gain_shape),
            *back_e,
            section_scalar,
            first_e,
            gains_e,
            stream_two_e,
            stream_one_d,
            ties=(feed_sum_e,),
        )
        stream_got = swap(stream_sent)
        stream_one, branch_grad, projected_grad = call(
            self_back_kernel,
            (((tokens, width), f32), ((tokens, width), bf16), ((3 * inner, tokens), bf16)),
            section_scalar,
            stream_kept,
            stream_got,
            out_w,
            projected,
            allowed,
        )
        projected_grad, *cross_terms = together(projected_grad, *cross_terms)
        parts = projected_grad.reshape(lines, PLANE, in_cols, tokens)
        grad_parts = [at(parts, j, 1)] + [hop(at(parts, j ^ k, 1), k) for k in range(1, PLANE)]
        branch_grad, *grad_parts = together(
            branch_grad, *[part.reshape(lines * in_cols, tokens) for part in grad_parts]
        )
        out_part = total_of(scattered(by_plane(nn(context, branch_grad)))).astype(bf16)
        cross_part = total_of(cross_terms).astype(bf16)
        (in_part,) = call(
            in_grad_kernel,
            (((lines * in_cols, width), bf16),),
            *grad_parts,
            *normed_plane,
        )
        padded = -(-(vocabulary + 6) // 64) * 64
        (small,) = call(
            table_kernel,
            (((padded, width), bf16),),
            *grad_parts,
            *codes_plane,
            gain_one_e,
            gain_two_e,
            gain_one_d,
            gain_two_d,
            section_scalar,
            in_column,
            embedding,
            gain_self,
            stream_one,
            specs={4 + k: whole((1, tokens)) for k in range(PLANE)},
        )
        plane_sum = rounded(total_of(scattered(small.reshape(PLANE, -1, width))))
        plane_sum, summed_e, *part_d = together(plane_sum, summed_e, *part_d)
        part_d = collected(part_d)
        halves = plane_sum.reshape(2, padded // 8, width)
        chip_sum = rounded(at(halves, section).astype(f32) + swap(at(halves, 1 - section)).astype(f32))
        rest_pack = jnp.concatenate([in_part.reshape(lines, in_cols, width), cross_part, out_part], 1)
        chip_sum, rest_pack = together(chip_sum, rest_pack)
        line_sum, summed_d, summed_e = together(sum_line(chip_sum), summed_d, summed_e)
        rest_sum = lax.psum_scatter(rest_pack, "line", scatter_dimension=0).astype(f32)
        pieces = together(*spread(in_order(line_sum, swap(line_sum))), *part_d)
        second_out_d = second_d + sum(part.astype(f32) for part in pieces[PLANE:])
        embedding_grad, gains_grad = call(
            assemble_kernel,
            (((vocabulary, width), f32), ((1, 3, width), f32)),
            section_scalar,
            j.astype(jnp.int32).reshape(1),
            *pieces[:PLANE],
            scratch=(pltpu.VMEM((padded, width), f32),),
        )

        narrow = permute(
            jnp.concatenate([summed_e[padded_widen:], summed_d[padded_widen:]], 0),
            AXES,
            [(b, a) for a, b in narrow_route],
        )
        half_e = jnp.concatenate([summed_e[:padded_widen], narrow[:padded_narrow]], 0)
        half_d = jnp.concatenate([summed_d[:padded_widen], narrow[padded_narrow:]], 0)
        half_kept, half_sent = by_section(half_e, half_d)
        both = in_order(half_kept[None], swap(half_sent)[None])
        both = both.reshape(2, 3, padded_narrow, width)[:, :, :narrow_half]
        widen_t = both[:, :2].reshape(2 * widen_half, width)
        narrow_grad = both[:, 2].reshape(2 * narrow_half, width).astype(f32)

        output_kept, output_sent = by_section(second_e.astype(bf16), second_out_d.astype(bf16))
        block_output = in_order(output_kept, swap(output_sent)).reshape(rows, length, width)
        cuts = [0, in_cols, in_cols + cross_cols, in_cols + 2 * cross_cols, in_cols + 3 * cross_cols]
        in_sum, first_cross_sum, second_cross_sum, out_sum = (
            rest_sum[a:b] for a, b in zip(cuts[:-1], cuts[1:])
        )
        return (
            block_output[None],
            embedding_grad,
            in_sum.T[None],
            out_sum[None],
            widen_t.astype(f32).T[None],
            narrow_grad[None],
            first_cross_sum.T[None],
            second_cross_sum.T[None],
            gains_grad,
        )

    return per_device


def solution(mesh):
    lines = mesh.shape["dp"] // PLANE
    inner_mesh = Mesh(mesh.devices.reshape(2, lines, PLANE), AXES)
    dp = ("line", "plane")
    return jax.shard_map(
        build(lines),
        mesh=inner_mesh,
        in_specs=(
            P("section", dp, None),
            P(dp, None),
            P(dp, None),
            P(),
            P("section", None, dp),
            P("section", dp, None),
            P("section", None, dp),
            P("section", dp, None),
            P("section", None, dp),
            P("section", None, dp),
            P("section", None, None),
            P("section", dp, None, None),
        ),
        out_specs=(
            P("section", dp, None, None),
            P(),
            P("section", None, dp),
            P("section", dp, None),
            P("section", None, dp),
            P("section", dp, None),
            P("section", None, dp),
            P("section", None, dp),
            P("section", None, None),
        ),
        check_vma=False,
    )
```
